128 devices in a mesh: lat: 8 (over z, y_lo), lon: 16 (over y_hi, x, core).
Axes of the slice: x: 4, y: 4 (y_hi: 2, y_lo: 2; y = y_hi * 2 + y_lo), z: 4, core: 2. Of those that a mesh axis runs over, the one named last changes fastest.
Arguments:
- tokens: bfloat16 [4, 48, 384, 512], P(None, 'lat', 'lon'), may hold values from -6 to 6
- cotangent: bfloat16 [4, 48, 384, 512], P(None, 'lat', 'lon'), may hold values from -6 to 6
- w_qkv: bfloat16 [512, 1536], replicated, may hold values from -12 to 12
- w_proj: bfloat16 [512, 512], replicated, may hold values from -0.25 to 0.25
Outputs:
- output: bfloat16 [4, 48, 384, 512], P(None, 'lat', 'lon')
- grad_tokens: bfloat16 [4, 48, 384, 512], P(None, 'lat', 'lon')
- grad_qkv: float32 [512, 1536], replicated
- grad_proj: float32 [512, 512], replicated
The draws below stay inside these ranges and needn't reach their ends.
All inputs are finite; a program needn't handle non-finite values.
Results may differ from the reference program's by a relative error of at most 0.011.
Values may be sent and summed in bfloat16 or wider, within the bound.
A program may use at most 128 MiB of HBM per device.

```python
import math
import jax
import jax.numpy as jnp
from jax import lax

D = 512
HEADS = 16
LV = 4
NLAT = 48
NLON = 384
TOKENS = 73728


def draw_w_qkv(key, part):
    key = jax.random.fold_in(key, 7)
    first = jax.random.fold_in(key, 0)
    base = jax.random.normal(first, (D, 3 * D), jnp.float32) / math.sqrt(D)
    return jnp.clip(base, -11.0, 11.0).astype(jnp.bfloat16)


def steps_of(key, dims, pieces, low, high):
    factor_of, own = 1.0, jax.random.fold_in(key, 6)
    for axis_at, shards_of in pieces:
        steps = jnp.exp(jax.random.uniform(jax.random.fold_in(own, axis_at), (shards_of,), jnp.float32, low / len(pieces), high / len(pieces)))
        factor_of = factor_of * jnp.repeat(steps, dims[axis_at] // shards_of).reshape([-1 if axis == axis_at else 1 for axis in range(len(dims))])
    return factor_of


def bell_draw(key, extent, deviation, most, shards=(), kind=jnp.bfloat16):
    array = deviation * jax.random.normal(key, extent, jnp.float32)
    if shards:
        array = array * steps_of(key, extent, shards, -0.22, 0.18)
    return jnp.clip(array, -most, most).astype(kind)


def setup_inputs(seed: int = 0) -> dict:
    splits = jax.random.split(jax.random.key(seed), 5)
    return {
        "tokens": bell_draw(splits[0], (LV, NLAT, NLON, D), 1.0, 6.0, ((1, 8), (2, 16))),
        "cotangent": bell_draw(splits[1], (LV, NLAT, NLON, D), 1.0, 6.0, ((1, 8), (2, 16))),
        "w_qkv": draw_w_qkv(jax.random.fold_in(splits[4], 71), 0),
        "w_proj": bell_draw(splits[3], (D, D), D ** -0.5, 0.25),
    }


def to_windows(field):
    levels, rows, cols = field.shape[:3]
    rest = field.shape[3:]
    field = field.reshape((levels // 2, 2, rows // 6, 6, cols // 12, 12) + rest)
    order = (0, 2, 4, 1, 3, 5) + tuple(range(6, 6 + len(rest)))
    return field.transpose(order).reshape((-1, 144) + rest)

def from_windows(field, levels, rows, cols):
    rest = field.shape[2:]
    field = field.reshape((levels // 2, rows // 6, cols // 12, 2, 6, 12) + rest)
    order = (0, 3, 1, 4, 2, 5) + tuple(range(6, 6 + len(rest)))
    return field.transpose(order).reshape((levels, rows, cols) + rest)

def region_of(place, count, width, shift):
    return jnp.where(place < count - width, 0, jnp.where(place < count - shift, 1, 2)).astype(jnp.int32)

def window_block(rolled, rolled_cot, region, w_qkv, w_proj):
    levels, rows, cols, width = rolled.shape
    head_size = width // HEADS
    scale = 1.0 / head_size ** 0.5
    flat = to_windows(rolled).reshape(-1, width).astype(jnp.float32)
    cot = to_windows(rolled_cot).reshape(-1, width)
    labels = to_windows(region)
    allowed = labels[:, :, None] == labels[:, None, :]
    mean = lax.optimization_barrier(jnp.mean(flat, axis=1, keepdims=True))
    centred = flat - mean
    inv_std = lax.rsqrt(lax.optimization_barrier(jnp.mean(centred * centred, axis=1, keepdims=True)) + 1e-05)
    normed_hat = centred * inv_std
    normed = normed_hat.astype(jnp.bfloat16)
    qkv = jnp.dot(normed, w_qkv, preferred_element_type=jnp.float32).astype(jnp.bfloat16)
    qkv = qkv.reshape(-1, 144, 3, HEADS, head_size).astype(jnp.float32)
    query, keys, values = (qkv[:, :, 0], qkv[:, :, 1], qkv[:, :, 2])
    scores = jnp.einsum('wqhd,wkhd->whqk', query, keys) * scale
    scores = jnp.where(allowed[:, None], scores, -1e+30)
    top = lax.optimization_barrier(jnp.max(scores, axis=-1, keepdims=True))
    expd = jnp.exp(scores - top)
    probs = expd / lax.optimization_barrier(jnp.sum(expd, axis=-1, keepdims=True))
    probs_b = probs.astype(jnp.bfloat16).astype(jnp.float32)
    context = jnp.einsum('whqk,wkhd->wqhd', probs_b, values).astype(jnp.bfloat16).reshape(-1, width)
    attended = jnp.dot(context, w_proj, preferred_element_type=jnp.float32).astype(jnp.bfloat16)
    d_context = jnp.dot(cot, w_proj.T, preferred_element_type=jnp.float32).astype(jnp.bfloat16)
    gproj = jnp.dot(context.T, cot, preferred_element_type=jnp.float32)
    d_heads = d_context.reshape(-1, 144, HEADS, head_size).astype(jnp.float32)
    d_probs = jnp.einsum('wqhd,wkhd->whqk', d_heads, values)
    d_values = jnp.einsum('whqk,wqhd->wkhd', probs_b, d_heads)
    inner = lax.optimization_barrier(jnp.sum(probs * d_probs, axis=-1, keepdims=True))
    d_scores = (probs * (d_probs - inner) * scale).astype(jnp.bfloat16).astype(jnp.float32)
    d_query = jnp.einsum('whqk,wkhd->wqhd', d_scores, keys)
    d_keys = jnp.einsum('whqk,wqhd->wkhd', d_scores, query)
    d_qkv = jnp.stack([d_query, d_keys, d_values], axis=2).astype(jnp.bfloat16).reshape(-1, 3 * width)
    gqkv = jnp.dot(normed.T, d_qkv, preferred_element_type=jnp.float32)
    d_normed = jnp.dot(d_qkv, w_qkv.T, preferred_element_type=jnp.float32)
    d_flat = (d_normed - lax.optimization_barrier(jnp.mean(d_normed, axis=1, keepdims=True)) - normed_hat * lax.optimization_barrier(jnp.mean(d_normed * normed_hat, axis=1, keepdims=True))) * inv_std
    d_flat = d_flat.astype(jnp.bfloat16)
    attended = from_windows(attended.reshape(-1, 144, width), levels, rows, cols)
    d_rolled = from_windows(d_flat.reshape(-1, 144, width), levels, rows, cols)
    return (attended, d_rolled, gqkv, gproj)

def reference(tokens, cotangent, w_qkv, w_proj):
    rolled = jnp.roll(tokens, (-1, -3, -6), axis=(0, 1, 2))
    rolled_cot = jnp.roll(cotangent, (-1, -3, -6), axis=(0, 1, 2))
    lev = region_of(jnp.arange(LV), LV, 2, 1)
    lat = region_of(jnp.arange(NLAT), NLAT, 6, 3)
    lon = region_of(jnp.arange(NLON), NLON, 12, 6)
    region = (9 * lev[:, None, None] + 3 * lat[None, :, None] + lon[None, None, :]).astype(jnp.int32)
    bands = NLAT // 6
    xs = jnp.moveaxis(rolled.reshape(LV, bands, 6, NLON, D), 1, 0)
    cs = jnp.moveaxis(rolled_cot.reshape(LV, bands, 6, NLON, D), 1, 0)
    rs = jnp.moveaxis(region.reshape(LV, bands, 6, NLON), 1, 0)

    def step(carry, band):
        attended, d_rolled, gqkv, gproj = window_block(band[0], band[1], band[2], w_qkv, w_proj)
        return ((carry[0] + gqkv, carry[1] + gproj), (attended, d_rolled))
    start = (jnp.zeros((D, 3 * D), jnp.float32), jnp.zeros((D, D), jnp.float32))
    sums, outs = lax.scan(step, start, (xs, cs, rs))
    attended = jnp.moveaxis(outs[0], 0, 1).reshape(LV, NLAT, NLON, D)
    d_rolled = jnp.moveaxis(outs[1], 0, 1).reshape(LV, NLAT, NLON, D)
    attended = jnp.roll(attended, (1, 3, 6), axis=(0, 1, 2))
    d_rolled = jnp.roll(d_rolled, (1, 3, 6), axis=(0, 1, 2))
    output = (tokens.astype(jnp.float32) + attended.astype(jnp.float32)).astype(jnp.bfloat16)
    grad_tokens = (cotangent.astype(jnp.float32) + d_rolled.astype(jnp.float32)).astype(jnp.bfloat16)
    norm = 1.0 / TOKENS ** 0.5
    return (output, grad_tokens, sums[0] * norm, sums[1] * norm)
```

```python
import functools
import numpy as np
import jax
import jax.numpy as jnp
from jax import lax
from jax.experimental import pallas as pl
from jax.experimental.pallas import tpu as pltpu

HEADS = 16
BF = jnp.bfloat16
F32 = jnp.float32
SCALE = 1.0 / 32**0.5
EXP2 = SCALE * 1.4426950408889634
NT = (((1,), (1,)), ((), ()))
TN = (((0,), (0,)), ((), ()))


def dot(a, b, dims=(((1,), (0,)), ((), ()))):
    return lax.dot_general(a, b, dims, preferred_element_type=F32)


def head_mask(dtype):
    head = lax.broadcasted_iota(jnp.int32, (128, 256), 0) >> 4
    col = lax.broadcasted_iota(jnp.int32, (128, 256), 1) >> 5
    return (head == col).astype(dtype)


def project(w, tok, cot, w_qkv, w_proj, hat, normed, inv, q, k, v, dc):
    x = tok[w].astype(F32)
    x = x - jnp.mean(x, axis=1, keepdims=True)
    scale = lax.rsqrt(jnp.mean(x * x, axis=1, keepdims=True) + 1e-05)
    x = x * scale
    hat[w] = x
    inv[w] = jnp.broadcast_to(scale, (144, 128))
    x = x.astype(BF)
    rows = pl.ds(pl.multiple_of(w * 144, 16), 144)
    normed[rows, :] = x
    for part, ref in enumerate((q, k, v)):
        for g in range(2):
            at = 512 * part + 256 * g
            ref[g, w] = dot(x, w_qkv[:, at : at + 256]).astype(BF)
    c = cot[rows, :]
    for g in range(2):
        dc[g, w] = dot(c, w_proj[256 * g : 256 * g + 256, :], NT).astype(BF)


def attend(g, w, klab, qlab, mask, maskf, q, k, v, dc, qs, cs, pt, st, ctx, dqkv, sf, df):
    keys = k[g, w]
    vals = v[g, w]
    rows0 = pl.multiple_of(w * 144, 16)
    for c in range(9):
        at = slice(128 * c, 128 * c + 128)
        q16 = q[g, w, 16 * c : 16 * c + 16, :]
        d16 = dc[g, w, 16 * c : 16 * c + 16, :]
        qs[at, :] = jnp.concatenate([q16] * 8, axis=0) * mask
        cs[at, :] = jnp.concatenate([d16] * 8, axis=0) * mask
    sf[...] = dot(keys, qs[...], NT)
    df[...] = dot(vals, cs[...], NT)
    for c in range(9):
        at = slice(128 * c, 128 * c + 128)
        s = sf[:, at]
        s = jnp.where(klab == qlab[c], s, -1e30)
        e = jnp.exp2((s - jnp.max(s, axis=0, keepdims=True)) * EXP2)
        p = e * (1.0 / jnp.sum(e, axis=0, keepdims=True))
        pt[:, at] = p.astype(BF)
        dp = df[:, at]
        inner = jnp.sum(p * dp, axis=0, keepdims=True)
        st[:, at] = ((p * SCALE) * (dp - inner)).astype(BF)
    out = dot(pt[...], vals, TN).reshape(9, 8, 16, 256) * maskf.reshape(1, 8, 16, 256)
    ctx[g, pl.ds(rows0, 144), :] = jnp.sum(out, axis=1).reshape(144, 256).astype(BF)
    out = dot(st[...], keys, TN).reshape(9, 8, 16, 256) * maskf.reshape(1, 8, 16, 256)
    dqkv[g, pl.ds(rows0, 144), 0:256] = jnp.sum(out, axis=1).reshape(144, 256).astype(BF)
    rows = pl.ds(rows0, 144)
    dqkv[g, rows, 256:512] = dot(st[...], qs[...]).astype(BF)
    dqkv[g, rows, 512:768] = dot(pt[...], cs[...]).astype(BF)


def finish(w, w_qkv, w_proj, hat, inv, ctx, dqkv, att, dflat):
    rows = pl.ds(pl.multiple_of(w * 144, 16), 144)
    a = dot(ctx[0, rows, :], w_proj[0:256, :]) + dot(ctx[1, rows, :], w_proj[256:512, :])
    att[w] = a.astype(BF)
    d = None
    for g in range(2):
        for part in range(3):
            at = 512 * part + 256 * g
            t = dot(dqkv[g, rows, 256 * part : 256 * part + 256], w_qkv[:, at : at + 256], NT)
            d = t if d is None else d + t
    h = hat[w]
    d = d - jnp.mean(d, axis=1, keepdims=True) - h * jnp.mean(d * h, axis=1, keepdims=True)
    scale = jnp.concatenate([inv[w]] * 4, axis=1)
    dflat[w] = (d * scale).astype(BF)


def labels(w, lat_last, lon_last):
    def flags(t):
        level = (t >= 72).astype(jnp.int32)
        t = t - 72 * level
        row = (t >= 36).astype(jnp.int32)
        t = t - 36 * row
        t = jnp.where(t >= 24, t - 24, jnp.where(t >= 12, t - 12, t))
        col = (t >= 6).astype(jnp.int32)
        return level * is_b + row * lat_last + col * last

    is_b = 4 * (w // 2)
    last = lon_last * (w % 2)
    klab = flags(lax.broadcasted_iota(jnp.int32, (144, 128), 0))
    lane = lax.broadcasted_iota(jnp.int32, (1, 128), 1) & 15
    qlab = [flags(lane + 16 * c) for c in range(9)]
    return klab, qlab


def kernel(tok, cot, w_qkv, w_proj, att, dflat, gqkv, gproj, hat, normed, inv, q, k, v, dc, qs, cs, pt, st, ctx, dqkv, sf, df):
    lat_last = 2 * (lax.axis_index("lat") == lax.axis_size("lat") - 1).astype(jnp.int32)
    lon_last = (lax.axis_index("lon") == lax.axis_size("lon") - 1).astype(jnp.int32)

    @pl.loop(0, 4)
    def _(w):
        project(w, tok, cot, w_qkv, w_proj, hat, normed, inv, q, k, v, dc)

    mask = head_mask(BF)
    maskf = head_mask(F32)

    @pl.loop(0, 8)
    def _(i):
        g, w = i // 4, i % 4
        klab, qlab = labels(w, lat_last, lon_last)
        attend(g, w, klab, qlab, mask, maskf, q, k, v, dc, qs, cs, pt, st, ctx, dqkv, sf, df)

    for g in range(2):
        gproj[256 * g : 256 * g + 256, :] = dot(ctx[g], cot[...], TN)
        for part in range(3):
            gqkv[:, 512 * part + 256 * g : 512 * part + 256 * g + 256] = dot(
                normed[...], dqkv[g, :, 256 * part : 256 * part + 256], TN
            )

    @pl.loop(0, 4)
    def _(w):
        finish(w, w_qkv, w_proj, hat, inv, ctx, dqkv, att, dflat)


def local_block(tok, cot, w_qkv, w_proj):
    vm = pl.BlockSpec(memory_space=pltpu.VMEM)
    return pl.pallas_call(
        kernel,
        out_shape=(
            jax.ShapeDtypeStruct((4, 144, 512), BF),
            jax.ShapeDtypeStruct((4, 144, 512), BF),
            jax.ShapeDtypeStruct((512, 1536), F32),
            jax.ShapeDtypeStruct((512, 512), F32),
        ),
        in_specs=[vm] * 4,
        out_specs=(vm,) * 4,
        scratch_shapes=[
            pltpu.VMEM((4, 144, 512), F32),
            pltpu.VMEM((576, 512), BF),
            pltpu.VMEM((4, 144, 128), F32),
            pltpu.VMEM((2, 4, 144, 256), BF),
            pltpu.VMEM((2, 4, 144, 256), BF),
            pltpu.VMEM((2, 4, 144, 256), BF),
            pltpu.VMEM((2, 4, 144, 256), BF),
            pltpu.VMEM((1152, 256), BF),
            pltpu.VMEM((1152, 256), BF),
            pltpu.VMEM((144, 1152), BF),
            pltpu.VMEM((144, 1152), BF),
            pltpu.VMEM((2, 576, 256), BF),
            pltpu.VMEM((2, 576, 768), BF),
            pltpu.VMEM((144, 1152), F32),
            pltpu.VMEM((144, 1152), F32),
        ],
        compiler_params=pltpu.CompilerParams(vmem_limit_bytes=56 * 2**20),
        name="window_block",
    )(tok, cot.reshape(576, 512), w_qkv, w_proj)
from jax.sharding import PartitionSpec as P


def shifted(value, axis, steps):
    count = lax.axis_size(axis)
    pairs = [(source, (source + steps) % count) for source in range(count)]
    return lax.ppermute(value, axis, pairs)


def to_windows(field):
    levels, rows, cols, width = field.shape
    field = field.reshape(levels // 2, 2, rows // 6, 6, cols // 12, 12, width)
    return field.transpose(0, 2, 4, 1, 3, 5, 6).reshape(-1, 144, width)


def from_windows(field, levels, rows, cols):
    field = field.reshape(levels // 2, rows // 6, cols // 12, 2, 6, 12, -1)
    return field.transpose(0, 3, 1, 4, 2, 5, 6).reshape(levels, rows, cols, -1)


def roll_in(x):
    x = jnp.concatenate([x[:, 3:], shifted(x[:, :3], "lat", -1)], axis=1)
    x = jnp.concatenate([x[:, :, 6:], shifted(x[:, :, :6], "lon", -1)], axis=2)
    return jnp.roll(x, -1, axis=0)


def roll_out(x):
    x = jnp.roll(x, 1, axis=0)
    x = jnp.concatenate([shifted(x[:, :, -6:], "lon", 1), x[:, :, :-6]], axis=2)
    return jnp.concatenate([shifted(x[:, -3:], "lat", 1), x[:, :-3]], axis=1)


def body(tokens, cotangent, w_qkv, w_proj):
    tok = to_windows(roll_in(tokens))
    cot = to_windows(roll_in(cotangent))
    att, dflat, gqkv, gproj = local_block(tok, cot, w_qkv, w_proj)
    att = roll_out(from_windows(att, 4, 6, 24))
    dflat = roll_out(from_windows(dflat, 4, 6, 24))
    output = (tokens.astype(F32) + att.astype(F32)).astype(BF)
    grad_tokens = (cotangent.astype(F32) + dflat.astype(F32)).astype(BF)
    gqkv, gproj = lax.psum((gqkv, gproj), ("lat", "lon"))
    norm = 1.0 / 73728**0.5
    return (output, grad_tokens, gqkv * norm, gproj * norm)


def solution(mesh):
    spec = P(None, "lat", "lon", None)
    return jax.shard_map(
        body,
        mesh=mesh,
        in_specs=(spec, spec, P(), P()),
        out_specs=(spec, spec, P(), P()),
        check_vma=False,
    )
```

```python
import functools
import numpy as np
import jax
import jax.numpy as jnp
from jax import lax
from jax.experimental import pallas as pl
from jax.experimental.pallas import tpu as pltpu

HEADS = 16
BF = jnp.bfloat16
F32 = jnp.float32
SCALE = 1.0 / 32**0.5
EXP2 = SCALE * 1.4426950408889634
NT = (((1,), (1,)), ((), ()))
TN = (((0,), (0,)), ((), ()))


def dot(a, b, dims=(((1,), (0,)), ((), ()))):
    return lax.dot_general(a, b, dims, preferred_element_type=F32)


def head_mask(dtype):
    head = lax.broadcasted_iota(jnp.int32, (128, 256), 0) >> 4
    col = lax.broadcasted_iota(jnp.int32, (128, 256), 1) >> 5
    return (head == col).astype(dtype)


def project(w, tok, cot, w_qkv, w_proj, hat, normed, inv, q, k, v, dc):
    x = tok[w].astype(F32)
    x = x - jnp.mean(x, axis=1, keepdims=True)
    scale = lax.rsqrt(jnp.mean(x * x, axis=1, keepdims=True) + 1e-05)
    x = x * scale
    hat[w] = x
    inv[w] = jnp.broadcast_to(scale, (144, 128))
    x = x.astype(BF)
    rows = pl.ds(pl.multiple_of(w * 144, 16), 144)
    normed[rows, :] = x
    for part, ref in enumerate((q, k, v)):
        for g in range(2):
            at = 512 * part + 256 * g
            ref[g, w] = dot(x, w_qkv[:, at : at + 256]).astype(BF)
    c = cot[rows, :]
    for g in range(2):
        dc[g, w] = dot(c, w_proj[256 * g : 256 * g + 256, :], NT).astype(BF)


def attend(g, w, klab, qlab, mask, maskf, q, k, v, dc, qs, cs, pt, st, ctx, dqkv, sf, df):
    keys = k[g, w]
    vals = v[g, w]
    rows0 = pl.multiple_of(w * 144, 16)
    for c in range(9):
        at = slice(128 * c, 128 * c + 128)
        q16 = q[g, w, 16 * c : 16 * c + 16, :]
        d16 = dc[g, w, 16 * c : 16 * c + 16, :]
        qs[at, :] = jnp.concatenate([q16] * 8, axis=0) * mask
        cs[at, :] = jnp.concatenate([d16] * 8, axis=0) * mask
    sf[...] = dot(keys, qs[...], NT)
    df[...] = dot(vals, cs[...], NT)
    for c in range(9):
        at = slice(128 * c, 128 * c + 128)
        s = sf[:, at]
        s = jnp.where(klab == qlab[c], s, -1e30)
        e = jnp.exp2((s - jnp.max(s, axis=0, keepdims=True)) * EXP2)
        p = e * (1.0 / jnp.sum(e, axis=0, keepdims=True))
        pt[:, at] = p.astype(BF)
        dp = df[:, at]
        inner = jnp.sum(p * dp, axis=0, keepdims=True)
        st[:, at] = ((p * SCALE) * (dp - inner)).astype(BF)
    out = dot(pt[...], vals, TN).reshape(9, 8, 16, 256) * maskf.reshape(1, 8, 16, 256)
    ctx[g, pl.ds(rows0, 144), :] = jnp.sum(out, axis=1).reshape(144, 256).astype(BF)
    out = dot(st[...], keys, TN).reshape(9, 8, 16, 256) * maskf.reshape(1, 8, 16, 256)
    dqkv[g, pl.ds(rows0, 144), 0:256] = jnp.sum(out, axis=1).reshape(144, 256).astype(BF)
    rows = pl.ds(rows0, 144)
    dqkv[g, rows, 256:512] = dot(st[...], qs[...]).astype(BF)
    dqkv[g, rows, 512:768] = dot(pt[...], cs[...]).astype(BF)


def finish(w, w_qkv, w_proj, hat, inv, ctx, dqkv, att, dflat):
    rows = pl.ds(pl.multiple_of(w * 144, 16), 144)
    a = dot(ctx[0, rows, :], w_proj[0:256, :]) + dot(ctx[1, rows, :], w_proj[256:512, :])
    att[w] = a.astype(BF)
    d = None
    for g in range(2):
        for part in range(3):
            at = 512 * part + 256 * g
            t = dot(dqkv[g, rows, 256 * part : 256 * part + 256], w_qkv[:, at : at + 256], NT)
            d = t if d is None else d + t
    h = hat[w]
    d = d - jnp.mean(d, axis=1, keepdims=True) - h * jnp.mean(d * h, axis=1, keepdims=True)
    scale = jnp.concatenate([inv[w]] * 4, axis=1)
    dflat[w] = (d * scale).astype(BF)


def labels(w, lat_last, lon_last):
    def flags(t):
        level = (t >= 72).astype(jnp.int32)
        t = t - 72 * level
        row = (t >= 36).astype(jnp.int32)
        t = t - 36 * row
        t = jnp.where(t >= 24, t - 24, jnp.where(t >= 12, t - 12, t))
        col = (t >= 6).astype(jnp.int32)
        return level * is_b + row * lat_last + col * last

    is_b = 4 * (w // 2)
    last = lon_last * (w % 2)
    klab = flags(lax.broadcasted_iota(jnp.int32, (144, 128), 0))
    lane = lax.broadcasted_iota(jnp.int32, (1, 128), 1) & 15
    qlab = [flags(lane + 16 * c) for c in range(9)]
    return klab, qlab


def kernel(tok, cot, w_qkv, w_proj, att, dflat, gqkv, gproj, hat, normed, inv, q, k, v, dc, qs, cs, pt, st, ctx, dqkv, sf, df):
    lat_last = 2 * (lax.axis_index("lat") == lax.axis_size("lat") - 1).astype(jnp.int32)
    lon_last = (lax.axis_index("lon") == lax.axis_size("lon") - 1).astype(jnp.int32)

    @pl.loop(0, 4)
    def _(w):
        project(w, tok, cot, w_qkv, w_proj, hat, normed, inv, q, k, v, dc)

    mask = head_mask(BF)
    maskf = head_mask(F32)

    @pl.loop(0, 8)
    def _(i):
        g, w = i // 4, i % 4
        klab, qlab = labels(w, lat_last, lon_last)
        attend(g, w, klab, qlab, mask, maskf, q, k, v, dc, qs, cs, pt, st, ctx, dqkv, sf, df)

    for g in range(2):
        gproj[256 * g : 256 * g + 256, :] = dot(ctx[g], cot[...], TN)
        for part in range(3):
            gqkv[:, 512 * part + 256 * g : 512 * part + 256 * g + 256] = dot(
                normed[...], dqkv[g, :, 256 * part : 256 * part + 256], TN
            )

    @pl.loop(0, 4)
    def _(w):
        finish(w, w_qkv, w_proj, hat, inv, ctx, dqkv, att, dflat)


def local_block(tok, cot, w_qkv, w_proj):
    vm = pl.BlockSpec(memory_space=pltpu.VMEM)
    return pl.pallas_call(
        kernel,
        out_shape=(
            jax.ShapeDtypeStruct((4, 144, 512), BF),
            jax.ShapeDtypeStruct((4, 144, 512), BF),
            jax.ShapeDtypeStruct((512, 1536), F32),
            jax.ShapeDtypeStruct((512, 512), F32),
        ),
        in_specs=[vm] * 4,
        out_specs=(vm,) * 4,
        scratch_shapes=[
            pltpu.VMEM((4, 144, 512), F32),
            pltpu.VMEM((576, 512), BF),
            pltpu.VMEM((4, 144, 128), F32),
            pltpu.VMEM((2, 4, 144, 256), BF),
            pltpu.VMEM((2, 4, 144, 256), BF),
            pltpu.VMEM((2, 4, 144, 256), BF),
            pltpu.VMEM((2, 4, 144, 256), BF),
            pltpu.VMEM((1152, 256), BF),
            pltpu.VMEM((1152, 256), BF),
            pltpu.VMEM((144, 1152), BF),
            pltpu.VMEM((144, 1152), BF),
            pltpu.VMEM((2, 576, 256), BF),
            pltpu.VMEM((2, 576, 768), BF),
            pltpu.VMEM((144, 1152), F32),
            pltpu.VMEM((144, 1152), F32),
        ],
        compiler_params=pltpu.CompilerParams(vmem_limit_bytes=56 * 2**20),
        name="window_block",
    )(tok, cot.reshape(576, 512), w_qkv, w_proj)
MESH = pl.DeviceIdType.MESH
NORM = 1.0 / 73728**0.5


def place():
    lat, lon = lax.axis_index("lat"), lax.axis_index("lon")
    return lat * 8 + lon // 2, lon % 2


def device(chip, core):
    return chip // 8, (chip % 8) * 2 + core


def drain(ref, sem):
    pltpu.make_async_copy(ref, ref, sem).wait()


def greet():
    chip, core = place()
    barrier = pltpu.get_barrier_semaphore()
    pl.semaphore_signal(barrier, inc=1, device_id=device(chip, 1 - core), device_id_type=MESH)

    @pl.loop(1, 64)
    def _(t):
        pl.semaphore_signal(barrier, inc=1, device_id=device(chip ^ t, core), device_id_type=MESH)

    pl.semaphore_wait(barrier, 64)


def core_swap(src, dst, send, recv):
    chip, core = place()
    return pltpu.make_async_remote_copy(
        src_ref=src, dst_ref=dst, send_sem=send, recv_sem=recv,
        device_id=device(chip, 1 - core), device_id_type=MESH,
    )


def scatter_start(mixed, parts, send, recv):
    chip, core = place()

    @pl.loop(1, 64)
    def _(t):
        pltpu.make_async_remote_copy(
            src_ref=mixed.at[chip ^ t], dst_ref=parts.at[chip], send_sem=send, recv_sem=recv,
            device_id=device(chip ^ t, core), device_id_type=MESH,
        ).start()


def gather_start(total, send, recv):
    chip, core = place()

    @pl.loop(1, 64)
    def _(t):
        pltpu.make_async_remote_copy(
            src_ref=total.at[core, chip], dst_ref=total.at[core, chip], send_sem=send, recv_sem=recv,
            device_id=device(chip ^ t, core), device_id_type=MESH,
        ).start()


def sum_kernel(grad_in, gqkv, gproj, grad, swapped, mixed, parts, total, send, recv):
    chip, core = place()
    greet()
    for g in range(2):
        grad[g] = grad_in[g]
        swap = core_swap(grad.at[g, 1 - core], swapped.at[g], send.at[g, 0], recv.at[g, 0])
        swap.start()
        swap.wait()
        mixed[g] = (grad[g, core].astype(F32) + swapped[g].astype(F32)).astype(BF)
        scatter_start(mixed.at[g], parts.at[g], send.at[g, 1], recv.at[g, 1])
        parts[g, chip] = mixed[g, chip]
    for g in range(2):
        drain(parts.at[g, pl.ds(0, 63)], recv.at[g, 1])
        acc = jnp.sum(parts[g].astype(F32), axis=0) * NORM
        total[g, core, chip] = acc.astype(BF)
        gather_start(total.at[g], send.at[g, 2], recv.at[g, 2])
    for g in range(2):
        drain(parts.at[g, pl.ds(0, 63)], recv.at[g, 2])
        swap = core_swap(total.at[g, core], total.at[g, core], send.at[g, 3], recv.at[g, 3])
        swap.start()
        swap.wait()
        for part in range(3):
            at = 512 * part + 256 * g
            gqkv[:, at : at + 256] = rows_of(total, g, 512 * part, 512)
        for half in range(2):
            gproj[256 * g : 256 * g + 256, 256 * half : 256 * half + 256] = rows_of(total, g, 1536 + 256 * half, 256)
        for i in range(1, 3):
            drain(parts.at[g, pl.ds(0, 63)], send.at[g, i])


def rows_of(total, g, start, count):
    first, n = start // 16, count // 16
    pieces = []
    for half in range(2):
        lo, hi = max(first, 64 * half), min(first + n, 64 * half + 64)
        if lo < hi:
            pieces.append(total[g, half, lo - 64 * half : hi - 64 * half].reshape(-1, 256))
    return jnp.concatenate(pieces, axis=0).astype(F32)


def sum_over_devices(gqkv, gproj):
    halves = []
    for g in range(2):
        at = slice(256 * g, 256 * g + 256)
        halves.append(jnp.concatenate(
            [gqkv[:, 512 * part :][:, at] for part in range(3)] + [gproj[at, :256], gproj[at, 256:]], axis=0
        ).astype(BF))
    grad = jnp.stack(halves).reshape(2, 2, 64, 16, 256)
    vm = pl.BlockSpec(memory_space=pltpu.VMEM)
    return pl.pallas_call(
        sum_kernel,
        out_shape=(jax.ShapeDtypeStruct((512, 1536), F32), jax.ShapeDtypeStruct((512, 512), F32)),
        in_specs=[vm],
        out_specs=(vm, vm),
        scratch_shapes=[
            pltpu.VMEM((2, 2, 64, 16, 256), BF),
            pltpu.VMEM((2, 64, 16, 256), BF),
            pltpu.VMEM((2, 64, 16, 256), BF),
            pltpu.VMEM((2, 64, 16, 256), BF),
            pltpu.VMEM((2, 2, 64, 16, 256), BF),
            pltpu.SemaphoreType.DMA((2, 4)),
            pltpu.SemaphoreType.DMA((2, 4)),
        ],
        compiler_params=pltpu.CompilerParams(
            vmem_limit_bytes=56 * 2**20, collective_id=0, has_side_effects=True
        ),
        name="sum_gradients",
    )(grad)


from jax.sharding import PartitionSpec as P


def shifted(value, axis, steps):
    count = lax.axis_size(axis)
    pairs = [(source, (source + steps) % count) for source in range(count)]
    return lax.ppermute(value, axis, pairs)


def to_windows(field):
    levels, rows, cols, width = field.shape
    field = field.reshape(levels // 2, 2, rows // 6, 6, cols // 12, 12, width)
    return field.transpose(0, 2, 4, 1, 3, 5, 6).reshape(-1, 144, width)


def from_windows(field, levels, rows, cols):
    field = field.reshape(levels // 2, rows // 6, cols // 12, 2, 6, 12, -1)
    return field.transpose(0, 3, 1, 4, 2, 5, 6).reshape(levels, rows, cols, -1)


def roll_in(x):
    x = jnp.concatenate([x[:, 3:], shifted(x[:, :3], "lat", -1)], axis=1)
    x = jnp.concatenate([x[:, :, 6:], shifted(x[:, :, :6], "lon", -1)], axis=2)
    return jnp.roll(x, -1, axis=0)


def roll_out(x):
    x = jnp.roll(x, 1, axis=0)
    x = jnp.concatenate([shifted(x[:, :, -6:], "lon", 1), x[:, :, :-6]], axis=2)
    return jnp.concatenate([shifted(x[:, -3:], "lat", 1), x[:, :-3]], axis=1)


def body(tokens, cotangent, w_qkv, w_proj):
    tok = to_windows(roll_in(tokens))
    cot = to_windows(roll_in(cotangent))
    att, dflat, gqkv, gproj = local_block(tok, cot, w_qkv, w_proj)
    att = roll_out(from_windows(att, 4, 6, 24))
    dflat = roll_out(from_windows(dflat, 4, 6, 24))
    output = (tokens.astype(F32) + att.astype(F32)).astype(BF)
    grad_tokens = (cotangent.astype(F32) + dflat.astype(F32)).astype(BF)
    gqkv, gproj = sum_over_devices(gqkv, gproj)
    return (output, grad_tokens, gqkv, gproj)


def solution(mesh):
    spec = P(None, "lat", "lon", None)
    return jax.shard_map(
        body,
        mesh=mesh,
        in_specs=(spec, spec, P(), P()),
        out_specs=(spec, spec, P(), P()),
        check_vma=False,
    )
```

```python
import numpy as np
import jax
import jax.numpy as jnp
from jax import lax
from jax.experimental import pallas as pl
from jax.experimental.pallas import tpu as pltpu
from jax.sharding import PartitionSpec as P

BF = jnp.bfloat16
F32 = jnp.float32
SCALE = 1.0 / 32**0.5
EXP2 = SCALE * 1.4426950408889634
NORM = 1.0 / 73728**0.5
NN = (((1,), (0,)), ((), ()))
NT = (((1,), (1,)), ((), ()))
TN = (((0,), (0,)), ((), ()))
MESH = pl.DeviceIdType.MESH

STARTS = (0, 224, 448, 528)
ROWS = 608
SECTIONS = ((224, 224), (448, 80), (528, 80))


def section_row(array, level, row, col):
    section = (2 if col < 6 else 0) + (1 if row < 3 else 0)
    width, first = (18, 6) if col >= 6 else (6, 0)
    at = (level * 3 + row % 3) * width + col - first
    return STARTS[section] + array * 6 * width + at


def orders():
    pack = np.zeros((ROWS, 576), np.float32)
    place = np.zeros((576, ROWS), np.float32)
    for array in range(2):
        for level in range(2):
            for row in range(6):
                for col in range(24):
                    at = array * 288 + level * 144 + row * 24 + col
                    pack[section_row(array, level, row, col), at] = 1
            for row in range(6):
                for col in range(24):
                    at = array * 288 + col // 12 * 144 + level * 72 + row * 12 + col % 12
                    source = section_row(array, level, (row + 3) % 6, (col + 6) % 24)
                    place[at, source] = 1
    return [jnp.asarray(m, BF) for m in (pack, place, place.T, pack.T)]


def dot(a, b, dims=NN):
    return lax.dot_general(a, b, dims, preferred_element_type=F32)


def head_mask(dtype):
    head = lax.broadcasted_iota(jnp.int32, (128, 256), 0) >> 4
    col = lax.broadcasted_iota(jnp.int32, (128, 256), 1) >> 5
    return (head == col).astype(dtype)


def window_rows(w):
    return pl.ds(pl.multiple_of(w * 144, 16), 144)


def project(w, tok, cot, w_qkv, w_proj, hat, normed, inv, q, k, v, dc):
    x = tok[window_rows(w), :].astype(F32)
    x = x - jnp.mean(x, axis=1, keepdims=True)
    scale = lax.rsqrt(jnp.mean(x * x, axis=1, keepdims=True) + 1e-05)
    x = x * scale
    hat[w] = x
    inv[w] = jnp.broadcast_to(scale, (144, 128))
    x = x.astype(BF)
    rows = window_rows(w)
    normed[rows, :] = x
    for part, ref in enumerate((q, k, v)):
        for g in range(2):
            at = 512 * part + 256 * g
            ref[g, w] = dot(x, w_qkv[:, at : at + 256]).astype(BF)
    c = cot[rows, :]
    for g in range(2):
        dc[g, w] = dot(c, w_proj[256 * g : 256 * g + 256, :], NT).astype(BF)


def attend(g, w, lat_last, lon_last, mask, maskf, q, k, v, dc, qs, cs, pt, st, sf, df, ctx, dqkv):
    klab, qlab = labels(w, lat_last, lon_last)
    keys = k[g, w]
    vals = v[g, w]
    rows = window_rows(w)
    for c in range(9):
        at = slice(128 * c, 128 * c + 128)
        q16 = q[g, w, 16 * c : 16 * c + 16, :]
        d16 = dc[g, w, 16 * c : 16 * c + 16, :]
        qs[at, :] = jnp.concatenate([q16] * 8, axis=0) * mask
        cs[at, :] = jnp.concatenate([d16] * 8, axis=0) * mask
    sf[...] = dot(keys, qs[...], NT)
    df[...] = dot(vals, cs[...], NT)
    for c in range(9):
        at = slice(128 * c, 128 * c + 128)
        s = sf[:, at]
        s = jnp.where(klab == qlab[c], s, -1e30)
        e = jnp.exp2((s - jnp.max(s, axis=0, keepdims=True)) * EXP2)
        p = e * (1.0 / jnp.sum(e, axis=0, keepdims=True))
        pt[:, at] = p.astype(BF)
        dp = df[:, at]
        inner = jnp.sum(p * dp, axis=0, keepdims=True)
        st[:, at] = ((p * SCALE) * (dp - inner)).astype(BF)
    out = dot(pt[...], vals, TN).reshape(9, 8, 16, 256) * maskf.reshape(1, 8, 16, 256)
    ctx[g, rows, :] = jnp.sum(out, axis=1).reshape(144, 256).astype(BF)
    out = dot(st[...], keys, TN).reshape(9, 8, 16, 256) * maskf.reshape(1, 8, 16, 256)
    dqkv[g, rows, 0:256] = jnp.sum(out, axis=1).reshape(144, 256).astype(BF)
    dqkv[g, rows, 256:512] = dot(st[...], qs[...]).astype(BF)
    dqkv[g, rows, 512:768] = dot(pt[...], cs[...]).astype(BF)


def finish(p, i, w_qkv, w_proj, hat, inv, ctx, dqkv, done):
    w = 2 * p + i
    rows = window_rows(w)
    a = dot(ctx[0, rows, :], w_proj[0:256, :]) + dot(ctx[1, rows, :], w_proj[256:512, :])
    done[p, window_rows(i), :] = a.astype(BF)
    d = None
    for g in range(2):
        for part in range(3):
            at = 512 * part + 256 * g
            t = dot(dqkv[g, rows, 256 * part : 256 * part + 256], w_qkv[:, at : at + 256], NT)
            d = t if d is None else d + t
    h = hat[w]
    d = d - jnp.mean(d, axis=1, keepdims=True) - h * jnp.mean(d * h, axis=1, keepdims=True)
    scale = jnp.concatenate([inv[w]] * 4, axis=1)
    done[p, window_rows(2 + i), :] = (d * scale).astype(BF)


def labels(w, lat_last, lon_last):
    def flags(t):
        level = (t >= 72).astype(jnp.int32)
        t = t - 72 * level
        row = (t >= 36).astype(jnp.int32)
        t = t - 36 * row
        t = jnp.where(t >= 24, t - 24, jnp.where(t >= 12, t - 12, t))
        col = (t >= 6).astype(jnp.int32)
        return level * is_b + row * lat_last + col * last

    is_b = 4 * (w // 2)
    last = lon_last * (w % 2)
    klab = flags(lax.broadcasted_iota(jnp.int32, (144, 128), 0))
    lane = lax.broadcasted_iota(jnp.int32, (1, 128), 1) & 15
    qlab = [flags(lane + 16 * c) for c in range(9)]
    return klab, qlab


def weight_gradients(g, normed, cot, ctx, dqkv, grad):
    for part in range(3):
        d = dot(normed[...], dqkv[g, :, 256 * part : 256 * part + 256], TN).astype(BF)
        at = 32 * (part % 2)
        grad[g, part // 2, at : at + 32] = d.reshape(32, 16, 256)
    for half in range(2):
        d = dot(ctx[g], cot[:, 256 * half : 256 * half + 256], TN).astype(BF)
        at = 32 + 16 * half
        grad[g, 1, at : at + 16] = d.reshape(16, 16, 256)


def place():
    lat, lon = lax.axis_index("lat"), lax.axis_index("lon")
    return lat * 8 + lon // 2, lon % 2


def device(chip, core):
    return chip // 8, (chip % 8) * 2 + core


def beside(lat_step, lon_step):
    lat, lon = lax.axis_index("lat"), lax.axis_index("lon")
    return lax.rem(lat + lat_step + 8, 8), lax.rem(lon + lon_step + 16, 16)


def drain(ref, sem):
    pltpu.make_async_copy(ref, ref, sem).wait()


def greet():
    chip, core = place()
    barrier = pltpu.get_barrier_semaphore()
    for steps in ((0, -1), (0, 1), (-1, -1), (1, 1)):
        pl.semaphore_signal(barrier, inc=1, device_id=beside(*steps), device_id_type=MESH)
    pl.semaphore_signal(barrier, inc=1, device_id=device(chip, 1 - core), device_id_type=MESH)

    @pl.loop(1, 64)
    def _(t):
        pl.semaphore_signal(barrier, inc=1, device_id=device(chip ^ t, core), device_id_type=MESH)


def meet():
    pl.semaphore_wait(pltpu.get_barrier_semaphore(), 68)


def halo(p, step, src, dst, send, recv):
    copies = []
    for s, (at, count) in enumerate(SECTIONS):
        lat_step, lon_step = ((step, 0), (0, step), (step, step))[s]
        copies.append(pltpu.make_async_remote_copy(
            src_ref=src.at[p, pl.ds(at, count)], dst_ref=dst.at[p, pl.ds(at, count)],
            send_sem=send.at[p, s], recv_sem=recv.at[p, s],
            device_id=beside(lat_step, lon_step), device_id_type=MESH,
        ))
    return copies


def core_swap(src, dst, send, recv):
    chip, core = place()
    return pltpu.make_async_remote_copy(
        src_ref=src, dst_ref=dst, send_sem=send, recv_sem=recv,
        device_id=device(chip, 1 - core), device_id_type=MESH,
    )


def scatter_start(mixed, parts, send, recv):
    chip, core = place()

    @pl.loop(1, 64)
    def _(t):
        pltpu.make_async_remote_copy(
            src_ref=mixed.at[chip ^ t], dst_ref=parts.at[chip], send_sem=send, recv_sem=recv,
            device_id=device(chip ^ t, core), device_id_type=MESH,
        ).start()


def gather_start(total, send, recv):
    chip, core = place()

    @pl.loop(1, 64)
    def _(t):
        pltpu.make_async_remote_copy(
            src_ref=total.at[core, chip], dst_ref=total.at[core, chip], send_sem=send, recv_sem=recv,
            device_id=device(chip ^ t, core), device_id_type=MESH,
        ).start()


def kernel(
    tokens, cotangent, w_qkv_in, w_proj_in, pack_in, place_in, unplace_in, unpack_in,
    att, dflat, total,
    both, w_qkv, w_proj, pack, place_m, unplace, unpack, out_halo, in_halo, out_back, in_back,
    tok, cot, hat, normed, inv, q, k, v, dc, qs, cs, pt, st, sf, df, ctx, dqkv, done,
    grad, swapped, mixed, parts, load, send, recv, hsend, hrecv, bsend, brecv,
):
    chip, core = place()
    greet()
    loads = []

    def fetch(src, dst):
        copy = pltpu.make_async_copy(src, dst, load.at[len(loads)])
        copy.start()
        loads.append(copy)

    for p in range(2):
        for half, src in enumerate((tokens, cotangent)):
            for level in range(2):
                fetch(
                    src.at[pl.ds(144 * ((2 * p + 1 + level) % 4), 144)],
                    both.at[p, pl.ds(288 * half + 144 * level, 144)],
                )
    fetch(pack_in, pack)
    early = len(loads)
    fetch(place_in, place_m)
    fetch(w_qkv_in, w_qkv)
    fetch(w_proj_in, w_proj)
    fetch(unplace_in, unplace)
    fetch(unpack_in, unpack)
    for copy in loads[:early]:
        copy.wait()
    out_halo[0] = dot(pack[...], both[0]).astype(BF)
    meet()
    coming = [halo(p, -1, out_halo, in_halo, hsend, hrecv) for p in range(2)]
    for copy in coming[0]:
        copy.start()
    out_halo[1] = dot(pack[...], both[1]).astype(BF)
    for copy in coming[1]:
        copy.start()
    for copy in loads[early:]:
        copy.wait()
    lat_last = 2 * (lax.axis_index("lat") == 7).astype(jnp.int32)
    lon_last = (lax.axis_index("lon") == 15).astype(jnp.int32)
    mask = head_mask(BF)
    maskf = head_mask(F32)

    def arrive(p):
        in_halo[p, 0:224] = out_halo[p, 0:224]
        for copy in coming[p]:
            copy.wait_recv()
        tok[288 * p : 288 * p + 288, :] = dot(place_m[0:288, :], in_halo[p]).astype(BF)
        cot[288 * p : 288 * p + 288, :] = dot(place_m[288:576, :], in_halo[p]).astype(BF)

        @pl.loop(2 * p, 2 * p + 2)
        def _(w):
            project(w, tok, cot, w_qkv, w_proj, hat, normed, inv, q, k, v, dc)

    def attention(g, w):
        attend(g, w, lat_last, lon_last, mask, maskf, q, k, v, dc, qs, cs, pt, st, sf, df, ctx, dqkv)

    def swap_in(g):
        return core_swap(grad.at[g, 1 - core], swapped.at[g], send.at[g, 0], recv.at[g, 0])

    def mix(g):
        swap_in(g).wait()
        mixed[g] = (grad[g, core].astype(F32) + swapped[g].astype(F32)).astype(BF)
        scatter_start(mixed.at[g], parts.at[g], send.at[g, 1], recv.at[g, 1])
        parts[g, chip] = mixed[g, chip]

    def leave(p):
        @pl.loop(0, 2)
        def _(i):
            finish(p, i, w_qkv, w_proj, hat, inv, ctx, dqkv, done)

        out_back[p] = dot(unplace[...], done[p]).astype(BF)
        for copy in going[p]:
            copy.start()

    going = [halo(p, 1, out_back, in_back, bsend, brecv) for p in range(2)]
    arrive(0)

    @pl.loop(0, 4)
    def _(i):
        attention(i // 2, i % 2)

    arrive(1)

    @pl.loop(0, 2)
    def _(g):
        @pl.loop(2, 4)
        def _(w):
            attention(g, w)

        weight_gradients(g, normed, cot, ctx, dqkv, grad)
        swap_in(g).start()

        @pl.when(g == 1)
        def _():
            mix(0)

    leave(0)
    mix(1)
    leave(1)
    for g in range(2):
        drain(parts.at[g, pl.ds(0, 63)], recv.at[g, 1])
        acc = jnp.sum(parts[g].astype(F32), axis=0) * NORM
        total[g, core, chip] = acc.astype(BF)
        gather_start(total.at[g], send.at[g, 2], recv.at[g, 2])
    for p in range(2):
        in_back[p, 0:224] = out_back[p, 0:224]
        for copy in going[p]:
            copy.wait_recv()
        for half, out in enumerate((att, dflat)):
            for level in range(2):
                at = 144 * ((2 * p + 1 + level) % 4)
                rows = slice(288 * half + 144 * level, 288 * half + 144 * level + 144)
                out[at : at + 144, :] = dot(unpack[rows, :], in_back[p]).astype(BF)
    swaps = []
    for g in range(2):
        drain(parts.at[g, pl.ds(0, 63)], recv.at[g, 2])
        swaps.append(core_swap(total.at[g, core], total.at[g, core], send.at[g, 3], recv.at[g, 3]))
        swaps[g].start()
    for g in range(2):
        swaps[g].wait()
        for i in range(1, 3):
            drain(parts.at[g, pl.ds(0, 63)], send.at[g, i])
    for p in range(2):
        for copy in coming[p] + going[p]:
            copy.wait_send()


def block(tokens, cotangent, w_qkv, w_proj):
    hbm = pl.BlockSpec(memory_space=pl.ANY)
    vm = pl.BlockSpec(memory_space=pltpu.VMEM)
    dma = pltpu.SemaphoreType.DMA
    return pl.pallas_call(
        kernel,
        out_shape=(
            jax.ShapeDtypeStruct((576, 512), BF),
            jax.ShapeDtypeStruct((576, 512), BF),
            jax.ShapeDtypeStruct((2, 2, 64, 16, 256), BF),
        ),
        in_specs=[hbm] * 8,
        out_specs=(vm,) * 3,
        scratch_shapes=[
            pltpu.VMEM((2, 576, 512), BF),
            pltpu.VMEM((512, 1536), BF),
            pltpu.VMEM((512, 512), BF),
            pltpu.VMEM((ROWS, 576), BF),
            pltpu.VMEM((576, ROWS), BF),
            pltpu.VMEM((ROWS, 576), BF),
            pltpu.VMEM((576, ROWS), BF),
            pltpu.VMEM((2, ROWS, 512), BF),
            pltpu.VMEM((2, ROWS, 512), BF),
            pltpu.VMEM((2, ROWS, 512), BF),
            pltpu.VMEM((2, ROWS, 512), BF),
            pltpu.VMEM((576, 512), BF),
            pltpu.VMEM((576, 512), BF),
            pltpu.VMEM((4, 144, 512), F32),
            pltpu.VMEM((576, 512), BF),
            pltpu.VMEM((4, 144, 128), F32),
            pltpu.VMEM((2, 4, 144, 256), BF),
            pltpu.VMEM((2, 4, 144, 256), BF),
            pltpu.VMEM((2, 4, 144, 256), BF),
            pltpu.VMEM((2, 4, 144, 256), BF),
            pltpu.VMEM((1152, 256), BF),
            pltpu.VMEM((1152, 256), BF),
            pltpu.VMEM((144, 1152), BF),
            pltpu.VMEM((144, 1152), BF),
            pltpu.VMEM((144, 1152), F32),
            pltpu.VMEM((144, 1152), F32),
            pltpu.VMEM((2, 576, 256), BF),
            pltpu.VMEM((2, 576, 768), BF),
            pltpu.VMEM((2, 576, 512), BF),
            pltpu.VMEM((2, 2, 64, 16, 256), BF),
            pltpu.VMEM((2, 64, 16, 256), BF),
            pltpu.VMEM((2, 64, 16, 256), BF),
            pltpu.VMEM((2, 64, 16, 256), BF),
            dma((16,)),
            dma((2, 4)),
            dma((2, 4)),
            dma((2, 3)),
            dma((2, 3)),
            dma((2, 3)),
            dma((2, 3)),
        ],
        compiler_params=pltpu.CompilerParams(
            vmem_limit_bytes=56 * 2**20, collective_id=0, has_side_effects=True
        ),
        name="window_block",
    )(tokens, cotangent, w_qkv, w_proj, *orders())


def body(tokens, cotangent, w_qkv, w_proj):
    shape = tokens.shape
    att, dflat, total = block(tokens.reshape(576, 512), cotangent.reshape(576, 512), w_qkv, w_proj)
    output = (tokens.astype(F32) + att.reshape(shape).astype(F32)).astype(BF)
    grad_tokens = (cotangent.astype(F32) + dflat.reshape(shape).astype(F32)).astype(BF)
    total = total.reshape(2, 2048, 256)
    gqkv = total[:, :1536].reshape(2, 3, 512, 256).transpose(2, 1, 0, 3).reshape(512, 1536)
    gproj = total[:, 1536:].reshape(2, 2, 256, 256).transpose(0, 2, 1, 3).reshape(512, 512)
    return (output, grad_tokens, gqkv.astype(F32), gproj.astype(F32))


def solution(mesh):
    spec = P(None, "lat", "lon", None)
    return jax.shard_map(
        body,
        mesh=mesh,
        in_specs=(spec, spec, P(), P()),
        out_specs=(spec, spec, P(), P()),
        check_vma=False,
    )
```

```python
import numpy as np
import jax
import jax.numpy as jnp
from jax import lax
from jax.experimental import pallas as pl
from jax.experimental.pallas import tpu as pltpu
from jax.sharding import PartitionSpec as P

BF = jnp.bfloat16
F32 = jnp.float32
SCALE = 1.0 / 32**0.5
EXP2 = SCALE * 1.4426950408889634
NORM = 1.0 / 73728**0.5
NN = (((1,), (0,)), ((), ()))
NT = (((1,), (1,)), ((), ()))
TN = (((0,), (0,)), ((), ()))
MESH = pl.DeviceIdType.MESH

STARTS = (0, 224, 448, 528)
ROWS = 608
SECTIONS = ((224, 224), (448, 80), (528, 80))


def section_row(array, level, row, col):
    section = (2 if col < 6 else 0) + (1 if row < 3 else 0)
    width, first = (18, 6) if col >= 6 else (6, 0)
    at = (level * 3 + row % 3) * width + col - first
    return STARTS[section] + array * 6 * width + at


def orders():
    pack = np.zeros((ROWS, 576), np.float32)
    place = np.zeros((576, ROWS), np.float32)
    for array in range(2):
        for level in range(2):
            for row in range(6):
                for col in range(24):
                    at = array * 288 + level * 144 + row * 24 + col
                    pack[section_row(array, level, row, col), at] = 1
            for row in range(6):
                for col in range(24):
                    at = array * 288 + col // 12 * 144 + level * 72 + row * 12 + col % 12
                    source = section_row(array, level, (row + 3) % 6, (col + 6) % 24)
                    place[at, source] = 1
    return [jnp.asarray(m, BF) for m in (pack, place, place.T, pack.T)]


def dot(a, b, dims=NN):
    return lax.dot_general(a, b, dims, preferred_element_type=F32)


def head_mask(dtype):
    head = lax.broadcasted_iota(jnp.int32, (128, 256), 0) >> 4
    col = lax.broadcasted_iota(jnp.int32, (128, 256), 1) >> 5
    return (head == col).astype(dtype)


def window_rows(w):
    return pl.ds(pl.multiple_of(w * 144, 16), 144)


def project(w, tok, cot, w_qkv, w_proj, hat, normed, inv, q, k, v, dc):
    x = tok[window_rows(w), :].astype(F32)
    x = x - jnp.mean(x, axis=1, keepdims=True)
    scale = lax.rsqrt(jnp.mean(x * x, axis=1, keepdims=True) + 1e-05)
    x = x * scale
    hat[w] = x
    inv[w] = jnp.broadcast_to(scale, (144, 128))
    x = x.astype(BF)
    rows = window_rows(w)
    normed[rows, :] = x
    for part, ref in enumerate((q, k, v)):
        for g in range(2):
            at = 512 * part + 256 * g
            ref[g, w] = dot(x, w_qkv[:, at : at + 256]).astype(BF)
    c = cot[rows, :]
    for g in range(2):
        dc[g, w] = dot(c, w_proj[256 * g : 256 * g + 256, :], NT).astype(BF)


def attend(g, w, lat_last, lon_last, mask, maskf, q, k, v, dc, qs, cs, pt, st, sf, df, ctx, dqkv):
    klab, qlab = labels(w, lat_last, lon_last)
    keys = k[g, w]
    vals = v[g, w]
    rows = window_rows(w)
    for c in range(9):
        at = slice(128 * c, 128 * c + 128)
        q16 = q[g, w, 16 * c : 16 * c + 16, :]
        d16 = dc[g, w, 16 * c : 16 * c + 16, :]
        qs[at, :] = jnp.concatenate([q16] * 8, axis=0) * mask
        cs[at, :] = jnp.concatenate([d16] * 8, axis=0) * mask
    sf[...] = dot(keys, qs[...], NT)
    df[...] = dot(vals, cs[...], NT)
    for c in range(9):
        at = slice(128 * c, 128 * c + 128)
        s = sf[:, at]
        s = jnp.where(klab == qlab[c], s, -1e30)
        e = jnp.exp2((s - jnp.max(s, axis=0, keepdims=True)) * EXP2)
        p = e * (1.0 / jnp.sum(e, axis=0, keepdims=True))
        pt[:, at] = p.astype(BF)
        dp = df[:, at]
        inner = jnp.sum(p * dp, axis=0, keepdims=True)
        st[:, at] = ((p * SCALE) * (dp - inner)).astype(BF)
    out = dot(pt[...], vals, TN).reshape(9, 8, 16, 256) * maskf.reshape(1, 8, 16, 256)
    ctx[g, rows, :] = jnp.sum(out, axis=1).reshape(144, 256).astype(BF)
    out = dot(st[...], keys, TN).reshape(9, 8, 16, 256) * maskf.reshape(1, 8, 16, 256)
    dqkv[g, rows, 0:256] = jnp.sum(out, axis=1).reshape(144, 256).astype(BF)
    dqkv[g, rows, 256:512] = dot(st[...], qs[...]).astype(BF)
    dqkv[g, rows, 512:768] = dot(pt[...], cs[...]).astype(BF)


def finish(p, i, w_qkv, w_proj, hat, inv, ctx, dqkv, done):
    w = 2 * p + i
    rows = window_rows(w)
    a = dot(ctx[0, rows, :], w_proj[0:256, :]) + dot(ctx[1, rows, :], w_proj[256:512, :])
    done[p, window_rows(i), :] = a.astype(BF)
    d = None
    for g in range(2):
        for part in range(3):
            at = 512 * part + 256 * g
            t = dot(dqkv[g, rows, 256 * part : 256 * part + 256], w_qkv[:, at : at + 256], NT)
            d = t if d is None else d + t
    h = hat[w]
    d = d - jnp.mean(d, axis=1, keepdims=True) - h * jnp.mean(d * h, axis=1, keepdims=True)
    scale = jnp.concatenate([inv[w]] * 4, axis=1)
    done[p, window_rows(2 + i), :] = (d * scale).astype(BF)


def labels(w, lat_last, lon_last):
    def flags(t):
        level = (t >= 72).astype(jnp.int32)
        t = t - 72 * level
        row = (t >= 36).astype(jnp.int32)
        t = t - 36 * row
        t = jnp.where(t >= 24, t - 24, jnp.where(t >= 12, t - 12, t))
        col = (t >= 6).astype(jnp.int32)
        return level * is_b + row * lat_last + col * last

    is_b = 4 * (w // 2)
    last = lon_last * (w % 2)
    klab = flags(lax.broadcasted_iota(jnp.int32, (144, 128), 0))
    lane = lax.broadcasted_iota(jnp.int32, (1, 128), 1) & 15
    qlab = [flags(lane + 16 * c) for c in range(9)]
    return klab, qlab


def weight_gradients(g, normed, cot, ctx, dqkv, grad):
    def keep(d, half, at, count):
        for b in range(2):
            piece = d[:, 128 * b : 128 * b + 128].astype(BF)
            grad[g, half, b, at : at + count] = piece.reshape(count, 16, 128)

    for part in range(3):
        d = dot(normed[...], dqkv[g, :, 256 * part : 256 * part + 256], TN)
        keep(d, part // 2, 32 * (part % 2), 32)
    for half in range(2):
        d = dot(ctx[g], cot[:, 256 * half : 256 * half + 256], TN)
        keep(d, 1, 32 + 16 * half, 16)


def place():
    lat, lon = lax.axis_index("lat"), lax.axis_index("lon")
    return (lon // 2) % 4, (lon // 8) * 2 + lat % 2, lat // 2, lon % 2


def device(x, y, z, core):
    return z * 2 + y % 2, ((y // 2) * 4 + x) * 2 + core


def first_at(b):
    x, y, z, core = place()
    return x if b == 0 else z


def first_device(b, to):
    x, y, z, core = place()
    return device(to, y, z, core) if b == 0 else device(x, y, to, core)


def second_at(b):
    x, y, z, core = place()
    return y * 4 + (z if b == 0 else x)


def second_device(b, to):
    x, y, z, core = place()
    return device(x, to // 4, to % 4, core) if b == 0 else device(to % 4, to // 4, z, core)


def beside(lat_step, lon_step):
    lat, lon = lax.axis_index("lat"), lax.axis_index("lon")
    return lax.rem(lat + lat_step + 8, 8), lax.rem(lon + lon_step + 16, 16)


def drain(ref, sem):
    pltpu.make_async_copy(ref, ref, sem).wait()


def greet():
    x, y, z, core = place()
    barrier = pltpu.get_barrier_semaphore()

    def signal(to):
        pl.semaphore_signal(barrier, inc=1, device_id=to, device_id_type=MESH)

    for steps in ((-1, 0), (0, -1), (-1, -1), (1, 0), (0, 1), (1, 1)):
        signal(beside(*steps))
    signal(device(x, y, z, 1 - core))
    for b in range(2):
        for k in range(1, 4):
            signal(first_device(b, first_at(b) ^ k))

        @pl.loop(1, 16)
        def _(t):
            signal(second_device(b, second_at(b) ^ t))


def meet():
    pl.semaphore_wait(pltpu.get_barrier_semaphore(), 43)


def halo(p, step, src, dst, send, recv):
    copies = []
    for s, (at, count) in enumerate(SECTIONS):
        lat_step, lon_step = ((step, 0), (0, step), (step, step))[s]
        copies.append(pltpu.make_async_remote_copy(
            src_ref=src.at[p, pl.ds(at, count)], dst_ref=dst.at[p, pl.ds(at, count)],
            send_sem=send.at[p, s], recv_sem=recv.at[p, s],
            device_id=beside(lat_step, lon_step), device_id_type=MESH,
        ))
    return copies


def core_swap(src, dst, send, recv):
    x, y, z, core = place()
    return pltpu.make_async_remote_copy(
        src_ref=src, dst_ref=dst, send_sem=send, recv_sem=recv,
        device_id=device(x, y, z, 1 - core), device_id_type=MESH,
    )


def scatter_first(mixed, parts, send, recv):
    for b in range(2):
        at = first_at(b)
        for k in (2, 1, 3):
            pltpu.make_async_remote_copy(
                src_ref=mixed.at[b, pl.ds((at ^ k) * 16, 16)], dst_ref=parts.at[b, at],
                send_sem=send.at[b], recv_sem=recv.at[b],
                device_id=first_device(b, at ^ k), device_id_type=MESH,
            ).start()


def scatter_second(mixed, parts, send, recv):
    for b in range(2):
        at = second_at(b)

        @pl.loop(0, 15)
        def _(t):
            to = at ^ (15 - t)
            pltpu.make_async_remote_copy(
                src_ref=mixed.at[b, to], dst_ref=parts.at[b, at],
                send_sem=send.at[b], recv_sem=recv.at[b],
                device_id=second_device(b, to), device_id_type=MESH,
            ).start()


def gather_second(total, send, recv):
    for b in range(2):
        at = second_at(b)
        piece = total.at[b, first_at(b) * 16 + at]

        @pl.loop(0, 15)
        def _(t):
            pltpu.make_async_remote_copy(
                src_ref=piece, dst_ref=piece, send_sem=send.at[b], recv_sem=recv.at[b],
                device_id=second_device(b, at ^ (15 - t)), device_id_type=MESH,
            ).start()


def gather_first(total, send, recv):
    for b in range(2):
        at = first_at(b)
        piece = total.at[b, pl.ds(at * 16, 16)]
        for k in (2, 1, 3):
            pltpu.make_async_remote_copy(
                src_ref=piece, dst_ref=piece, send_sem=send.at[b], recv_sem=recv.at[b],
                device_id=first_device(b, at ^ k), device_id_type=MESH,
            ).start()


def kernel(
    tokens, cotangent, w_qkv_in, w_proj_in, pack_in, place_in, unplace_in, unpack_in,
    output, grad_tokens, gqkv, gproj,
    both, w_qkv, w_proj, pack, place_m, unplace, unpack, out_halo, in_halo, out_back, in_back,
    tok, cot, hat, normed, inv, q, k, v, dc, qs, cs, pt, st, sf, df, ctx, dqkv, done,
    grad, swapped, mixed, parts, mixed2, parts2, total, load, swap_send, swap_recv, send, recv, hsend, hrecv, bsend, brecv,
):
    x, y, z, core = place()
    greet()
    loads = []

    def fetch(src, dst):
        copy = pltpu.make_async_copy(src, dst, load.at[len(loads)])
        copy.start()
        loads.append(copy)

    for p in range(2):
        for half, src in enumerate((tokens, cotangent)):
            for level in range(2):
                fetch(
                    src.at[pl.ds(144 * ((2 * p + 1 + level) % 4), 144)],
                    both.at[p, pl.ds(288 * half + 144 * level, 144)],
                )
    fetch(pack_in, pack)
    early = len(loads)
    fetch(place_in, place_m)
    fetch(w_qkv_in, w_qkv)
    fetch(w_proj_in, w_proj)
    fetch(unplace_in, unplace)
    fetch(unpack_in, unpack)
    for copy in loads[:early]:
        copy.wait()
    out_halo[0] = dot(pack[...], both[0]).astype(BF)
    meet()
    coming = [halo(p, -1, out_halo, in_halo, hsend, hrecv) for p in range(2)]
    for copy in coming[0]:
        copy.start()
    out_halo[1] = dot(pack[...], both[1]).astype(BF)
    for copy in coming[1]:
        copy.start()
    for copy in loads[early:]:
        copy.wait()
    lat_last = 2 * (lax.axis_index("lat") == 7).astype(jnp.int32)
    lon_last = (lax.axis_index("lon") == 15).astype(jnp.int32)
    mask = head_mask(BF)
    maskf = head_mask(F32)

    def arrive(p):
        in_halo[p, 0:224] = out_halo[p, 0:224]
        for copy in coming[p]:
            copy.wait_recv()
        tok[288 * p : 288 * p + 288, :] = dot(place_m[0:288, :], in_halo[p]).astype(BF)
        cot[288 * p : 288 * p + 288, :] = dot(place_m[288:576, :], in_halo[p]).astype(BF)

        @pl.loop(2 * p, 2 * p + 2)
        def _(w):
            project(w, tok, cot, w_qkv, w_proj, hat, normed, inv, q, k, v, dc)

    def attention(g, w):
        attend(g, w, lat_last, lon_last, mask, maskf, q, k, v, dc, qs, cs, pt, st, sf, df, ctx, dqkv)

    def swap_in(g):
        return core_swap(grad.at[g, 1 - core], swapped.at[g], swap_send.at[g, 0], swap_recv.at[g, 0])

    def swap_out(g):
        part = total.at[g, core]
        return core_swap(part, part, swap_send.at[g, 1], swap_recv.at[g, 1])

    def sum_first(g):
        swap_in(g).wait()
        mixed[g] = (grad[g, core].astype(F32) + swapped[g].astype(F32)).astype(BF)
        scatter_first(mixed.at[g], parts.at[g], send.at[g, 0], recv.at[g, 0])
        for b in range(2):
            at = first_at(b)
            parts[g, b, at] = mixed[g, b, pl.ds(at * 16, 16)]

    def sum_second(g):
        for b in range(2):
            drain(parts.at[g, b, pl.ds(0, 3)], recv.at[g, 0, b])
            mixed2[g, b] = jnp.sum(parts[g, b].astype(F32), axis=0).astype(BF)
        scatter_second(mixed2.at[g], parts2.at[g], send.at[g, 1], recv.at[g, 1])
        for b in range(2):
            at = second_at(b)
            parts2[g, b, at] = mixed2[g, b, at]

    def spread_second(g):
        for b in range(2):
            drain(parts2.at[g, b, pl.ds(0, 15)], recv.at[g, 1, b])
            final = jnp.sum(parts2[g, b].astype(F32), axis=0) * NORM
            total[g, core, b, first_at(b) * 16 + second_at(b)] = final.astype(BF)
        gather_second(total.at[g, core], send.at[g, 2], recv.at[g, 2])

    def spread_first(g):
        for b in range(2):
            drain(parts2.at[g, b, pl.ds(0, 15)], recv.at[g, 2, b])
        gather_first(total.at[g, core], send.at[g, 3], recv.at[g, 3])

    def spread_core(g):
        for b in range(2):
            drain(parts.at[g, b, pl.ds(0, 3)], recv.at[g, 3, b])
        swap_out(g).start()

    def drain_sends(g):
        for b in range(2):
            for i, ref in enumerate((parts, parts2, parts2, parts)):
                drain(ref.at[g, b, pl.ds(0, 15 if i in (1, 2) else 3)], send.at[g, i, b])

    def write_gradients(g):
        swap_out(g).wait()
        for b in range(2):
            for part in range(3):
                at = 512 * part + 256 * g + 128 * b
                rows = slice(32 * (part % 2), 32 * (part % 2) + 32)
                gqkv[:, at : at + 128] = total[g, part // 2, b, rows].reshape(512, 128)
            for half in range(2):
                at = 256 * half + 128 * b
                rows = slice(32 + 16 * half, 48 + 16 * half)
                gproj[256 * g : 256 * g + 256, at : at + 128] = total[g, 1, b, rows].reshape(256, 128)

    def back(p):
        in_back[p, 0:224] = out_back[p, 0:224]
        for copy in going[p]:
            copy.wait_recv()
        for half, out in enumerate((output, grad_tokens)):
            for level in range(2):
                at = 144 * ((2 * p + 1 + level) % 4)
                rows = slice(288 * half + 144 * level, 288 * half + 144 * level + 144)
                moved = dot(unpack[rows, :], in_back[p])
                out[at : at + 144, :] = (both[p, rows, :].astype(F32) + moved).astype(BF)

    def leave(p):
        @pl.loop(0, 2)
        def _(i):
            finish(p, i, w_qkv, w_proj, hat, inv, ctx, dqkv, done)

        out_back[p] = dot(unplace[...], done[p]).astype(BF)
        for copy in going[p]:
            copy.start()

    going = [halo(p, 1, out_back, in_back, bsend, brecv) for p in range(2)]
    arrive(0)

    @pl.loop(0, 4)
    def _(i):
        attention(i // 2, i % 2)

    leave(0)
    arrive(1)

    @pl.loop(0, 2)
    def _(g):
        @pl.loop(2, 4)
        def _(w):
            attention(g, w)

        @pl.when(g == 1)
        def _():
            sum_first(0)

        weight_gradients(g, normed, cot, ctx, dqkv, grad)
        swap_in(g).start()

    leave(1)
    sum_first(1)
    sum_second(0)
    back(0)
    sum_second(1)
    spread_second(0)
    spread_second(1)
    spread_first(0)
    back(1)
    spread_first(1)
    spread_core(0)
    drain_sends(0)
    for p in range(2):
        for copy in coming[p] + going[p]:
            copy.wait_send()
    write_gradients(0)
    spread_core(1)
    drain_sends(1)
    write_gradients(1)


def block(tokens, cotangent, w_qkv, w_proj):
    hbm = pl.BlockSpec(memory_space=pl.ANY)
    vm = pl.BlockSpec(memory_space=pltpu.VMEM)
    dma = pltpu.SemaphoreType.DMA
    return pl.pallas_call(
        kernel,
        out_shape=(
            jax.ShapeDtypeStruct((576, 512), BF),
            jax.ShapeDtypeStruct((576, 512), BF),
            jax.ShapeDtypeStruct((512, 1536), BF),
            jax.ShapeDtypeStruct((512, 512), BF),
        ),
        in_specs=[hbm] * 8,
        out_specs=(vm,) * 4,
        scratch_shapes=[
            pltpu.VMEM((2, 576, 512), BF),
            pltpu.VMEM((512, 1536), BF),
            pltpu.VMEM((512, 512), BF),
            pltpu.VMEM((ROWS, 576), BF),
            pltpu.VMEM((576, ROWS), BF),
            pltpu.VMEM((ROWS, 576), BF),
            pltpu.VMEM((576, ROWS), BF),
            pltpu.VMEM((2, ROWS, 512), BF),
            pltpu.VMEM((2, ROWS, 512), BF),
            pltpu.VMEM((2, ROWS, 512), BF),
            pltpu.VMEM((2, ROWS, 512), BF),
            pltpu.VMEM((576, 512), BF),
            pltpu.VMEM((576, 512), BF),
            pltpu.VMEM((4, 144, 512), F32),
            pltpu.VMEM((576, 512), BF),
            pltpu.VMEM((4, 144, 128), F32),
            pltpu.VMEM((2, 4, 144, 256), BF),
            pltpu.VMEM((2, 4, 144, 256), BF),
            pltpu.VMEM((2, 4, 144, 256), BF),
            pltpu.VMEM((2, 4, 144, 256), BF),
            pltpu.VMEM((1152, 256), BF),
            pltpu.VMEM((1152, 256), BF),
            pltpu.VMEM((144, 1152), BF),
            pltpu.VMEM((144, 1152), BF),
            pltpu.VMEM((144, 1152), F32),
            pltpu.VMEM((144, 1152), F32),
            pltpu.VMEM((2, 576, 256), BF),
            pltpu.VMEM((2, 576, 768), BF),
            pltpu.VMEM((2, 576, 512), BF),
            pltpu.VMEM((2, 2, 2, 64, 16, 128), BF),
            pltpu.VMEM((2, 2, 64, 16, 128), BF),
            pltpu.VMEM((2, 2, 64, 16, 128), BF),
            pltpu.VMEM((2, 2, 4, 16, 16, 128), BF),
            pltpu.VMEM((2, 2, 16, 16, 128), BF),
            pltpu.VMEM((2, 2, 16, 16, 128), BF),
            pltpu.VMEM((2, 2, 2, 64, 16, 128), BF),
            dma((16,)),
            dma((2, 2)),
            dma((2, 2)),
            dma((2, 4, 2)),
            dma((2, 4, 2)),
            dma((2, 3)),
            dma((2, 3)),
            dma((2, 3)),
            dma((2, 3)),
        ],
        compiler_params=pltpu.CompilerParams(
            vmem_limit_bytes=56 * 2**20, collective_id=0, has_side_effects=True
        ),
        name="window_block",
    )(tokens, cotangent, w_qkv, w_proj, *orders())


def body(tokens, cotangent, w_qkv, w_proj):
    shape = tokens.shape
    output, grad_tokens, gqkv, gproj = block(
        tokens.reshape(576, 512), cotangent.reshape(576, 512), w_qkv, w_proj
    )
    return (output.reshape(shape), grad_tokens.reshape(shape), gqkv.astype(F32), gproj.astype(F32))


def solution(mesh):
    spec = P(None, "lat", "lon", None)
    return jax.shard_map(
        body,
        mesh=mesh,
        in_specs=(spec, spec, P(), P()),
        out_specs=(spec, spec, P(), P()),
        check_vma=False,
    )
```

```python
import numpy as np
import jax
import jax.numpy as jnp
from jax import lax
from jax.experimental import pallas as pl
from jax.experimental.pallas import tpu as pltpu
from jax.sharding import PartitionSpec as P

BF = jnp.bfloat16
F32 = jnp.float32
SCALE = 1.0 / 32**0.5
EXP2 = SCALE * 1.4426950408889634
NORM = 1.0 / 73728**0.5
NN = (((1,), (0,)), ((), ()))
NT = (((1,), (1,)), ((), ()))
TN = (((0,), (0,)), ((), ()))
MESH = pl.DeviceIdType.MESH

STARTS = (0, 224, 448, 528)
ROWS = 608
SECTIONS = ((224, 224), (448, 80), (528, 80))


def section_row(array, level, row, col):
    section = (2 if col < 6 else 0) + (1 if row < 3 else 0)
    width, first = (18, 6) if col >= 6 else (6, 0)
    at = (level * 3 + row % 3) * width + col - first
    return STARTS[section] + array * 6 * width + at


def orders():
    pack = np.zeros((ROWS, 576), np.float32)
    place = np.zeros((576, ROWS), np.float32)
    for array in range(2):
        for level in range(2):
            for row in range(6):
                for col in range(24):
                    at = array * 288 + level * 144 + row * 24 + col
                    pack[section_row(array, level, row, col), at] = 1
            for row in range(6):
                for col in range(24):
                    at = array * 288 + col // 12 * 144 + level * 72 + row * 12 + col % 12
                    source = section_row(array, level, (row + 3) % 6, (col + 6) % 24)
                    place[at, source] = 1
    return [jnp.asarray(m, BF) for m in (pack, place, place.T, pack.T)]


def dot(a, b, dims=NN):
    return lax.dot_general(a, b, dims, preferred_element_type=F32)


def head_mask(dtype):
    head = lax.broadcasted_iota(jnp.int32, (128, 256), 0) >> 4
    col = lax.broadcasted_iota(jnp.int32, (128, 256), 1) >> 5
    return (head == col).astype(dtype)


def window_rows(w):
    return pl.ds(pl.multiple_of(w * 144, 16), 144)


def pair_rows(p):
    return slice(288 * p, 288 * p + 288)


def project(p, tok, cot, w_qkv, w_proj_t, hat, normed, inv, q, k, v, dc):
    rows = pair_rows(p)
    x = tok[rows, :].astype(F32)
    x = x - jnp.mean(x, axis=1, keepdims=True)
    scale = lax.rsqrt(jnp.mean(x * x, axis=1, keepdims=True) + 1e-05)
    x = x * scale
    hat[rows, :] = x
    inv[rows, :] = jnp.broadcast_to(scale, (288, 128))
    x = x.astype(BF)
    normed[rows, :] = x
    for g in range(2):
        for part, ref in enumerate((q, k, v)):
            at = 512 * part + 256 * g
            ref[g, rows, :] = dot(x, w_qkv[:, at : at + 256]).astype(BF)
        dc[g, rows, :] = dot(cot[rows, :], w_proj_t[:, 256 * g : 256 * g + 256]).astype(BF)


def key_rows(p, c):
    if p == 0 or c == 4:
        return slice(0, 144)
    return slice(0, 80) if c < 4 else slice(64, 144)


def spans(p):
    if p == 0:
        return [(slice(0, 144), slice(0, 1152))]
    return [(key_rows(p, c), slice(128 * c, 128 * d)) for c, d in ((0, 4), (4, 5), (5, 9))]


def attend(p, g, lat_last, lon_last, mask, maskf, q, k, v, dc, qs, cs, pt, st, sf, df, ctx, dqkv):
    def rows(i):
        return slice(144 * (2 * p + i), 144 * (2 * p + i) + 144)

    def scores(i):
        first = 144 * (2 * p + i)
        keys, vals = k[g, rows(i), :], v[g, rows(i), :]
        for c in range(9):
            at = slice(128 * c, 128 * c + 128)
            q16 = q[g, first + 16 * c : first + 16 * c + 16, :]
            d16 = dc[g, first + 16 * c : first + 16 * c + 16, :]
            qs[i, at, :] = jnp.concatenate([q16] * 8, axis=0) * mask
            cs[i, at, :] = jnp.concatenate([d16] * 8, axis=0) * mask
        for kr, at in spans(p):
            sf[i, kr, at] = dot(keys[kr], qs[i, at, :], NT)
            df[i, kr, at] = dot(vals[kr], cs[i, at, :], NT)

    def softmax(i):
        klab, qlab = labels(2 * p + i, lat_last, lon_last)
        for c in range(9):
            at = slice(128 * c, 128 * c + 128)
            kr = key_rows(p, c)
            s = jnp.where(klab[kr] == qlab[c], sf[i, kr, at], -1e30)
            e = jnp.exp2((s - jnp.max(s, axis=0, keepdims=True)) * EXP2)
            prob = e * (1.0 / jnp.sum(e, axis=0, keepdims=True))
            pt[2 * p + i, kr, at] = prob.astype(BF)
            dp = df[i, kr, at]
            inner = jnp.sum(prob * dp, axis=0, keepdims=True)
            st[2 * p + i, kr, at] = ((prob * SCALE) * (dp - inner)).astype(BF)

    def fold(m, i, ref):
        out = [dot(m[2 * p + i, kr, at], ref[g, rows(i), :][kr], TN) for kr, at in spans(p)]
        out = jnp.concatenate(out, axis=0) if len(out) > 1 else out[0]
        out = out.reshape(9, 8, 16, 256) * maskf.reshape(1, 8, 16, 256)
        return jnp.sum(out, axis=1).reshape(144, 256).astype(BF)

    def columns(part):
        return pl.ds(pl.multiple_of(768 * g + 256 * part, 256), 256)

    def results(i):
        ctx[rows(i), pl.ds(pl.multiple_of(256 * g, 256), 256)] = fold(pt, i, v)
        dqkv[rows(i), columns(0)] = fold(st, i, k)
        dqkv[rows(i), columns(1)] = dot(st[2 * p + i], qs[i]).astype(BF)
        dqkv[rows(i), columns(2)] = dot(pt[2 * p + i], cs[i]).astype(BF)

    scores(0)
    scores(1)
    softmax(0)
    results(0)
    softmax(1)
    results(1)


def finish(p, w_qkv_t, w_proj, hat, inv, ctx, dqkv, done):
    rows = pair_rows(p)
    done[p, 0:288, :] = dot(ctx[rows, :], w_proj[...]).astype(BF)
    d = dot(dqkv[rows, :], w_qkv_t[...])
    h = hat[rows, :]
    d = d - jnp.mean(d, axis=1, keepdims=True) - h * jnp.mean(d * h, axis=1, keepdims=True)
    scale = jnp.concatenate([inv[rows, :]] * 4, axis=1)
    done[p, 288:576, :] = (d * scale).astype(BF)


def labels(w, lat_last, lon_last):
    def flags(t):
        level = (t >= 72).astype(jnp.int32)
        t = t - 72 * level
        row = (t >= 36).astype(jnp.int32)
        t = t - 36 * row
        t = jnp.where(t >= 24, t - 24, jnp.where(t >= 12, t - 12, t))
        col = (t >= 6).astype(jnp.int32)
        return level * is_b + row * lat_last + col * last

    is_b = 4 * (w // 2)
    last = lon_last * (w % 2)
    klab = flags(lax.broadcasted_iota(jnp.int32, (144, 128), 0))
    lane = lax.broadcasted_iota(jnp.int32, (1, 128), 1) & 15
    qlab = [flags(lane + 16 * c) for c in range(9)]
    return klab, qlab


def weight_gradients(g, normed, cot, ctx, dqkv, grad):
    def keep(d, half, at, count):
        for b in range(2):
            piece = d[:, 128 * b : 128 * b + 128].astype(BF)
            grad[g, half, b, at : at + count] = piece.reshape(count, 16, 128)

    for part in range(3):
        at = 768 * g + 256 * part
        d = dot(normed[...], dqkv[:, at : at + 256], TN)
        keep(d, part // 2, 32 * (part % 2), 32)
    d = dot(ctx[:, 256 * g : 256 * g + 256], cot[...], TN)
    for half in range(2):
        keep(d[:, 256 * half : 256 * half + 256], 1, 32 + 16 * half, 16)


def place():
    lat, lon = lax.axis_index("lat"), lax.axis_index("lon")
    return (lon // 2) % 4, (lon // 8) * 2 + lat % 2, lat // 2, lon % 2


def device(x, y, z, core):
    return z * 2 + y % 2, ((y // 2) * 4 + x) * 2 + core


def first_at(b):
    x, y, z, core = place()
    return x if b == 0 else z


def first_device(b, to):
    x, y, z, core = place()
    return device(to, y, z, core) if b == 0 else device(x, y, to, core)


def second_at(b):
    x, y, z, core = place()
    return y * 4 + (z if b == 0 else x)


def second_device(b, to):
    x, y, z, core = place()
    return device(x, to // 4, to % 4, core) if b == 0 else device(to % 4, to // 4, z, core)


def beside(lat_step, lon_step):
    lat, lon = lax.axis_index("lat"), lax.axis_index("lon")
    return lax.rem(lat + lat_step + 8, 8), lax.rem(lon + lon_step + 16, 16)


def drain(ref, sem):
    pltpu.make_async_copy(ref, ref, sem).wait()


def greet():
    x, y, z, core = place()
    barrier = pltpu.get_barrier_semaphore()

    def signal(to):
        pl.semaphore_signal(barrier, inc=1, device_id=to, device_id_type=MESH)

    for steps in ((-1, 0), (0, -1), (-1, -1), (1, 0), (0, 1), (1, 1)):
        signal(beside(*steps))
    signal(device(x, y, z, 1 - core))
    for b in range(2):
        for k in range(1, 4):
            signal(first_device(b, first_at(b) ^ k))

        @pl.loop(1, 16)
        def _(t):
            signal(second_device(b, second_at(b) ^ t))


def meet():
    pl.semaphore_wait(pltpu.get_barrier_semaphore(), 43)


def halo(p, step, src, dst, send, recv):
    copies = []
    for s, (at, count) in enumerate(SECTIONS):
        lat_step, lon_step = ((step, 0), (0, step), (step, step))[s]
        copies.append(pltpu.make_async_remote_copy(
            src_ref=src.at[p, pl.ds(at, count)], dst_ref=dst.at[p, pl.ds(at, count)],
            send_sem=send.at[p, s], recv_sem=recv.at[p, s],
            device_id=beside(lat_step, lon_step), device_id_type=MESH,
        ))
    return copies


def core_swap(src, dst, send, recv):
    x, y, z, core = place()
    return pltpu.make_async_remote_copy(
        src_ref=src, dst_ref=dst, send_sem=send, recv_sem=recv,
        device_id=device(x, y, z, 1 - core), device_id_type=MESH,
    )


def scatter_first(mixed, parts, send, recv):
    for b in range(2):
        at = first_at(b)
        for k in (2, 1, 3):
            pltpu.make_async_remote_copy(
                src_ref=mixed.at[b, pl.ds((at ^ k) * 16, 16)], dst_ref=parts.at[b, at],
                send_sem=send.at[b], recv_sem=recv.at[b],
                device_id=first_device(b, at ^ k), device_id_type=MESH,
            ).start()


def scatter_second(mixed, parts, send, recv):
    for b in range(2):
        at = second_at(b)

        @pl.loop(0, 15)
        def _(t):
            to = at ^ (15 - t)
            pltpu.make_async_remote_copy(
                src_ref=mixed.at[b, to], dst_ref=parts.at[b, at],
                send_sem=send.at[b], recv_sem=recv.at[b],
                device_id=second_device(b, to), device_id_type=MESH,
            ).start()


def gather_second(total, send, recv):
    for b in range(2):
        at = second_at(b)
        piece = total.at[b, first_at(b) * 16 + at]

        @pl.loop(0, 15)
        def _(t):
            pltpu.make_async_remote_copy(
                src_ref=piece, dst_ref=piece, send_sem=send.at[b], recv_sem=recv.at[b],
                device_id=second_device(b, at ^ (15 - t)), device_id_type=MESH,
            ).start()


def gather_first(b, total, send, recv):
    at = first_at(b)
    piece = total.at[b, pl.ds(at * 16, 16)]
    for k in (2, 1, 3):
        pltpu.make_async_remote_copy(
            src_ref=piece, dst_ref=piece, send_sem=send.at[b, k], recv_sem=recv.at[b, k],
            device_id=first_device(b, at ^ k), device_id_type=MESH,
        ).start()


def kernel(
    tokens, cotangent, w_qkv_in, w_proj_in, pack_in, place_in, unplace_in, unpack_in,
    output, grad_tokens, gqkv_out, gproj_out,
    moved, gqkv, gproj, both, w_qkv, w_proj, w_qkv_t, w_proj_t, pack, place_m, unplace, unpack, out_halo, in_halo, out_back, in_back,
    tok, cot, hat, normed, inv, q, k, v, dc, qs, cs, pt, st, sf, df, ctx, dqkv, done,
    grad, swapped, mixed, parts, mixed2, parts2, total, load, store, swap_send, swap_recv, send, recv, core_send, core_recv, wide_send, wide_recv, hsend, hrecv, bsend, brecv,
):
    x, y, z, core = place()
    greet()
    loads = []

    def fetch(src, dst):
        copy = pltpu.make_async_copy(src, dst, load.at[len(loads)])
        copy.start()
        loads.append(copy)

    for p in range(2):
        for half, src in enumerate((tokens, cotangent)):
            for level in range(2):
                fetch(
                    src.at[pl.ds(144 * ((2 * p + 1 + level) % 4), 144)],
                    both.at[p, pl.ds(288 * half + 144 * level, 144)],
                )
    fetch(pack_in, pack)
    early = len(loads)
    fetch(place_in, place_m)
    fetch(w_qkv_in, w_qkv)
    fetch(w_proj_in, w_proj)
    fetch(unplace_in, unplace)
    fetch(unpack_in, unpack)
    for copy in loads[:early]:
        copy.wait()
    out_halo[0] = dot(pack[...], both[0]).astype(BF)
    meet()
    coming = [halo(p, -1, out_halo, in_halo, hsend, hrecv) for p in range(2)]
    for copy in coming[0]:
        copy.start()
    out_halo[1] = dot(pack[...], both[1]).astype(BF)
    for copy in coming[1]:
        copy.start()
    for copy in loads[early:]:
        copy.wait()
    for g in range(2):
        for part in range(3):
            at = 512 * part + 256 * g
            to = 768 * g + 256 * part
            w_qkv_t[to : to + 256, :] = w_qkv[:, at : at + 256].T
    w_proj_t[...] = w_proj[...].T
    for i in range(2):
        pt[2 + i] = jnp.zeros((144, 1152), BF)
        st[2 + i] = jnp.zeros((144, 1152), BF)
    lat_last = 2 * (lax.axis_index("lat") == 7).astype(jnp.int32)
    lon_last = (lax.axis_index("lon") == 15).astype(jnp.int32)
    mask = head_mask(BF)
    maskf = head_mask(F32)

    def arrive(p):
        in_halo[p, 0:224] = out_halo[p, 0:224]
        for copy in coming[p]:
            copy.wait_recv()
        tok[pair_rows(p), :] = dot(place_m[0:288, :], in_halo[p]).astype(BF)
        cot[pair_rows(p), :] = dot(place_m[288:576, :], in_halo[p]).astype(BF)
        project(p, tok, cot, w_qkv, w_proj_t, hat, normed, inv, q, k, v, dc)

    def attention(p, g):
        attend(p, g, lat_last, lon_last, mask, maskf, q, k, v, dc, qs, cs, pt, st, sf, df, ctx, dqkv)

    def swap_in(g):
        return core_swap(grad.at[g, 1 - core], swapped.at[g], swap_send.at[g], swap_recv.at[g])

    def sum_first(g):
        swap_in(g).wait()
        mixed[g] = (grad[g, core].astype(F32) + swapped[g].astype(F32)).astype(BF)
        scatter_first(mixed.at[g], parts.at[g], send.at[g], recv.at[g])
        for b in range(2):
            at = first_at(b)
            parts[g, b, at] = mixed[g, b, pl.ds(at * 16, 16)]

    def sum_second():
        for b in range(2):
            for g in range(2):
                drain(parts.at[g, b, pl.ds(0, 3)], recv.at[g, b])
                mixed2[b, :, g] = jnp.sum(parts[g, b].astype(F32), axis=0).astype(BF)
        scatter_second(mixed2, parts2, send.at[2], recv.at[2])
        for b in range(2):
            at = second_at(b)
            parts2[b, at] = mixed2[b, at]

    def spread_second():
        for b in range(2):
            drain(parts2.at[b, pl.ds(0, 15)], recv.at[2, b])
            final = jnp.sum(parts2[b].astype(F32), axis=0) * NORM
            total[core, b, first_at(b) * 16 + second_at(b)] = final.astype(BF)
        gather_second(total.at[core], send.at[3], recv.at[3])

    def core_out(b, i):
        part = total.at[core, b, pl.ds((first_at(b) ^ i) * 16, 16)]
        return core_swap(part, part, core_send.at[b, i], core_recv.at[b, i])

    def spread_first():
        for b in range(2):
            drain(parts2.at[b, pl.ds(0, 15)], recv.at[3, b])
            gather_first(b, total.at[core], wide_send, wide_recv)
        for b in range(2):
            core_out(b, 0).start()
        for i in (1, 3, 2):
            for b in range(2):
                drain(total.at[core, b, pl.ds(0, 16)], wide_recv.at[b, i])
                core_out(b, i).start()

    def write_half(half):
        for g in range(2):
            for b in range(2):
                if half == 0:
                    for part in range(2):
                        at = 512 * part + 256 * g + 128 * b
                        rows = slice(32 * part, 32 * part + 32)
                        gqkv[:, at : at + 128] = total[0, b, rows, g].reshape(512, 128).astype(F32)
                    continue
                at = 1024 + 256 * g + 128 * b
                gqkv[:, at : at + 128] = total[1, b, 0:32, g].reshape(512, 128).astype(F32)
                for side in range(2):
                    at = 256 * side + 128 * b
                    piece = total[1, b, 32 + 16 * side : 48 + 16 * side, g].reshape(256, 128)
                    gproj[256 * g : 256 * g + 256, at : at + 128] = piece.astype(F32)
        for copy in write_copies(half):
            copy.start()

    def write_copies(half):
        if half == 0:
            at = pl.ds(0, 1024)
            return [pltpu.make_async_copy(gqkv.at[:, at], gqkv_out.at[:, at], store.at[2])]
        at = pl.ds(1024, 512)
        return [
            pltpu.make_async_copy(gqkv.at[:, at], gqkv_out.at[:, at], store.at[3]),
            pltpu.make_async_copy(gproj, gproj_out, store.at[4]),
        ]

    def write_own():
        for half in range(2):
            @pl.when(core == half)
            def _():
                write_half(half)

    def write_other():
        for b in range(2):
            for i in range(4):
                core_out(b, i).wait()
        for half in range(2):
            @pl.when(core != half)
            def _():
                write_half(half)

    def drain_sends():
        for b in range(2):
            for g in range(2):
                drain(parts.at[g, b, pl.ds(0, 3)], send.at[g, b])
                drain(parts2.at[b, pl.ds(0, 15)], send.at[2 + g, b])
            for i in range(1, 4):
                drain(total.at[core, b, pl.ds(0, 16)], wide_send.at[b, i])

    def back(p):
        in_back[p, 0:224] = out_back[p, 0:224]
        for copy in going[p]:
            copy.wait_recv()
        for half in range(2):
            for level in range(2):
                at = 144 * ((2 * p + 1 + level) % 4)
                rows = slice(288 * half + 144 * level, 288 * half + 144 * level + 144)
                d = dot(unpack[rows, :], in_back[p]).astype(BF)
                moved[half, at : at + 144, :] = (both[p, rows, :].astype(F32) + d.astype(F32)).astype(BF)

    going = [halo(p, 1, out_back, in_back, bsend, brecv) for p in range(2)]

    def leave(p):
        finish(p, w_qkv_t, w_proj, hat, inv, ctx, dqkv, done)
        out_back[p] = dot(unplace[...], done[p]).astype(BF)
        for copy in going[p]:
            copy.start()

    arrive(0)

    @pl.loop(0, 2)
    def _(g):
        attention(0, g)

    leave(0)
    arrive(1)
    attention(1, 0)
    weight_gradients(0, normed, cot, ctx, dqkv, grad)
    swap_in(0).start()
    attention(1, 1)
    sum_first(0)
    weight_gradients(1, normed, cot, ctx, dqkv, grad)
    swap_in(1).start()
    leave(1)
    sum_first(1)
    sum_second()
    back(0)
    spread_second()
    back(1)
    outs = [pltpu.make_async_copy(moved.at[i], (output, grad_tokens)[i], store.at[i]) for i in range(2)]
    for copy in outs:
        copy.start()
    spread_first()
    write_own()
    drain_sends()
    for p in range(2):
        for copy in coming[p] + going[p]:
            copy.wait_send()
    write_other()
    for copy in outs + write_copies(0) + write_copies(1):
        copy.wait()


def block(tokens, cotangent, w_qkv, w_proj):
    hbm = pl.BlockSpec(memory_space=pl.ANY)
    dma = pltpu.SemaphoreType.DMA
    return pl.pallas_call(
        kernel,
        out_shape=(
            jax.ShapeDtypeStruct((576, 512), BF),
            jax.ShapeDtypeStruct((576, 512), BF),
            jax.ShapeDtypeStruct((512, 1536), F32),
            jax.ShapeDtypeStruct((512, 512), F32),
        ),
        in_specs=[hbm] * 8,
        out_specs=(hbm,) * 4,
        scratch_shapes=[
            pltpu.VMEM((2, 576, 512), BF),
            pltpu.VMEM((512, 1536), F32),
            pltpu.VMEM((512, 512), F32),
            pltpu.VMEM((2, 576, 512), BF),
            pltpu.VMEM((512, 1536), BF),
            pltpu.VMEM((512, 512), BF),
            pltpu.VMEM((1536, 512), BF),
            pltpu.VMEM((512, 512), BF),
            pltpu.VMEM((ROWS, 576), BF),
            pltpu.VMEM((576, ROWS), BF),
            pltpu.VMEM((ROWS, 576), BF),
            pltpu.VMEM((576, ROWS), BF),
            pltpu.VMEM((2, ROWS, 512), BF),
            pltpu.VMEM((2, ROWS, 512), BF),
            pltpu.VMEM((2, ROWS, 512), BF),
            pltpu.VMEM((2, ROWS, 512), BF),
            pltpu.VMEM((576, 512), BF),
            pltpu.VMEM((576, 512), BF),
            pltpu.VMEM((576, 512), F32),
            pltpu.VMEM((576, 512), BF),
            pltpu.VMEM((576, 128), F32),
            pltpu.VMEM((2, 576, 256), BF),
            pltpu.VMEM((2, 576, 256), BF),
            pltpu.VMEM((2, 576, 256), BF),
            pltpu.VMEM((2, 576, 256), BF),
            pltpu.VMEM((2, 1152, 256), BF),
            pltpu.VMEM((2, 1152, 256), BF),
            pltpu.VMEM((4, 144, 1152), BF),
            pltpu.VMEM((4, 144, 1152), BF),
            pltpu.VMEM((2, 144, 1152), F32),
            pltpu.VMEM((2, 144, 1152), F32),
            pltpu.VMEM((576, 512), BF),
            pltpu.VMEM((576, 1536), BF),
            pltpu.VMEM((2, 576, 512), BF),
            pltpu.VMEM((2, 2, 2, 64, 16, 128), BF),
            pltpu.VMEM((2, 2, 64, 16, 128), BF),
            pltpu.VMEM((2, 2, 64, 16, 128), BF),
            pltpu.VMEM((2, 2, 4, 16, 16, 128), BF),
            pltpu.VMEM((2, 16, 2, 16, 128), BF),
            pltpu.VMEM((2, 16, 2, 16, 128), BF),
            pltpu.VMEM((2, 2, 64, 2, 16, 128), BF),
            dma((16,)),
            dma((5,)),
            dma((2,)),
            dma((2,)),
            dma((4, 2)),
            dma((4, 2)),
            dma((2, 4)),
            dma((2, 4)),
            dma((2, 4)),
            dma((2, 4)),
            dma((2, 3)),
            dma((2, 3)),
            dma((2, 3)),
            dma((2, 3)),
        ],
        compiler_params=pltpu.CompilerParams(
            vmem_limit_bytes=56 * 2**20, collective_id=0, has_side_effects=True
        ),
        name="window_block",
    )(tokens, cotangent, w_qkv, w_proj, *orders())


def body(tokens, cotangent, w_qkv, w_proj):
    shape = tokens.shape
    output, grad_tokens, gqkv, gproj = block(
        tokens.reshape(576, 512), cotangent.reshape(576, 512), w_qkv, w_proj
    )
    return (output.reshape(shape), grad_tokens.reshape(shape), gqkv, gproj)


def solution(mesh):
    spec = P(None, "lat", "lon", None)
    return jax.shard_map(
        body,
        mesh=mesh,
        in_specs=(spec, spec, P(), P()),
        out_specs=(spec, spec, P(), P()),
        check_vma=False,
    )
```

```python
import numpy as np
import jax
import jax.numpy as jnp
from jax import lax
from jax.experimental import pallas as pl
from jax.experimental.pallas import tpu as pltpu
from jax.sharding import PartitionSpec as P

BF = jnp.bfloat16
F32 = jnp.float32
SCALE = 1.0 / 32**0.5
EXP2 = SCALE * 1.4426950408889634
NORM = 1.0 / 73728**0.5
NN = (((1,), (0,)), ((), ()))
NT = (((1,), (1,)), ((), ()))
TN = (((0,), (0,)), ((), ()))
MESH = pl.DeviceIdType.MESH

STARTS = (0, 224, 448, 528)
ROWS = 608
SECTIONS = ((224, 224), (448, 80), (528, 80))


def section_row(array, level, row, col):
    section = (2 if col < 6 else 0) + (1 if row < 3 else 0)
    width, first = (18, 6) if col >= 6 else (6, 0)
    at = (level * 3 + row % 3) * width + col - first
    return STARTS[section] + array * 6 * width + at


def orders():
    pack = np.zeros((ROWS, 576), np.float32)
    place = np.zeros((576, ROWS), np.float32)
    for array in range(2):
        for level in range(2):
            for row in range(6):
                for col in range(24):
                    at = array * 288 + level * 144 + row * 24 + col
                    pack[section_row(array, level, row, col), at] = 1
            for row in range(6):
                for col in range(24):
                    at = array * 288 + col // 12 * 144 + level * 72 + row * 12 + col % 12
                    source = section_row(array, level, (row + 3) % 6, (col + 6) % 24)
                    place[at, source] = 1
    return [jnp.asarray(m, BF) for m in (pack, place, place.T, pack.T)]


def dot(a, b, dims=NN):
    return lax.dot_general(a, b, dims, preferred_element_type=F32)


def head_mask(dtype):
    head = lax.broadcasted_iota(jnp.int32, (128, 256), 0) >> 4
    col = lax.broadcasted_iota(jnp.int32, (128, 256), 1) >> 5
    return (head == col).astype(dtype)


def window_rows(w):
    return pl.ds(pl.multiple_of(w * 144, 16), 144)


def pair_rows(p):
    return slice(288 * p, 288 * p + 288)


def project(p, tok, cot, w_qkv, w_proj_t, hat, normed, inv, q, k, v, dc):
    rows = pair_rows(p)
    x = tok[rows, :].astype(F32)
    x = x - jnp.mean(x, axis=1, keepdims=True)
    scale = lax.rsqrt(jnp.mean(x * x, axis=1, keepdims=True) + 1e-05)
    x = x * scale
    hat[rows, :] = x
    inv[rows, :] = jnp.broadcast_to(scale, (288, 128))
    x = x.astype(BF)
    normed[rows, :] = x
    for g in range(2):
        for part, ref in enumerate((q, k, v)):
            at = 512 * part + 256 * g
            ref[g, rows, :] = dot(x, w_qkv[:, at : at + 256]).astype(BF)
        dc[g, rows, :] = dot(cot[rows, :], w_proj_t[:, 256 * g : 256 * g + 256]).astype(BF)


def key_rows(p, c):
    if p == 0 or c == 4:
        return slice(0, 144)
    return slice(0, 80) if c < 4 else slice(64, 144)


def spans(p):
    if p == 0:
        return [(slice(0, 144), slice(0, 1152))]
    return [(key_rows(p, c), slice(128 * c, 128 * d)) for c, d in ((0, 4), (4, 5), (5, 9))]


def attend(p, g, lat_last, lon_last, mask, maskf, q, k, v, dc, qs, cs, pt, st, sf, df, ctx, dqkv):
    def rows(i):
        return slice(144 * (2 * p + i), 144 * (2 * p + i) + 144)

    def scores(i):
        first = 144 * (2 * p + i)
        keys, vals = k[g, rows(i), :], v[g, rows(i), :]
        for c in range(9):
            at = slice(128 * c, 128 * c + 128)
            q16 = q[g, first + 16 * c : first + 16 * c + 16, :]
            d16 = dc[g, first + 16 * c : first + 16 * c + 16, :]
            qs[i, at, :] = jnp.concatenate([q16] * 8, axis=0) * mask
            cs[i, at, :] = jnp.concatenate([d16] * 8, axis=0) * mask
        for kr, at in spans(p):
            sf[i, kr, at] = dot(keys[kr], qs[i, at, :], NT)
            df[i, kr, at] = dot(vals[kr], cs[i, at, :], NT)

    def softmax(i):
        klab, qlab = labels(2 * p + i, lat_last, lon_last)
        for c in range(9):
            at = slice(128 * c, 128 * c + 128)
            kr = key_rows(p, c)
            s = jnp.where(klab[kr] == qlab[c], sf[i, kr, at], -1e30)
            e = jnp.exp2((s - jnp.max(s, axis=0, keepdims=True)) * EXP2)
            prob = e * (1.0 / jnp.sum(e, axis=0, keepdims=True))
            pt[2 * p + i, kr, at] = prob.astype(BF)
            dp = df[i, kr, at]
            inner = jnp.sum(prob * dp, axis=0, keepdims=True)
            st[2 * p + i, kr, at] = ((prob * SCALE) * (dp - inner)).astype(BF)

    def fold(m, i, ref):
        out = [dot(m[2 * p + i, kr, at], ref[g, rows(i), :][kr], TN) for kr, at in spans(p)]
        out = jnp.concatenate(out, axis=0) if len(out) > 1 else out[0]
        out = out.reshape(9, 8, 16, 256) * maskf.reshape(1, 8, 16, 256)
        return jnp.sum(out, axis=1).reshape(144, 256).astype(BF)

    def columns(part):
        return pl.ds(pl.multiple_of(768 * g + 256 * part, 256), 256)

    def results(i):
        ctx[rows(i), pl.ds(pl.multiple_of(256 * g, 256), 256)] = fold(pt, i, v)
        dqkv[rows(i), columns(0)] = fold(st, i, k)
        dqkv[rows(i), columns(1)] = dot(st[2 * p + i], qs[i]).astype(BF)
        dqkv[rows(i), columns(2)] = dot(pt[2 * p + i], cs[i]).astype(BF)

    scores(0)
    scores(1)
    softmax(0)
    results(0)
    softmax(1)
    results(1)


def finish(p, w_qkv_t, w_proj, hat, inv, ctx, dqkv, done):
    rows = pair_rows(p)
    done[p, 0:288, :] = dot(ctx[rows, :], w_proj[...]).astype(BF)
    d = dot(dqkv[rows, :], w_qkv_t[...])
    h = hat[rows, :]
    d = d - jnp.mean(d, axis=1, keepdims=True) - h * jnp.mean(d * h, axis=1, keepdims=True)
    scale = jnp.concatenate([inv[rows, :]] * 4, axis=1)
    done[p, 288:576, :] = (d * scale).astype(BF)


def labels(w, lat_last, lon_last):
    def flags(t):
        level = (t >= 72).astype(jnp.int32)
        t = t - 72 * level
        row = (t >= 36).astype(jnp.int32)
        t = t - 36 * row
        t = jnp.where(t >= 24, t - 24, jnp.where(t >= 12, t - 12, t))
        col = (t >= 6).astype(jnp.int32)
        return level * is_b + row * lat_last + col * last

    is_b = 4 * (w // 2)
    last = lon_last * (w % 2)
    klab = flags(lax.broadcasted_iota(jnp.int32, (144, 128), 0))
    lane = lax.broadcasted_iota(jnp.int32, (1, 128), 1) & 15
    qlab = [flags(lane + 16 * c) for c in range(9)]
    return klab, qlab


def weight_gradients(g, normed, cot, ctx, dqkv, grad):
    def keep(d, half, at, count):
        for b in range(2):
            piece = d[:, 128 * b : 128 * b + 128].astype(BF)
            grad[g, half, b, at : at + count] = piece.reshape(count, 16, 128)

    for part in range(3):
        at = 768 * g + 256 * part
        d = dot(normed[...], dqkv[:, at : at + 256], TN)
        keep(d, part // 2, 32 * (part % 2), 32)
    d = dot(ctx[:, 256 * g : 256 * g + 256], cot[...], TN)
    for half in range(2):
        keep(d[:, 256 * half : 256 * half + 256], 1, 32 + 16 * half, 16)


def place():
    lat, lon = lax.axis_index("lat"), lax.axis_index("lon")
    return (lon // 2) % 4, (lon // 8) * 2 + lat % 2, lat // 2, lon % 2


def device(x, y, z, core):
    return z * 2 + y % 2, ((y // 2) * 4 + x) * 2 + core


def first_at(b):
    x, y, z, core = place()
    return x if b == 0 else z


def first_device(b, to):
    x, y, z, core = place()
    return device(to, y, z, core) if b == 0 else device(x, y, to, core)


def second_at(b):
    x, y, z, core = place()
    return y * 4 + (z if b == 0 else x)


def second_device(b, to):
    x, y, z, core = place()
    return device(x, to // 4, to % 4, core) if b == 0 else device(to % 4, to // 4, z, core)


def beside(lat_step, lon_step):
    lat, lon = lax.axis_index("lat"), lax.axis_index("lon")
    return lax.rem(lat + lat_step + 8, 8), lax.rem(lon + lon_step + 16, 16)


def drain(ref, sem):
    pltpu.make_async_copy(ref, ref, sem).wait()


def greet():
    x, y, z, core = place()
    barrier = pltpu.get_barrier_semaphore()

    def signal(to):
        pl.semaphore_signal(barrier, inc=1, device_id=to, device_id_type=MESH)

    for steps in ((-1, 0), (0, -1), (-1, -1), (1, 0), (0, 1), (1, 1)):
        signal(beside(*steps))
    signal(device(x, y, z, 1 - core))
    for b in range(2):
        for k in range(1, 4):
            signal(first_device(b, first_at(b) ^ k))

        @pl.loop(1, 16)
        def _(t):
            signal(second_device(b, second_at(b) ^ t))


def meet():
    pl.semaphore_wait(pltpu.get_barrier_semaphore(), 43)


def halo(p, step, src, dst, send, recv):
    copies = []
    for s, (at, count) in enumerate(SECTIONS):
        lat_step, lon_step = ((step, 0), (0, step), (step, step))[s]
        copies.append(pltpu.make_async_remote_copy(
            src_ref=src.at[p, pl.ds(at, count)], dst_ref=dst.at[p, pl.ds(at, count)],
            send_sem=send.at[p, s], recv_sem=recv.at[p, s],
            device_id=beside(lat_step, lon_step), device_id_type=MESH,
        ))
    return copies


def core_swap(src, dst, send, recv):
    x, y, z, core = place()
    return pltpu.make_async_remote_copy(
        src_ref=src, dst_ref=dst, send_sem=send, recv_sem=recv,
        device_id=device(x, y, z, 1 - core), device_id_type=MESH,
    )


def scatter_first(mixed, parts, send, recv):
    for b in range(2):
        at = first_at(b)
        for k in (2, 1, 3):
            pltpu.make_async_remote_copy(
                src_ref=mixed.at[b, pl.ds((at ^ k) * 16, 16)], dst_ref=parts.at[b, at],
                send_sem=send.at[b], recv_sem=recv.at[b],
                device_id=first_device(b, at ^ k), device_id_type=MESH,
            ).start()


def scatter_second(mixed, parts, send, recv):
    for b in range(2):
        at = second_at(b)

        @pl.loop(0, 15)
        def _(t):
            to = at ^ (15 - t)
            pltpu.make_async_remote_copy(
                src_ref=mixed.at[b, to], dst_ref=parts.at[b, at],
                send_sem=send.at[b], recv_sem=recv.at[b],
                device_id=second_device(b, to), device_id_type=MESH,
            ).start()


def gather_second(total, send, recv):
    for b in range(2):
        at = second_at(b)
        piece = total.at[b, first_at(b) * 16 + at]

        @pl.loop(0, 15)
        def _(t):
            pltpu.make_async_remote_copy(
                src_ref=piece, dst_ref=piece, send_sem=send.at[b], recv_sem=recv.at[b],
                device_id=second_device(b, at ^ (15 - t)), device_id_type=MESH,
            ).start()


def gather_first(b, total, send, recv):
    at = first_at(b)
    piece = total.at[b, pl.ds(at * 16, 16)]
    for k in (2, 1, 3):
        pltpu.make_async_remote_copy(
            src_ref=piece, dst_ref=piece, send_sem=send.at[b, k], recv_sem=recv.at[b, k],
            device_id=first_device(b, at ^ k), device_id_type=MESH,
        ).start()


def kernel(
    tokens, cotangent, w_qkv_in, w_proj_in, pack_in, place_in, unplace_in, unpack_in,
    output, grad_tokens, gqkv, gproj,
    both, w_qkv, w_proj, w_qkv_t, w_proj_t, pack, place_m, unplace, unpack, out_halo, in_halo, out_back, in_back,
    tok, cot, hat, normed, inv, q, k, v, dc, qs, cs, pt, st, sf, df, ctx, dqkv, done,
    grad, swapped, mixed, parts, mixed2, parts2, total, load, swap_send, swap_recv, send, recv, core_send, core_recv, wide_send, wide_recv, hsend, hrecv, bsend, brecv,
):
    x, y, z, core = place()
    greet()
    loads = []

    def fetch(src, dst):
        copy = pltpu.make_async_copy(src, dst, load.at[len(loads)])
        copy.start()
        loads.append(copy)

    for p in range(2):
        for half, src in enumerate((tokens, cotangent)):
            for level in range(2):
                fetch(
                    src.at[pl.ds(144 * ((2 * p + 1 + level) % 4), 144)],
                    both.at[p, pl.ds(288 * half + 144 * level, 144)],
                )
    fetch(pack_in, pack)
    early = len(loads)
    fetch(place_in, place_m)
    fetch(w_qkv_in, w_qkv)
    fetch(w_proj_in, w_proj)
    fetch(unplace_in, unplace)
    fetch(unpack_in, unpack)
    for copy in loads[:early]:
        copy.wait()
    out_halo[0] = dot(pack[...], both[0]).astype(BF)
    meet()
    coming = [halo(p, -1, out_halo, in_halo, hsend, hrecv) for p in range(2)]
    for copy in coming[0]:
        copy.start()
    out_halo[1] = dot(pack[...], both[1]).astype(BF)
    for copy in coming[1]:
        copy.start()
    for copy in loads[early:]:
        copy.wait()
    for g in range(2):
        for part in range(3):
            at = 512 * part + 256 * g
            to = 768 * g + 256 * part
            w_qkv_t[to : to + 256, :] = w_qkv[:, at : at + 256].T
    w_proj_t[...] = w_proj[...].T
    for i in range(2):
        pt[2 + i] = jnp.zeros((144, 1152), BF)
        st[2 + i] = jnp.zeros((144, 1152), BF)
    lat_last = 2 * (lax.axis_index("lat") == 7).astype(jnp.int32)
    lon_last = (lax.axis_index("lon") == 15).astype(jnp.int32)
    mask = head_mask(BF)
    maskf = head_mask(F32)

    def arrive(p):
        in_halo[p, 0:224] = out_halo[p, 0:224]
        for copy in coming[p]:
            copy.wait_recv()
        tok[pair_rows(p), :] = dot(place_m[0:288, :], in_halo[p]).astype(BF)
        cot[pair_rows(p), :] = dot(place_m[288:576, :], in_halo[p]).astype(BF)
        project(p, tok, cot, w_qkv, w_proj_t, hat, normed, inv, q, k, v, dc)

    def attention(p, g):
        attend(p, g, lat_last, lon_last, mask, maskf, q, k, v, dc, qs, cs, pt, st, sf, df, ctx, dqkv)

    def swap_in(g):
        return core_swap(grad.at[g, 1 - core], swapped.at[g], swap_send.at[g], swap_recv.at[g])

    def sum_first(g):
        swap_in(g).wait()
        mixed[g] = (grad[g, core].astype(F32) + swapped[g].astype(F32)).astype(BF)
        scatter_first(mixed.at[g], parts.at[g], send.at[g], recv.at[g])
        for b in range(2):
            at = first_at(b)
            parts[g, b, at] = mixed[g, b, pl.ds(at * 16, 16)]

    def sum_second():
        for b in range(2):
            for g in range(2):
                drain(parts.at[g, b, pl.ds(0, 3)], recv.at[g, b])
                mixed2[b, :, g] = jnp.sum(parts[g, b].astype(F32), axis=0).astype(BF)
        scatter_second(mixed2, parts2, send.at[2], recv.at[2])
        for b in range(2):
            at = second_at(b)
            parts2[b, at] = mixed2[b, at]

    def spread_second():
        for b in range(2):
            drain(parts2.at[b, pl.ds(0, 15)], recv.at[2, b])
            final = jnp.sum(parts2[b].astype(F32), axis=0) * NORM
            total[core, b, first_at(b) * 16 + second_at(b)] = final.astype(BF)
        gather_second(total.at[core], send.at[3], recv.at[3])

    def core_out(b, i):
        part = total.at[core, b, pl.ds((first_at(b) ^ i) * 16, 16)]
        return core_swap(part, part, core_send.at[b, i], core_recv.at[b, i])

    def spread_first():
        for b in range(2):
            drain(parts2.at[b, pl.ds(0, 15)], recv.at[3, b])
            gather_first(b, total.at[core], wide_send, wide_recv)
        send_back(1)
        for b in range(2):
            core_out(b, 0).start()
        for i in (1, 3, 2):
            for b in range(2):
                drain(total.at[core, b, pl.ds(0, 16)], wide_recv.at[b, i])
                core_out(b, i).start()

    def write_half(half):
        for g in range(2):
            for b in range(2):
                if half == 0:
                    for part in range(2):
                        at = 512 * part + 256 * g + 128 * b
                        rows = slice(32 * part, 32 * part + 32)
                        gqkv[:, at : at + 128] = total[0, b, rows, g].reshape(512, 128).astype(F32)
                    continue
                at = 1024 + 256 * g + 128 * b
                gqkv[:, at : at + 128] = total[1, b, 0:32, g].reshape(512, 128).astype(F32)
                for side in range(2):
                    at = 256 * side + 128 * b
                    piece = total[1, b, 32 + 16 * side : 48 + 16 * side, g].reshape(256, 128)
                    gproj[256 * g : 256 * g + 256, at : at + 128] = piece.astype(F32)

    def write_own():
        for half in range(2):
            @pl.when(core == half)
            def _():
                write_half(half)

    def write_other():
        for b in range(2):
            for i in range(4):
                core_out(b, i).wait()
        for half in range(2):
            @pl.when(core != half)
            def _():
                write_half(half)

    def drain_sends():
        for b in range(2):
            for g in range(2):
                drain(parts.at[g, b, pl.ds(0, 3)], send.at[g, b])
                drain(parts2.at[b, pl.ds(0, 15)], send.at[2 + g, b])
            for i in range(1, 4):
                drain(total.at[core, b, pl.ds(0, 16)], wide_send.at[b, i])

    def back(p):
        in_back[p, 0:224] = out_back[p, 0:224]
        for copy in going[p]:
            copy.wait_recv()
        for half, out in enumerate((output, grad_tokens)):
            for level in range(2):
                at = 144 * ((2 * p + 1 + level) % 4)
                rows = slice(288 * half + 144 * level, 288 * half + 144 * level + 144)
                d = dot(unpack[rows, :], in_back[p]).astype(BF)
                out[at : at + 144, :] = (both[p, rows, :].astype(F32) + d.astype(F32)).astype(BF)

    going = [halo(p, 1, out_back, in_back, bsend, brecv) for p in range(2)]

    def leave(p):
        finish(p, w_qkv_t, w_proj, hat, inv, ctx, dqkv, done)
        out_back[p] = dot(unplace[...], done[p]).astype(BF)

    def send_back(p):
        for copy in going[p]:
            copy.start()

    arrive(0)

    @pl.loop(0, 2)
    def _(g):
        attention(0, g)

    leave(0)
    send_back(0)
    arrive(1)
    attention(1, 0)
    weight_gradients(0, normed, cot, ctx, dqkv, grad)
    swap_in(0).start()
    attention(1, 1)
    sum_first(0)
    weight_gradients(1, normed, cot, ctx, dqkv, grad)
    swap_in(1).start()
    finish(1, w_qkv_t, w_proj, hat, inv, ctx, dqkv, done)
    sum_first(1)
    out_back[1] = dot(unplace[...], done[1]).astype(BF)
    back(0)
    sum_second()
    spread_second()
    spread_first()
    write_own()
    back(1)
    drain_sends()
    for p in range(2):
        for copy in coming[p] + going[p]:
            copy.wait_send()
    write_other()


def block(tokens, cotangent, w_qkv, w_proj):
    hbm = pl.BlockSpec(memory_space=pl.ANY)
    dma = pltpu.SemaphoreType.DMA
    return pl.pallas_call(
        kernel,
        out_shape=(
            jax.ShapeDtypeStruct((576, 512), BF),
            jax.ShapeDtypeStruct((576, 512), BF),
            jax.ShapeDtypeStruct((512, 1536), F32),
            jax.ShapeDtypeStruct((512, 512), F32),
        ),
        in_specs=[hbm] * 8,
        out_specs=(pl.BlockSpec(memory_space=pltpu.VMEM),) * 4,
        scratch_shapes=[
            pltpu.VMEM((2, 576, 512), BF),
            pltpu.VMEM((512, 1536), BF),
            pltpu.VMEM((512, 512), BF),
            pltpu.VMEM((1536, 512), BF),
            pltpu.VMEM((512, 512), BF),
            pltpu.VMEM((ROWS, 576), BF),
            pltpu.VMEM((576, ROWS), BF),
            pltpu.VMEM((ROWS, 576), BF),
            pltpu.VMEM((576, ROWS), BF),
            pltpu.VMEM((2, ROWS, 512), BF),
            pltpu.VMEM((2, ROWS, 512), BF),
            pltpu.VMEM((2, ROWS, 512), BF),
            pltpu.VMEM((2, ROWS, 512), BF),
            pltpu.VMEM((576, 512), BF),
            pltpu.VMEM((576, 512), BF),
            pltpu.VMEM((576, 512), F32),
            pltpu.VMEM((576, 512), BF),
            pltpu.VMEM((576, 128), F32),
            pltpu.VMEM((2, 576, 256), BF),
            pltpu.VMEM((2, 576, 256), BF),
            pltpu.VMEM((2, 576, 256), BF),
            pltpu.VMEM((2, 576, 256), BF),
            pltpu.VMEM((2, 1152, 256), BF),
            pltpu.VMEM((2, 1152, 256), BF),
            pltpu.VMEM((4, 144, 1152), BF),
            pltpu.VMEM((4, 144, 1152), BF),
            pltpu.VMEM((2, 144, 1152), F32),
            pltpu.VMEM((2, 144, 1152), F32),
            pltpu.VMEM((576, 512), BF),
            pltpu.VMEM((576, 1536), BF),
            pltpu.VMEM((2, 576, 512), BF),
            pltpu.VMEM((2, 2, 2, 64, 16, 128), BF),
            pltpu.VMEM((2, 2, 64, 16, 128), BF),
            pltpu.VMEM((2, 2, 64, 16, 128), BF),
            pltpu.VMEM((2, 2, 4, 16, 16, 128), BF),
            pltpu.VMEM((2, 16, 2, 16, 128), BF),
            pltpu.VMEM((2, 16, 2, 16, 128), BF),
            pltpu.VMEM((2, 2, 64, 2, 16, 128), BF),
            dma((16,)),
            dma((2,)),
            dma((2,)),
            dma((4, 2)),
            dma((4, 2)),
            dma((2, 4)),
            dma((2, 4)),
            dma((2, 4)),
            dma((2, 4)),
            dma((2, 3)),
            dma((2, 3)),
            dma((2, 3)),
            dma((2, 3)),
        ],
        compiler_params=pltpu.CompilerParams(
            vmem_limit_bytes=50 * 2**20, collective_id=0, has_side_effects=True
        ),
        name="window_block",
    )(tokens, cotangent, w_qkv, w_proj, *orders())


def hand_over(*refs):
    copies = [pltpu.make_async_copy(refs[i], refs[4 + i], refs[8].at[i]) for i in range(4)]
    for copy in copies:
        copy.start()
    for copy in copies:
        copy.wait()


def body(tokens, cotangent, w_qkv, w_proj):
    shape = tokens.shape
    results = block(tokens.reshape(576, 512), cotangent.reshape(576, 512), w_qkv, w_proj)
    hbm = pl.BlockSpec(memory_space=pl.ANY)
    output, grad_tokens, gqkv, gproj = pl.pallas_call(
        hand_over,
        out_shape=tuple(jax.ShapeDtypeStruct(r.shape, r.dtype) for r in results),
        in_specs=[hbm] * 4,
        out_specs=(hbm,) * 4,
        scratch_shapes=[pltpu.SemaphoreType.DMA((4,))],
        name="hand_over",
    )(*results)
    return (output.reshape(shape), grad_tokens.reshape(shape), gqkv, gproj)


def solution(mesh):
    spec = P(None, "lat", "lon", None)
    return jax.shard_map(
        body,
        mesh=mesh,
        in_specs=(spec, spec, P(), P()),
        out_specs=(spec, spec, P(), P()),
        check_vma=False,
    )
```

```python
import numpy as np
import jax
import jax.numpy as jnp
from jax import lax
from jax.experimental import pallas as pl
from jax.experimental.pallas import tpu as pltpu
from jax.sharding import PartitionSpec as P

BF = jnp.bfloat16
F32 = jnp.float32
SCALE = 1.0 / 32**0.5
EXP2 = SCALE * 1.4426950408889634
NORM = 1.0 / 73728**0.5
NN = (((1,), (0,)), ((), ()))
NT = (((1,), (1,)), ((), ()))
TN = (((0,), (0,)), ((), ()))
MESH = pl.DeviceIdType.MESH

STARTS = (0, 224, 448, 528)
ROWS = 608
SECTIONS = ((224, 224), (448, 80), (528, 80))


def section_row(array, level, row, col):
    section = (2 if col < 6 else 0) + (1 if row < 3 else 0)
    width, first = (18, 6) if col >= 6 else (6, 0)
    at = (level * 3 + row % 3) * width + col - first
    return STARTS[section] + array * 6 * width + at


def orders():
    pack = np.zeros((ROWS, 576), np.float32)
    place = np.zeros((576, ROWS), np.float32)
    for array in range(2):
        for level in range(2):
            for row in range(6):
                for col in range(24):
                    at = array * 288 + level * 144 + row * 24 + col
                    pack[section_row(array, level, row, col), at] = 1
            for row in range(6):
                for col in range(24):
                    at = array * 288 + col // 12 * 144 + level * 72 + row * 12 + col % 12
                    source = section_row(array, level, (row + 3) % 6, (col + 6) % 24)
                    place[at, source] = 1
    return [jnp.asarray(m, BF) for m in (pack, place, place.T, pack.T)]


def dot(a, b, dims=NN):
    return lax.dot_general(a, b, dims, preferred_element_type=F32)


def head_mask(dtype):
    head = lax.broadcasted_iota(jnp.int32, (128, 256), 0) >> 4
    col = lax.broadcasted_iota(jnp.int32, (128, 256), 1) >> 5
    return (head == col).astype(dtype)


def window_rows(w):
    return pl.ds(pl.multiple_of(w * 144, 16), 144)


def pair_rows(p):
    return slice(288 * p, 288 * p + 288)


def project(p, tok, cot, w_qkv, w_proj_t, hat, normed, inv, q, k, v, dc):
    rows = pair_rows(p)
    x = tok[rows, :].astype(F32)
    x = x - jnp.mean(x, axis=1, keepdims=True)
    scale = lax.rsqrt(jnp.mean(x * x, axis=1, keepdims=True) + 1e-05)
    x = x * scale
    hat[rows, :] = x
    inv[rows, :] = jnp.broadcast_to(scale, (288, 128))
    x = x.astype(BF)
    normed[rows, :] = x
    for g in range(2):
        for part, ref in enumerate((q, k, v)):
            at = 512 * part + 256 * g
            ref[g, rows, :] = dot(x, w_qkv[:, at : at + 256]).astype(BF)
        dc[g, rows, :] = dot(cot[rows, :], w_proj_t[:, 256 * g : 256 * g + 256]).astype(BF)


def key_rows(p, c):
    if p == 0 or c == 4:
        return slice(0, 144)
    return slice(0, 80) if c < 4 else slice(64, 144)


def spans(p):
    if p == 0:
        return [(slice(0, 144), slice(0, 1152))]
    return [(key_rows(p, c), slice(128 * c, 128 * d)) for c, d in ((0, 4), (4, 5), (5, 9))]


def attend(p, g, lat_last, lon_last, mask, maskf, q, k, v, dc, qs, cs, pt, st, sf, df, ctx, dqkv):
    def rows(i):
        return slice(144 * (2 * p + i), 144 * (2 * p + i) + 144)

    def scores(i):
        first = 144 * (2 * p + i)
        keys, vals = k[g, rows(i), :], v[g, rows(i), :]
        for c in range(9):
            at = slice(128 * c, 128 * c + 128)
            q16 = q[g, first + 16 * c : first + 16 * c + 16, :]
            d16 = dc[g, first + 16 * c : first + 16 * c + 16, :]
            qs[i, at, :] = jnp.concatenate([q16] * 8, axis=0) * mask
            cs[i, at, :] = jnp.concatenate([d16] * 8, axis=0) * mask
        for kr, at in spans(p):
            sf[i, kr, at] = dot(keys[kr], qs[i, at, :], NT)
            df[i, kr, at] = dot(vals[kr], cs[i, at, :], NT)

    def softmax(i):
        klab, qlab = labels(2 * p + i, lat_last, lon_last)
        for c in range(9):
            at = slice(128 * c, 128 * c + 128)
            kr = key_rows(p, c)
            s = jnp.where(klab[kr] == qlab[c], sf[i, kr, at], -1e30)
            e = jnp.exp2((s - jnp.max(s, axis=0, keepdims=True)) * EXP2)
            prob = e * (1.0 / jnp.sum(e, axis=0, keepdims=True))
            pt[2 * p + i, kr, at] = prob.astype(BF)
            dp = df[i, kr, at]
            inner = jnp.sum(prob * dp, axis=0, keepdims=True)
            st[2 * p + i, kr, at] = ((prob * SCALE) * (dp - inner)).astype(BF)

    def fold(m, i, ref):
        out = [dot(m[2 * p + i, kr, at], ref[g, rows(i), :][kr], TN) for kr, at in spans(p)]
        out = jnp.concatenate(out, axis=0) if len(out) > 1 else out[0]
        out = out.reshape(9, 8, 16, 256) * maskf.reshape(1, 8, 16, 256)
        return jnp.sum(out, axis=1).reshape(144, 256).astype(BF)

    def columns(part):
        return pl.ds(pl.multiple_of(768 * g + 256 * part, 256), 256)

    def results(i):
        ctx[rows(i), pl.ds(pl.multiple_of(256 * g, 256), 256)] = fold(pt, i, v)
        dqkv[rows(i), columns(0)] = fold(st, i, k)
        dqkv[rows(i), columns(1)] = dot(st[2 * p + i], qs[i]).astype(BF)
        dqkv[rows(i), columns(2)] = dot(pt[2 * p + i], cs[i]).astype(BF)

    scores(0)
    scores(1)
    softmax(0)
    results(0)
    softmax(1)
    results(1)


def finish(p, w_qkv_t, w_proj, hat, inv, ctx, dqkv, done):
    rows = pair_rows(p)
    done[p, 0:288, :] = dot(ctx[rows, :], w_proj[...]).astype(BF)
    d = dot(dqkv[rows, :], w_qkv_t[...])
    h = hat[rows, :]
    d = d - jnp.mean(d, axis=1, keepdims=True) - h * jnp.mean(d * h, axis=1, keepdims=True)
    scale = jnp.concatenate([inv[rows, :]] * 4, axis=1)
    done[p, 288:576, :] = (d * scale).astype(BF)


def labels(w, lat_last, lon_last):
    def flags(t):
        level = (t >= 72).astype(jnp.int32)
        t = t - 72 * level
        row = (t >= 36).astype(jnp.int32)
        t = t - 36 * row
        t = jnp.where(t >= 24, t - 24, jnp.where(t >= 12, t - 12, t))
        col = (t >= 6).astype(jnp.int32)
        return level * is_b + row * lat_last + col * last

    is_b = 4 * (w // 2)
    last = lon_last * (w % 2)
    klab = flags(lax.broadcasted_iota(jnp.int32, (144, 128), 0))
    lane = lax.broadcasted_iota(jnp.int32, (1, 128), 1) & 15
    qlab = [flags(lane + 16 * c) for c in range(9)]
    return klab, qlab


def weight_gradients(g, normed, cot, ctx, dqkv, grad):
    def keep(d, half, at, count):
        for b in range(2):
            piece = d[:, 128 * b : 128 * b + 128].astype(BF)
            grad[g, half, b, at : at + count] = piece.reshape(count, 16, 128)

    for part in range(3):
        at = 768 * g + 256 * part
        d = dot(normed[...], dqkv[:, at : at + 256], TN)
        keep(d, part // 2, 32 * (part % 2), 32)
    d = dot(ctx[:, 256 * g : 256 * g + 256], cot[...], TN)
    for half in range(2):
        keep(d[:, 256 * half : 256 * half + 256], 1, 32 + 16 * half, 16)


def place():
    lat, lon = lax.axis_index("lat"), lax.axis_index("lon")
    return (lon // 2) % 4, (lon // 8) * 2 + lat % 2, lat // 2, lon % 2


def device(x, y, z, core):
    return z * 2 + y % 2, ((y // 2) * 4 + x) * 2 + core


def first_at(b):
    x, y, z, core = place()
    return x if b == 0 else z


def first_device(b, to):
    x, y, z, core = place()
    return device(to, y, z, core) if b == 0 else device(x, y, to, core)


def second_at(b):
    x, y, z, core = place()
    return y * 4 + (z if b == 0 else x)


def second_device(b, to):
    x, y, z, core = place()
    return device(x, to // 4, to % 4, core) if b == 0 else device(to % 4, to // 4, z, core)


def beside(lat_step, lon_step):
    lat, lon = lax.axis_index("lat"), lax.axis_index("lon")
    return lax.rem(lat + lat_step + 8, 8), lax.rem(lon + lon_step + 16, 16)


def drain(ref, sem):
    pltpu.make_async_copy(ref, ref, sem).wait()


def greet():
    x, y, z, core = place()
    barrier = pltpu.get_barrier_semaphore()

    def signal(to):
        pl.semaphore_signal(barrier, inc=1, device_id=to, device_id_type=MESH)

    for steps in ((-1, 0), (0, -1), (-1, -1), (1, 0), (0, 1), (1, 1)):
        signal(beside(*steps))
    signal(device(x, y, z, 1 - core))
    for b in range(2):
        for k in range(1, 4):
            signal(first_device(b, first_at(b) ^ k))

        @pl.loop(1, 16)
        def _(t):
            signal(second_device(b, second_at(b) ^ t))


def meet():
    pl.semaphore_wait(pltpu.get_barrier_semaphore(), 43)


def halo(p, step, src, dst, send, recv):
    copies = []
    for s, (at, count) in enumerate(SECTIONS):
        lat_step, lon_step = ((step, 0), (0, step), (step, step))[s]
        copies.append(pltpu.make_async_remote_copy(
            src_ref=src.at[p, pl.ds(at, count)], dst_ref=dst.at[p, pl.ds(at, count)],
            send_sem=send.at[p, s], recv_sem=recv.at[p, s],
            device_id=beside(lat_step, lon_step), device_id_type=MESH,
        ))
    return copies


def core_swap(src, dst, send, recv):
    x, y, z, core = place()
    return pltpu.make_async_remote_copy(
        src_ref=src, dst_ref=dst, send_sem=send, recv_sem=recv,
        device_id=device(x, y, z, 1 - core), device_id_type=MESH,
    )


def scatter_first(mixed, parts, send, recv):
    for b in range(2):
        at = first_at(b)
        for k in (2, 1, 3):
            pltpu.make_async_remote_copy(
                src_ref=mixed.at[b, pl.ds((at ^ k) * 16, 16)], dst_ref=parts.at[b, at],
                send_sem=send.at[b], recv_sem=recv.at[b],
                device_id=first_device(b, at ^ k), device_id_type=MESH,
            ).start()


def scatter_second(mixed, parts, send, recv):
    for b in range(2):
        at = second_at(b)

        @pl.loop(0, 15)
        def _(t):
            to = at ^ (15 - t)
            pltpu.make_async_remote_copy(
                src_ref=mixed.at[b, to], dst_ref=parts.at[b, at],
                send_sem=send.at[b], recv_sem=recv.at[b],
                device_id=second_device(b, to), device_id_type=MESH,
            ).start()


def gather_second(total, send, recv):
    for b in range(2):
        at = second_at(b)
        piece = total.at[b, first_at(b) * 16 + at]

        @pl.loop(0, 15)
        def _(t):
            pltpu.make_async_remote_copy(
                src_ref=piece, dst_ref=piece, send_sem=send.at[b], recv_sem=recv.at[b],
                device_id=second_device(b, at ^ (15 - t)), device_id_type=MESH,
            ).start()


def gather_first(b, total, send, recv):
    at = first_at(b)
    piece = total.at[b, pl.ds(at * 16, 16)]
    for k in (2, 1, 3):
        pltpu.make_async_remote_copy(
            src_ref=piece, dst_ref=piece, send_sem=send.at[b, k], recv_sem=recv.at[b, k],
            device_id=first_device(b, at ^ k), device_id_type=MESH,
        ).start()


def kernel(
    tokens, cotangent, w_qkv_in, w_proj_in, pack_in, place_in, unplace_in, unpack_in,
    output, grad_tokens, total_out,
    moved, both, w_qkv, w_proj, w_qkv_t, w_proj_t, pack, place_m, unplace, unpack, out_halo, in_halo, out_back, in_back,
    tok, cot, hat, normed, inv, q, k, v, dc, qs, cs, pt, st, sf, df, ctx, dqkv, done,
    grad, swapped, mixed, parts, mixed2, parts2, total, load, store, swap_send, swap_recv, send, recv, core_send, core_recv, wide_send, wide_recv, hsend, hrecv, bsend, brecv,
):
    x, y, z, core = place()
    greet()
    loads = []

    def fetch(src, dst):
        copy = pltpu.make_async_copy(src, dst, load.at[len(loads)])
        copy.start()
        loads.append(copy)

    for p in range(2):
        for half, src in enumerate((tokens, cotangent)):
            for level in range(2):
                fetch(
                    src.at[pl.ds(144 * ((2 * p + 1 + level) % 4), 144)],
                    both.at[p, pl.ds(288 * half + 144 * level, 144)],
                )
    fetch(pack_in, pack)
    early = len(loads)
    fetch(place_in, place_m)
    fetch(w_qkv_in, w_qkv)
    fetch(w_proj_in, w_proj)
    fetch(unplace_in, unplace)
    fetch(unpack_in, unpack)
    for copy in loads[:early]:
        copy.wait()
    out_halo[0] = dot(pack[...], both[0]).astype(BF)
    meet()
    coming = [halo(p, -1, out_halo, in_halo, hsend, hrecv) for p in range(2)]
    for copy in coming[0]:
        copy.start()
    out_halo[1] = dot(pack[...], both[1]).astype(BF)
    for copy in coming[1]:
        copy.start()
    for copy in loads[early:]:
        copy.wait()
    for g in range(2):
        for part in range(3):
            at = 512 * part + 256 * g
            to = 768 * g + 256 * part
            w_qkv_t[to : to + 256, :] = w_qkv[:, at : at + 256].T
    w_proj_t[...] = w_proj[...].T
    for i in range(2):
        pt[2 + i] = jnp.zeros((144, 1152), BF)
        st[2 + i] = jnp.zeros((144, 1152), BF)
    lat_last = 2 * (lax.axis_index("lat") == 7).astype(jnp.int32)
    lon_last = (lax.axis_index("lon") == 15).astype(jnp.int32)
    mask = head_mask(BF)
    maskf = head_mask(F32)

    def arrive(p):
        in_halo[p, 0:224] = out_halo[p, 0:224]
        for copy in coming[p]:
            copy.wait_recv()
        tok[pair_rows(p), :] = dot(place_m[0:288, :], in_halo[p]).astype(BF)
        cot[pair_rows(p), :] = dot(place_m[288:576, :], in_halo[p]).astype(BF)
        project(p, tok, cot, w_qkv, w_proj_t, hat, normed, inv, q, k, v, dc)

    def attention(p, g):
        attend(p, g, lat_last, lon_last, mask, maskf, q, k, v, dc, qs, cs, pt, st, sf, df, ctx, dqkv)

    def swap_in(g):
        return core_swap(grad.at[g, 1 - core], swapped.at[g], swap_send.at[g], swap_recv.at[g])

    def sum_first(g):
        swap_in(g).wait()
        mixed[g] = (grad[g, core].astype(F32) + swapped[g].astype(F32)).astype(BF)
        scatter_first(mixed.at[g], parts.at[g], send.at[g], recv.at[g])
        for b in range(2):
            at = first_at(b)
            parts[g, b, at] = mixed[g, b, pl.ds(at * 16, 16)]

    def sum_second():
        for b in range(2):
            for g in range(2):
                drain(parts.at[g, b, pl.ds(0, 3)], recv.at[g, b])
                mixed2[b, :, g] = jnp.sum(parts[g, b].astype(F32), axis=0).astype(BF)
        scatter_second(mixed2, parts2, send.at[2], recv.at[2])
        for b in range(2):
            at = second_at(b)
            parts2[b, at] = mixed2[b, at]

    def spread_second():
        for b in range(2):
            drain(parts2.at[b, pl.ds(0, 15)], recv.at[2, b])
            final = jnp.sum(parts2[b].astype(F32), axis=0) * NORM
            total[core, b, first_at(b) * 16 + second_at(b)] = final.astype(BF)
        gather_second(total.at[core], send.at[3], recv.at[3])

    def core_out(b, i):
        part = total.at[core, b, pl.ds((first_at(b) ^ i) * 16, 16)]
        return core_swap(part, part, core_send.at[b, i], core_recv.at[b, i])

    def spread_first():
        for b in range(2):
            drain(parts2.at[b, pl.ds(0, 15)], recv.at[3, b])
            gather_first(b, total.at[core], wide_send, wide_recv)
        send_back(1)
        for b in range(2):
            core_out(b, 0).start()
        for i in (1, 3, 2):
            for b in range(2):
                drain(total.at[core, b, pl.ds(0, 16)], wide_recv.at[b, i])
                core_out(b, i).start()

    def store_half(half, i):
        return pltpu.make_async_copy(total.at[half], total_out.at[half], store.at[2 + i])

    def store_moved():
        outs = (output, grad_tokens)
        return [pltpu.make_async_copy(moved.at[i], outs[i], store.at[i]) for i in range(2)]

    def drain_sends():
        for b in range(2):
            for g in range(2):
                drain(parts.at[g, b, pl.ds(0, 3)], send.at[g, b])
                drain(parts2.at[b, pl.ds(0, 15)], send.at[2 + g, b])
            for i in range(1, 4):
                drain(total.at[core, b, pl.ds(0, 16)], wide_send.at[b, i])

    def back(p):
        in_back[p, 0:224] = out_back[p, 0:224]
        for copy in going[p]:
            copy.wait_recv()
        for half in range(2):
            for level in range(2):
                at = 144 * ((2 * p + 1 + level) % 4)
                rows = slice(288 * half + 144 * level, 288 * half + 144 * level + 144)
                d = dot(unpack[rows, :], in_back[p]).astype(BF)
                moved[half, at : at + 144, :] = (both[p, rows, :].astype(F32) + d.astype(F32)).astype(BF)

    going = [halo(p, 1, out_back, in_back, bsend, brecv) for p in range(2)]

    def leave(p):
        finish(p, w_qkv_t, w_proj, hat, inv, ctx, dqkv, done)
        out_back[p] = dot(unplace[...], done[p]).astype(BF)

    def send_back(p):
        for copy in going[p]:
            copy.start()

    arrive(0)

    @pl.loop(0, 2)
    def _(g):
        attention(0, g)

    leave(0)
    send_back(0)
    arrive(1)
    attention(1, 0)
    weight_gradients(0, normed, cot, ctx, dqkv, grad)
    swap_in(0).start()
    attention(1, 1)
    sum_first(0)
    weight_gradients(1, normed, cot, ctx, dqkv, grad)
    swap_in(1).start()
    finish(1, w_qkv_t, w_proj, hat, inv, ctx, dqkv, done)
    sum_first(1)
    out_back[1] = dot(unplace[...], done[1]).astype(BF)
    back(0)
    sum_second()
    spread_second()
    spread_first()
    store_half(core, 0).start()
    back(1)
    for copy in store_moved():
        copy.start()
    drain_sends()
    for p in range(2):
        for copy in coming[p] + going[p]:
            copy.wait_send()
    for b in range(2):
        for i in range(4):
            core_out(b, i).wait()
    store_half(1 - core, 1).start()
    for copy in store_moved() + [store_half(core, 0), store_half(1 - core, 1)]:
        copy.wait()


def block(tokens, cotangent, w_qkv, w_proj):
    hbm = pl.BlockSpec(memory_space=pl.ANY)
    dma = pltpu.SemaphoreType.DMA
    return pl.pallas_call(
        kernel,
        out_shape=(
            jax.ShapeDtypeStruct((576, 512), BF),
            jax.ShapeDtypeStruct((576, 512), BF),
            jax.ShapeDtypeStruct((2, 2, 64, 2, 16, 128), BF),
        ),
        in_specs=[hbm] * 8,
        out_specs=(hbm,) * 3,
        scratch_shapes=[
            pltpu.VMEM((2, 576, 512), BF),
            pltpu.VMEM((2, 576, 512), BF),
            pltpu.VMEM((512, 1536), BF),
            pltpu.VMEM((512, 512), BF),
            pltpu.VMEM((1536, 512), BF),
            pltpu.VMEM((512, 512), BF),
            pltpu.VMEM((ROWS, 576), BF),
            pltpu.VMEM((576, ROWS), BF),
            pltpu.VMEM((ROWS, 576), BF),
            pltpu.VMEM((576, ROWS), BF),
            pltpu.VMEM((2, ROWS, 512), BF),
            pltpu.VMEM((2, ROWS, 512), BF),
            pltpu.VMEM((2, ROWS, 512), BF),
            pltpu.VMEM((2, ROWS, 512), BF),
            pltpu.VMEM((576, 512), BF),
            pltpu.VMEM((576, 512), BF),
            pltpu.VMEM((576, 512), F32),
            pltpu.VMEM((576, 512), BF),
            pltpu.VMEM((576, 128), F32),
            pltpu.VMEM((2, 576, 256), BF),
            pltpu.VMEM((2, 576, 256), BF),
            pltpu.VMEM((2, 576, 256), BF),
            pltpu.VMEM((2, 576, 256), BF),
            pltpu.VMEM((2, 1152, 256), BF),
            pltpu.VMEM((2, 1152, 256), BF),
            pltpu.VMEM((4, 144, 1152), BF),
            pltpu.VMEM((4, 144, 1152), BF),
            pltpu.VMEM((2, 144, 1152), F32),
            pltpu.VMEM((2, 144, 1152), F32),
            pltpu.VMEM((576, 512), BF),
            pltpu.VMEM((576, 1536), BF),
            pltpu.VMEM((2, 576, 512), BF),
            pltpu.VMEM((2, 2, 2, 64, 16, 128), BF),
            pltpu.VMEM((2, 2, 64, 16, 128), BF),
            pltpu.VMEM((2, 2, 64, 16, 128), BF),
            pltpu.VMEM((2, 2, 4, 16, 16, 128), BF),
            pltpu.VMEM((2, 16, 2, 16, 128), BF),
            pltpu.VMEM((2, 16, 2, 16, 128), BF),
            pltpu.VMEM((2, 2, 64, 2, 16, 128), BF),
            dma((16,)),
            dma((4,)),
            dma((2,)),
            dma((2,)),
            dma((4, 2)),
            dma((4, 2)),
            dma((2, 4)),
            dma((2, 4)),
            dma((2, 4)),
            dma((2, 4)),
            dma((2, 3)),
            dma((2, 3)),
            dma((2, 3)),
            dma((2, 3)),
        ],
        compiler_params=pltpu.CompilerParams(
            vmem_limit_bytes=56 * 2**20, collective_id=0, has_side_effects=True
        ),
        name="window_block",
    )(tokens, cotangent, w_qkv, w_proj, *orders())


def hand_over(moved_a, moved_b, total_in, out_a, out_b, gqkv_out, gproj_out, moved, total, gqkv, gproj, load, store):
    loads = [
        pltpu.make_async_copy(total_in.at[0], total.at[0], load.at[0]),
        pltpu.make_async_copy(total_in.at[1], total.at[1], load.at[1]),
        pltpu.make_async_copy(moved_a, moved.at[0], load.at[2]),
        pltpu.make_async_copy(moved_b, moved.at[1], load.at[3]),
    ]
    for copy in loads:
        copy.start()
    stores = []

    def write(src, dst):
        copy = pltpu.make_async_copy(src, dst, store.at[len(stores)])
        copy.start()
        stores.append(copy)

    for part in range(3):
        if part != 1:
            loads[part // 2].wait()
        for g in range(2):
            for b in range(2):
                at = 512 * part + 256 * g + 128 * b
                rows = slice(32 * (part % 2), 32 * (part % 2) + 32)
                gqkv[:, at : at + 128] = total[part // 2, b, rows, g].reshape(512, 128).astype(F32)
        at = pl.ds(512 * part, 512)
        write(gqkv.at[:, at], gqkv_out.at[:, at])
    for g in range(2):
        for b in range(2):
            for side in range(2):
                at = 256 * side + 128 * b
                piece = total[1, b, 32 + 16 * side : 48 + 16 * side, g].reshape(256, 128)
                gproj[256 * g : 256 * g + 256, at : at + 128] = piece.astype(F32)
    write(gproj, gproj_out)
    loads[2].wait()
    write(moved.at[0], out_a)
    loads[3].wait()
    write(moved.at[1], out_b)
    for copy in stores:
        copy.wait()


def body(tokens, cotangent, w_qkv, w_proj):
    shape = tokens.shape
    results = block(tokens.reshape(576, 512), cotangent.reshape(576, 512), w_qkv, w_proj)
    hbm = pl.BlockSpec(memory_space=pl.ANY)
    output, grad_tokens, gqkv, gproj = pl.pallas_call(
        hand_over,
        out_shape=(
            jax.ShapeDtypeStruct((576, 512), BF),
            jax.ShapeDtypeStruct((576, 512), BF),
            jax.ShapeDtypeStruct((512, 1536), F32),
            jax.ShapeDtypeStruct((512, 512), F32),
        ),
        in_specs=[hbm] * 3,
        out_specs=(hbm,) * 4,
        scratch_shapes=[
            pltpu.VMEM((2, 576, 512), BF),
            pltpu.VMEM((2, 2, 64, 2, 16, 128), BF),
            pltpu.VMEM((512, 1536), F32),
            pltpu.VMEM((512, 512), F32),
            pltpu.SemaphoreType.DMA((4,)),
            pltpu.SemaphoreType.DMA((6,)),
        ],
        compiler_params=pltpu.CompilerParams(vmem_limit_bytes=56 * 2**20),
        name="hand_over",
    )(*results)
    return (output.reshape(shape), grad_tokens.reshape(shape), gqkv, gproj)


def solution(mesh):
    spec = P(None, "lat", "lon", None)
    return jax.shard_map(
        body,
        mesh=mesh,
        in_specs=(spec, spec, P(), P()),
        out_specs=(spec, spec, P(), P()),
        check_vma=False,
    )
```

```python
import numpy as np
import jax
import jax.numpy as jnp
from jax import lax
from jax.experimental import pallas as pl
from jax.experimental.pallas import tpu as pltpu
from jax.sharding import PartitionSpec as P

BF = jnp.bfloat16
F32 = jnp.float32
SCALE = 1.0 / 32**0.5
EXP2 = SCALE * 1.4426950408889634
NORM = 1.0 / 73728**0.5
NN = (((1,), (0,)), ((), ()))
NT = (((1,), (1,)), ((), ()))
TN = (((0,), (0,)), ((), ()))
MESH = pl.DeviceIdType.MESH

ROWS = 608
KEPT = ((0, 144), (288, 80))
SENT = (((144, 144, 1, 0),), ((368, 80, 1, 0), (448, 80, 0, 1), (528, 80, 1, 1)))
SPAN = (slice(0, 288), slice(288, 608))


def section_row(array, level, row, col):
    line = level * 3 + row % 3
    if 6 <= col < 18:
        return (144 if row < 3 else 0) + array * 72 + line * 12 + col - 6
    start = (448 if col < 6 else 288) + (80 if row < 3 else 0)
    return start + array * 36 + line * 6 + col % 18


def orders():
    pack = np.zeros((ROWS, 576), np.float32)
    place = np.zeros((2, 288, ROWS), np.float32)
    for array in range(2):
        for level in range(2):
            for row in range(6):
                for col in range(24):
                    at = array * 288 + level * 144 + row * 24 + col
                    pack[section_row(array, level, row, col), at] = 1
                    loc, c = col // 12, col % 12
                    at = array * 144 + level * 72 + row * 12 + c
                    source = section_row(array, level, (row + 3) % 6, (col + 6) % 24)
                    place[loc, at, source] = 1
    place = [place[loc][:, SPAN[loc]] for loc in range(2)]
    return [jnp.asarray(m, BF) for m in (pack, *place, place[0].T, place[1].T, pack.T)]


def dot(a, b, dims=NN):
    return lax.dot_general(a, b, dims, preferred_element_type=F32)


def head_mask(dtype):
    head = lax.broadcasted_iota(jnp.int32, (128, 256), 0) >> 4
    col = lax.broadcasted_iota(jnp.int32, (128, 256), 1) >> 5
    return (head == col).astype(dtype)


def window_rows(w):
    return pl.ds(pl.multiple_of(w * 144, 16), 144)


def pair_rows(p):
    return slice(288 * p, 288 * p + 288)


def project(w, tok, cot, w_qkv, w_proj_t, hat, normed, inv, q, k, v, dc):
    rows = slice(144 * w, 144 * w + 144)
    x = tok[rows, :].astype(F32)
    x = x - jnp.mean(x, axis=1, keepdims=True)
    scale = lax.rsqrt(jnp.mean(x * x, axis=1, keepdims=True) + 1e-05)
    x = x * scale
    hat[rows, :] = x
    inv[rows, :] = jnp.broadcast_to(scale, (144, 128))
    x = x.astype(BF)
    normed[rows, :] = x
    for g in range(2):
        for part, ref in enumerate((q, k, v)):
            at = 512 * part + 256 * g
            ref[g, rows, :] = dot(x, w_qkv[:, at : at + 256]).astype(BF)
        dc[g, rows, :] = dot(cot[rows, :], w_proj_t[:, 256 * g : 256 * g + 256]).astype(BF)


def key_rows(p, c):
    if p == 0 or c == 4:
        return slice(0, 144)
    return slice(0, 80) if c < 4 else slice(64, 144)


def spans(p):
    if p == 0:
        return [(slice(0, 144), slice(0, 1152))]
    return [(key_rows(p, c), slice(128 * c, 128 * d)) for c, d in ((0, 4), (4, 5), (5, 9))]


def attend(w, groups, lat_last, lon_last, mask, maskf, q, k, v, dc, qs, cs, pt, st, sf, df, ctx, dqkv):
    p = w // 2
    first = 144 * w
    rows = slice(first, first + 144)
    klab, qlab = labels(w, lat_last, lon_last)

    def scores(g):
        keys, vals = k[g, rows, :], v[g, rows, :]
        for c in range(9):
            at = slice(128 * c, 128 * c + 128)
            q16 = q[g, first + 16 * c : first + 16 * c + 16, :]
            d16 = dc[g, first + 16 * c : first + 16 * c + 16, :]
            qs[g, at, :] = jnp.concatenate([q16] * 8, axis=0) * mask
            cs[g, at, :] = jnp.concatenate([d16] * 8, axis=0) * mask
        for kr, at in spans(p):
            sf[g, kr, at] = dot(keys[kr], qs[g, at, :], NT)
            df[g, kr, at] = dot(vals[kr], cs[g, at, :], NT)

    def softmax(g):
        for c in range(9):
            at = slice(128 * c, 128 * c + 128)
            kr = key_rows(p, c)
            s = jnp.where(klab[kr] == qlab[c], sf[g, kr, at], -1e30)
            e = jnp.exp2((s - jnp.max(s, axis=0, keepdims=True)) * EXP2)
            prob = e * (1.0 / jnp.sum(e, axis=0, keepdims=True))
            pt[2 * p + g, kr, at] = prob.astype(BF)
            dp = df[g, kr, at]
            inner = jnp.sum(prob * dp, axis=0, keepdims=True)
            st[2 * p + g, kr, at] = ((prob * SCALE) * (dp - inner)).astype(BF)

    def fold(m, g, ref):
        out = [dot(m[2 * p + g, kr, at], ref[g, rows, :][kr], TN) for kr, at in spans(p)]
        out = jnp.concatenate(out, axis=0) if len(out) > 1 else out[0]
        out = out.reshape(9, 8, 16, 256) * maskf.reshape(1, 8, 16, 256)
        return jnp.sum(out, axis=1).reshape(144, 256).astype(BF)

    def results(g):
        at = 768 * g
        ctx[rows, 256 * g : 256 * g + 256] = fold(pt, g, v)
        dqkv[rows, at : at + 256] = fold(st, g, k)
        dqkv[rows, at + 256 : at + 512] = dot(st[2 * p + g], qs[g]).astype(BF)
        dqkv[rows, at + 512 : at + 768] = dot(pt[2 * p + g], cs[g]).astype(BF)

    for g in groups:
        scores(g)
    for g in groups:
        softmax(g)
        results(g)


def finish(p, w_qkv_t, w_proj, hat, inv, ctx, dqkv, done):
    rows = pair_rows(p)
    a = dot(ctx[rows, :], w_proj[...]).astype(BF)
    d = dot(dqkv[rows, :], w_qkv_t[...])
    h = hat[rows, :]
    d = d - jnp.mean(d, axis=1, keepdims=True) - h * jnp.mean(d * h, axis=1, keepdims=True)
    scale = jnp.concatenate([inv[rows, :]] * 4, axis=1)
    d = (d * scale).astype(BF)
    for i in range(2):
        own = slice(144 * i, 144 * i + 144)
        done[2 * p + i, 0:144, :] = a[own]
        done[2 * p + i, 144:288, :] = d[own]


def labels(w, lat_last, lon_last):
    def flags(t):
        level = (t >= 72).astype(jnp.int32)
        t = t - 72 * level
        row = (t >= 36).astype(jnp.int32)
        t = t - 36 * row
        t = jnp.where(t >= 24, t - 24, jnp.where(t >= 12, t - 12, t))
        col = (t >= 6).astype(jnp.int32)
        return level * is_b + row * lat_last + col * last

    is_b = 4 * (w // 2)
    last = lon_last * (w % 2)
    klab = flags(lax.broadcasted_iota(jnp.int32, (144, 128), 0))
    lane = lax.broadcasted_iota(jnp.int32, (1, 128), 1) & 15
    qlab = [flags(lane + 16 * c) for c in range(9)]
    return klab, qlab


def weight_gradients(g, normed, cot, ctx, dqkv, grad):
    def keep(d, half, at, count):
        for b in range(2):
            piece = d[:, 128 * b : 128 * b + 128].astype(BF)
            grad[g, half, b, at : at + count] = piece.reshape(count, 16, 128)

    for part in range(3):
        at = 768 * g + 256 * part
        d = dot(normed[...], dqkv[:, at : at + 256], TN)
        keep(d, part // 2, 32 * (part % 2), 32)
    d = dot(ctx[:, 256 * g : 256 * g + 256], cot[...], TN)
    for half in range(2):
        keep(d[:, 256 * half : 256 * half + 256], 1, 32 + 16 * half, 16)


def place():
    lat, lon = lax.axis_index("lat"), lax.axis_index("lon")
    return (lon // 2) % 4, (lon // 8) * 2 + lat % 2, lat // 2, lon % 2


def device(x, y, z, core):
    return z * 2 + y % 2, ((y // 2) * 4 + x) * 2 + core


def first_at(b):
    x, y, z, core = place()
    return x if b == 0 else z


def first_device(b, to):
    x, y, z, core = place()
    return device(to, y, z, core) if b == 0 else device(x, y, to, core)


def second_at(b):
    x, y, z, core = place()
    return y * 4 + (z if b == 0 else x)


def second_device(b, to):
    x, y, z, core = place()
    return device(x, to // 4, to % 4, core) if b == 0 else device(to % 4, to // 4, z, core)


def beside(lat_step, lon_step):
    lat, lon = lax.axis_index("lat"), lax.axis_index("lon")
    return lax.rem(lat + lat_step + 8, 8), lax.rem(lon + lon_step + 16, 16)


def drain(ref, sem):
    pltpu.make_async_copy(ref, ref, sem).wait()


def greet():
    x, y, z, core = place()
    barrier = pltpu.get_barrier_semaphore()

    def signal(to):
        pl.semaphore_signal(barrier, inc=1, device_id=to, device_id_type=MESH)

    for steps in ((-1, 0), (0, -1), (-1, -1), (1, 0), (0, 1), (1, 1)):
        signal(beside(*steps))
    signal(device(x, y, z, 1 - core))
    for b in range(2):
        for k in range(1, 4):
            signal(first_device(b, first_at(b) ^ k))

        @pl.loop(1, 16)
        def _(t):
            signal(second_device(b, second_at(b) ^ t))


def meet():
    pl.semaphore_wait(pltpu.get_barrier_semaphore(), 43)


def halo(w, step, src, dst, send, recv):
    p, loc = w // 2, w % 2
    copies = []
    for s, (at, count, lat_step, lon_step) in enumerate(SENT[loc]):
        copies.append(pltpu.make_async_remote_copy(
            src_ref=src.at[p, pl.ds(at, count)], dst_ref=dst.at[p, pl.ds(at, count)],
            send_sem=send.at[w, s], recv_sem=recv.at[w, s],
            device_id=beside(step * lat_step, step * lon_step), device_id_type=MESH,
        ))
    return copies


def core_swap(src, dst, send, recv):
    x, y, z, core = place()
    return pltpu.make_async_remote_copy(
        src_ref=src, dst_ref=dst, send_sem=send, recv_sem=recv,
        device_id=device(x, y, z, 1 - core), device_id_type=MESH,
    )


def scatter_first(mixed, parts, send, recv):
    for b in range(2):
        at = first_at(b)
        for k in (2, 1, 3):
            pltpu.make_async_remote_copy(
                src_ref=mixed.at[b, pl.ds((at ^ k) * 16, 16)], dst_ref=parts.at[b, at],
                send_sem=send.at[b], recv_sem=recv.at[b],
                device_id=first_device(b, at ^ k), device_id_type=MESH,
            ).start()


def scatter_second(mixed, parts, send, recv):
    for b in range(2):
        at = second_at(b)

        @pl.loop(0, 15)
        def _(t):
            to = at ^ (15 - t)
            pltpu.make_async_remote_copy(
                src_ref=mixed.at[b, to], dst_ref=parts.at[b, at],
                send_sem=send.at[b], recv_sem=recv.at[b],
                device_id=second_device(b, to), device_id_type=MESH,
            ).start()


def gather_second(total, send, recv):
    for b in range(2):
        at = second_at(b)
        piece = total.at[b, first_at(b) * 16 + at]

        @pl.loop(0, 15)
        def _(t):
            pltpu.make_async_remote_copy(
                src_ref=piece, dst_ref=piece, send_sem=send.at[b], recv_sem=recv.at[b],
                device_id=second_device(b, at ^ (15 - t)), device_id_type=MESH,
            ).start()


def gather_first(b, total, send, recv):
    at = first_at(b)
    piece = total.at[b, pl.ds(at * 16, 16)]
    for k in (2, 1, 3):
        pltpu.make_async_remote_copy(
            src_ref=piece, dst_ref=piece, send_sem=send.at[b, k], recv_sem=recv.at[b, k],
            device_id=first_device(b, at ^ k), device_id_type=MESH,
        ).start()


def kernel(
    tokens, cotangent, w_qkv_in, w_proj_in, pack_in, place_0, place_1, unplace_0, unplace_1, unpack_in,
    output, grad_tokens, total_out,
    moved, both, w_qkv, w_proj, w_qkv_t, w_proj_t, pack, place_a, place_b, unplace_a, unplace_b, unpack, out_halo, in_halo, out_back, in_back,
    tok, cot, hat, normed, inv, q, k, v, dc, qs, cs, pt, st, sf, df, ctx, dqkv, done,
    grad, swapped, mixed, parts, mixed2, parts2, total, load, store, swap_send, swap_recv, send, recv, core_send, core_recv, wide_send, wide_recv, hsend, hrecv, bsend, brecv,
):
    x, y, z, core = place()
    greet()
    loads = []

    def fetch(src, dst):
        copy = pltpu.make_async_copy(src, dst, load.at[len(loads)])
        copy.start()
        loads.append(copy)

    for p in range(2):
        for half, src in enumerate((tokens, cotangent)):
            for level in range(2):
                fetch(
                    src.at[pl.ds(144 * ((2 * p + 1 + level) % 4), 144)],
                    both.at[p, pl.ds(288 * half + 144 * level, 144)],
                )
    fetch(pack_in, pack)
    early = len(loads)
    fetch(place_0, place_a)
    fetch(place_1, place_b)
    fetch(w_qkv_in, w_qkv)
    fetch(w_proj_in, w_proj)
    fetch(unplace_0, unplace_a)
    fetch(unplace_1, unplace_b)
    fetch(unpack_in, unpack)
    for copy in loads[:early]:
        copy.wait()
    out_halo[0] = dot(pack[...], both[0]).astype(BF)
    meet()
    coming = [halo(w, -1, out_halo, in_halo, hsend, hrecv) for w in range(4)]

    def send_in(w):
        for copy in coming[w]:
            copy.start()

    send_in(0)
    send_in(1)
    out_halo[1] = dot(pack[...], both[1]).astype(BF)
    send_in(3)
    send_in(2)
    for copy in loads[early:]:
        copy.wait()
    for g in range(2):
        for part in range(3):
            at = 512 * part + 256 * g
            to = 768 * g + 256 * part
            w_qkv_t[to : to + 256, :] = w_qkv[:, at : at + 256].T
    w_proj_t[...] = w_proj[...].T
    for i in range(2):
        pt[2 + i] = jnp.zeros((144, 1152), BF)
        st[2 + i] = jnp.zeros((144, 1152), BF)
    lat_last = 2 * (lax.axis_index("lat") == 7).astype(jnp.int32)
    lon_last = (lax.axis_index("lon") == 15).astype(jnp.int32)
    mask = head_mask(BF)
    maskf = head_mask(F32)

    def arrive(w):
        p, loc = w // 2, w % 2
        at, count = KEPT[loc]
        in_halo[p, at : at + count] = out_halo[p, at : at + count]
        for copy in coming[w]:
            copy.wait_recv()
        placed = dot((place_a, place_b)[loc][...], in_halo[p, SPAN[loc]]).astype(BF)
        tok[144 * w : 144 * w + 144, :] = placed[0:144]
        cot[144 * w : 144 * w + 144, :] = placed[144:288]
        project(w, tok, cot, w_qkv, w_proj_t, hat, normed, inv, q, k, v, dc)

    def attention(w, groups):
        attend(w, groups, lat_last, lon_last, mask, maskf, q, k, v, dc, qs, cs, pt, st, sf, df, ctx, dqkv)

    def swap_in(g):
        return core_swap(grad.at[g, 1 - core], swapped.at[g], swap_send.at[g], swap_recv.at[g])

    def sum_first(g):
        swap_in(g).wait()
        mixed[g] = (grad[g, core].astype(F32) + swapped[g].astype(F32)).astype(BF)
        scatter_first(mixed.at[g], parts.at[g], send.at[g], recv.at[g])
        for b in range(2):
            at = first_at(b)
            parts[g, b, at] = mixed[g, b, pl.ds(at * 16, 16)]

    def sum_second():
        for b in range(2):
            for g in range(2):
                drain(parts.at[g, b, pl.ds(0, 3)], recv.at[g, b])
                mixed2[b, :, g] = jnp.sum(parts[g, b].astype(F32), axis=0).astype(BF)
        scatter_second(mixed2, parts2, send.at[2], recv.at[2])
        for b in range(2):
            at = second_at(b)
            parts2[b, at] = mixed2[b, at]

    def spread_second():
        for b in range(2):
            drain(parts2.at[b, pl.ds(0, 15)], recv.at[2, b])
            final = jnp.sum(parts2[b].astype(F32), axis=0) * NORM
            total[core, b, first_at(b) * 16 + second_at(b)] = final.astype(BF)
        gather_second(total.at[core], send.at[3], recv.at[3])

    def core_out(b, i):
        part = total.at[core, b, pl.ds((first_at(b) ^ i) * 16, 16)]
        return core_swap(part, part, core_send.at[b, i], core_recv.at[b, i])

    def spread_first():
        for b in range(2):
            drain(parts2.at[b, pl.ds(0, 15)], recv.at[3, b])
            gather_first(b, total.at[core], wide_send, wide_recv)
        for b in range(2):
            core_out(b, 0).start()
        for i in (1, 3, 2):
            for b in range(2):
                drain(total.at[core, b, pl.ds(0, 16)], wide_recv.at[b, i])
                core_out(b, i).start()

    def store_half(half, i):
        return pltpu.make_async_copy(total.at[half], total_out.at[half], store.at[2 + i])

    def store_moved():
        outs = (output, grad_tokens)
        return [pltpu.make_async_copy(moved.at[i], outs[i], store.at[i]) for i in range(2)]

    def drain_sends():
        for b in range(2):
            for g in range(2):
                drain(parts.at[g, b, pl.ds(0, 3)], send.at[g, b])
                drain(parts2.at[b, pl.ds(0, 15)], send.at[2 + g, b])
            for i in range(1, 4):
                drain(total.at[core, b, pl.ds(0, 16)], wide_send.at[b, i])

    def back(p):
        for w in (2 * p, 2 * p + 1):
            at, count = KEPT[w % 2]
            in_back[p, at : at + count] = out_back[p, at : at + count]
            for copy in going[w]:
                copy.wait_recv()
        for half in range(2):
            for level in range(2):
                at = 144 * ((2 * p + 1 + level) % 4)
                rows = slice(288 * half + 144 * level, 288 * half + 144 * level + 144)
                d = dot(unpack[rows, :], in_back[p]).astype(BF)
                moved[half, at : at + 144, :] = (both[p, rows, :].astype(F32) + d.astype(F32)).astype(BF)

    going = [halo(w, 1, out_back, in_back, bsend, brecv) for w in range(4)]

    def leave(p):
        finish(p, w_qkv_t, w_proj, hat, inv, ctx, dqkv, done)

    def send_back(p):
        for w in (2 * p, 2 * p + 1):
            unplace = (unplace_a, unplace_b)[w % 2]
            out_back[p, SPAN[w % 2]] = dot(unplace[...], done[w]).astype(BF)
            for copy in going[w]:
                copy.start()

    for w in (0, 1):
        arrive(w)
        attention(w, (0, 1))
    leave(0)
    send_back(0)
    arrive(3)
    attention(3, (0, 1))
    arrive(2)
    attention(2, (0,))
    weight_gradients(0, normed, cot, ctx, dqkv, grad)
    swap_in(0).start()
    attention(2, (1,))
    sum_first(0)
    weight_gradients(1, normed, cot, ctx, dqkv, grad)
    swap_in(1).start()
    leave(1)
    sum_first(1)
    back(0)
    sum_second()
    spread_second()
    send_back(1)
    spread_first()
    store_half(core, 0).start()
    back(1)
    for copy in store_moved():
        copy.start()
    drain_sends()
    for w in range(4):
        for copy in coming[w] + going[w]:
            copy.wait_send()
    for b in range(2):
        for i in range(4):
            core_out(b, i).wait()
    store_half(1 - core, 1).start()
    for copy in store_moved() + [store_half(core, 0), store_half(1 - core, 1)]:
        copy.wait()


def block(tokens, cotangent, w_qkv, w_proj):
    hbm = pl.BlockSpec(memory_space=pl.ANY)
    dma = pltpu.SemaphoreType.DMA
    return pl.pallas_call(
        kernel,
        out_shape=(
            jax.ShapeDtypeStruct((576, 512), BF),
            jax.ShapeDtypeStruct((576, 512), BF),
            jax.ShapeDtypeStruct((2, 2, 64, 2, 16, 128), BF),
        ),
        in_specs=[hbm] * 10,
        out_specs=(hbm,) * 3,
        scratch_shapes=[
            pltpu.VMEM((2, 576, 512), BF),
            pltpu.VMEM((2, 576, 512), BF),
            pltpu.VMEM((512, 1536), BF),
            pltpu.VMEM((512, 512), BF),
            pltpu.VMEM((1536, 512), BF),
            pltpu.VMEM((512, 512), BF),
            pltpu.VMEM((ROWS, 576), BF),
            pltpu.VMEM((288, 288), BF),
            pltpu.VMEM((288, 320), BF),
            pltpu.VMEM((288, 288), BF),
            pltpu.VMEM((320, 288), BF),
            pltpu.VMEM((576, ROWS), BF),
            pltpu.VMEM((2, ROWS, 512), BF),
            pltpu.VMEM((2, ROWS, 512), BF),
            pltpu.VMEM((2, ROWS, 512), BF),
            pltpu.VMEM((2, ROWS, 512), BF),
            pltpu.VMEM((576, 512), BF),
            pltpu.VMEM((576, 512), BF),
            pltpu.VMEM((576, 512), F32),
            pltpu.VMEM((576, 512), BF),
            pltpu.VMEM((576, 128), F32),
            pltpu.VMEM((2, 576, 256), BF),
            pltpu.VMEM((2, 576, 256), BF),
            pltpu.VMEM((2, 576, 256), BF),
            pltpu.VMEM((2, 576, 256), BF),
            pltpu.VMEM((2, 1152, 256), BF),
            pltpu.VMEM((2, 1152, 256), BF),
            pltpu.VMEM((4, 144, 1152), BF),
            pltpu.VMEM((4, 144, 1152), BF),
            pltpu.VMEM((2, 144, 1152), F32),
            pltpu.VMEM((2, 144, 1152), F32),
            pltpu.VMEM((576, 512), BF),
            pltpu.VMEM((576, 1536), BF),
            pltpu.VMEM((4, 288, 512), BF),
            pltpu.VMEM((2, 2, 2, 64, 16, 128), BF),
            pltpu.VMEM((2, 2, 64, 16, 128), BF),
            pltpu.VMEM((2, 2, 64, 16, 128), BF),
            pltpu.VMEM((2, 2, 4, 16, 16, 128), BF),
            pltpu.VMEM((2, 16, 2, 16, 128), BF),
            pltpu.VMEM((2, 16, 2, 16, 128), BF),
            pltpu.VMEM((2, 2, 64, 2, 16, 128), BF),
            dma((16,)),
            dma((4,)),
            dma((2,)),
            dma((2,)),
            dma((4, 2)),
            dma((4, 2)),
            dma((2, 4)),
            dma((2, 4)),
            dma((2, 4)),
            dma((2, 4)),
            dma((4, 3)),
            dma((4, 3)),
            dma((4, 3)),
            dma((4, 3)),
        ],
        compiler_params=pltpu.CompilerParams(
            vmem_limit_bytes=56 * 2**20, collective_id=0, has_side_effects=True
        ),
        name="window_block",
    )(tokens, cotangent, w_qkv, w_proj, *orders())


def hand_over(moved_a, moved_b, total_in, out_a, out_b, gqkv_out, gproj_out, moved, total, gqkv, gproj, load, store):
    loads = [
        pltpu.make_async_copy(moved_a, moved.at[0], load.at[0]),
        pltpu.make_async_copy(moved_b, moved.at[1], load.at[1]),
    ]
    for half in range(2):
        for b in range(2):
            src, dst = total_in.at[half, b], total.at[half, b]
            loads.append(pltpu.make_async_copy(src, dst, load.at[2 + 2 * half + b]))
    for copy in loads:
        copy.start()
    stores = []

    def write(src, dst):
        copy = pltpu.make_async_copy(src, dst, store.at[len(stores)])
        copy.start()
        stores.append(copy)

    def widen(part):
        for g in range(2):
            for b in range(2):
                at = 512 * part + 256 * g + 128 * b
                rows = slice(32 * (part % 2), 32 * (part % 2) + 32)
                gqkv[:, at : at + 128] = total[part // 2, b, rows, g].reshape(512, 128).astype(F32)
        at = pl.ds(512 * part, 512)
        write(gqkv.at[:, at], gqkv_out.at[:, at])

    loads[0].wait()
    write(moved.at[0], out_a)
    loads[1].wait()
    write(moved.at[1], out_b)
    for copy in loads[2:4]:
        copy.wait()
    widen(0)
    widen(1)
    for copy in loads[4:6]:
        copy.wait()
    widen(2)
    for g in range(2):
        for b in range(2):
            for side in range(2):
                at = 256 * side + 128 * b
                piece = total[1, b, 32 + 16 * side : 48 + 16 * side, g].reshape(256, 128)
                gproj[256 * g : 256 * g + 256, at : at + 128] = piece.astype(F32)
    write(gproj, gproj_out)
    for copy in stores:
        copy.wait()


def body(tokens, cotangent, w_qkv, w_proj):
    shape = tokens.shape
    results = block(tokens.reshape(576, 512), cotangent.reshape(576, 512), w_qkv, w_proj)
    hbm = pl.BlockSpec(memory_space=pl.ANY)
    output, grad_tokens, gqkv, gproj = pl.pallas_call(
        hand_over,
        out_shape=(
            jax.ShapeDtypeStruct((576, 512), BF),
            jax.ShapeDtypeStruct((576, 512), BF),
            jax.ShapeDtypeStruct((512, 1536), F32),
            jax.ShapeDtypeStruct((512, 512), F32),
        ),
        in_specs=[hbm] * 3,
        out_specs=(hbm,) * 4,
        scratch_shapes=[
            pltpu.VMEM((2, 576, 512), BF),
            pltpu.VMEM((2, 2, 64, 2, 16, 128), BF),
            pltpu.VMEM((512, 1536), F32),
            pltpu.VMEM((512, 512), F32),
            pltpu.SemaphoreType.DMA((6,)),
            pltpu.SemaphoreType.DMA((6,)),
        ],
        compiler_params=pltpu.CompilerParams(vmem_limit_bytes=56 * 2**20),
        name="hand_over",
    )(*results)
    return (output.reshape(shape), grad_tokens.reshape(shape), gqkv, gproj)


def solution(mesh):
    spec = P(None, "lat", "lon", None)
    return jax.shard_map(
        body,
        mesh=mesh,
        in_specs=(spec, spec, P(), P()),
        out_specs=(spec, spec, P(), P()),
        check_vma=False,
    )
```

```python
import numpy as np
import jax
import jax.numpy as jnp
from jax import lax
from jax.experimental import pallas as pl
from jax.experimental.pallas import tpu as pltpu
from jax.sharding import PartitionSpec as P

BF = jnp.bfloat16
F32 = jnp.float32
SCALE = 1.0 / 32**0.5
EXP2 = SCALE * 1.4426950408889634
NORM = 1.0 / 73728**0.5
NN = (((1,), (0,)), ((), ()))
NT = (((1,), (1,)), ((), ()))
TN = (((0,), (0,)), ((), ()))
MESH = pl.DeviceIdType.MESH

ROWS = 608
KEPT = ((0, 144), (288, 80))
SENT = (((144, 144, 1, 0),), ((368, 80, 1, 0), (448, 80, 0, 1), (528, 80, 1, 1)))
SPAN = (slice(0, 288), slice(288, 608))


def section_row(array, level, row, col):
    line = level * 3 + row % 3
    if 6 <= col < 18:
        return (144 if row < 3 else 0) + array * 72 + line * 12 + col - 6
    start = (448 if col < 6 else 288) + (80 if row < 3 else 0)
    return start + array * 36 + line * 6 + col % 18


def orders():
    pack = np.zeros((ROWS, 576), np.float32)
    place = np.zeros((2, 288, ROWS), np.float32)
    for array in range(2):
        for level in range(2):
            for row in range(6):
                for col in range(24):
                    at = array * 288 + level * 144 + row * 24 + col
                    pack[section_row(array, level, row, col), at] = 1
                    loc, c = col // 12, col % 12
                    at = array * 144 + level * 72 + row * 12 + c
                    source = section_row(array, level, (row + 3) % 6, (col + 6) % 24)
                    place[loc, at, source] = 1
    place = [place[loc][:, SPAN[loc]] for loc in range(2)]
    return [jnp.asarray(m, BF) for m in (pack, *place, place[0].T, place[1].T, pack.T)]


def dot(a, b, dims=NN):
    return lax.dot_general(a, b, dims, preferred_element_type=F32)


def head_mask(dtype):
    head = lax.broadcasted_iota(jnp.int32, (128, 256), 0) >> 4
    col = lax.broadcasted_iota(jnp.int32, (128, 256), 1) >> 5
    return (head == col).astype(dtype)


def window_rows(w):
    return pl.ds(pl.multiple_of(w * 144, 16), 144)


def pair_rows(p):
    return slice(288 * p, 288 * p + 288)


def project(w, tok, cot, w_qkv, w_proj_t, hat, normed, inv, q, k, v, dc):
    rows = slice(144 * w, 144 * w + 144)
    x = tok[rows, :].astype(F32)
    x = x - jnp.mean(x, axis=1, keepdims=True)
    scale = lax.rsqrt(jnp.mean(x * x, axis=1, keepdims=True) + 1e-05)
    x = x * scale
    hat[rows, :] = x
    inv[rows, :] = jnp.broadcast_to(scale, (144, 128))
    x = x.astype(BF)
    normed[rows, :] = x
    for g in range(2):
        for part, ref in enumerate((q, k, v)):
            at = 512 * part + 256 * g
            ref[g, rows, :] = dot(x, w_qkv[:, at : at + 256]).astype(BF)
        dc[g, rows, :] = dot(cot[rows, :], w_proj_t[:, 256 * g : 256 * g + 256]).astype(BF)


def key_rows(p, c):
    if p == 0 or c == 4:
        return slice(0, 144)
    return slice(0, 80) if c < 4 else slice(64, 144)


def spans(p):
    if p == 0:
        return [(slice(0, 144), slice(0, 1152))]
    return [(key_rows(p, c), slice(128 * c, 128 * d)) for c, d in ((0, 4), (4, 5), (5, 9))]


def attend(w, groups, lat_last, lon_last, mask, maskf, q, k, v, dc, qs, cs, pt, st, sf, df, ctx, dqkv):
    p = w // 2
    first = 144 * w
    rows = slice(first, first + 144)
    klab, qlab = labels(w, lat_last, lon_last)

    def scores(g):
        keys, vals = k[g, rows, :], v[g, rows, :]
        for c in range(9):
            at = slice(128 * c, 128 * c + 128)
            q16 = q[g, first + 16 * c : first + 16 * c + 16, :]
            d16 = dc[g, first + 16 * c : first + 16 * c + 16, :]
            qs[g, at, :] = jnp.concatenate([q16] * 8, axis=0) * mask
            cs[g, at, :] = jnp.concatenate([d16] * 8, axis=0) * mask
        for kr, at in spans(p):
            sf[g, kr, at] = dot(keys[kr], qs[g, at, :], NT)
            df[g, kr, at] = dot(vals[kr], cs[g, at, :], NT)

    def softmax(g):
        for c in range(9):
            at = slice(128 * c, 128 * c + 128)
            kr = key_rows(p, c)
            s = jnp.where(klab[kr] == qlab[c], sf[g, kr, at], -1e30)
            e = jnp.exp2((s - jnp.max(s, axis=0, keepdims=True)) * EXP2)
            prob = e * (1.0 / jnp.sum(e, axis=0, keepdims=True))
            pt[2 * p + g, kr, at] = prob.astype(BF)
            dp = df[g, kr, at]
            inner = jnp.sum(prob * dp, axis=0, keepdims=True)
            st[2 * p + g, kr, at] = ((prob * SCALE) * (dp - inner)).astype(BF)

    def fold(m, g, ref):
        out = [dot(m[2 * p + g, kr, at], ref[g, rows, :][kr], TN) for kr, at in spans(p)]
        out = jnp.concatenate(out, axis=0) if len(out) > 1 else out[0]
        out = out.reshape(9, 8, 16, 256) * maskf.reshape(1, 8, 16, 256)
        return jnp.sum(out, axis=1).reshape(144, 256).astype(BF)

    def results(g):
        at = 768 * g
        ctx[rows, 256 * g : 256 * g + 256] = fold(pt, g, v)
        dqkv[rows, at : at + 256] = fold(st, g, k)
        dqkv[rows, at + 256 : at + 512] = dot(st[2 * p + g], qs[g]).astype(BF)
        dqkv[rows, at + 512 : at + 768] = dot(pt[2 * p + g], cs[g]).astype(BF)

    for g in groups:
        scores(g)
    for g in groups:
        softmax(g)
        results(g)


def finish(p, w_qkv_t, w_proj, hat, inv, ctx, dqkv, done):
    rows = pair_rows(p)
    a = dot(ctx[rows, :], w_proj[...]).astype(BF)
    d = dot(dqkv[rows, :], w_qkv_t[...])
    h = hat[rows, :]
    d = d - jnp.mean(d, axis=1, keepdims=True) - h * jnp.mean(d * h, axis=1, keepdims=True)
    scale = jnp.concatenate([inv[rows, :]] * 4, axis=1)
    d = (d * scale).astype(BF)
    for i in range(2):
        own = slice(144 * i, 144 * i + 144)
        done[2 * p + i, 0:144, :] = a[own]
        done[2 * p + i, 144:288, :] = d[own]


def labels(w, lat_last, lon_last):
    def flags(t):
        level = (t >= 72).astype(jnp.int32)
        t = t - 72 * level
        row = (t >= 36).astype(jnp.int32)
        t = t - 36 * row
        t = jnp.where(t >= 24, t - 24, jnp.where(t >= 12, t - 12, t))
        col = (t >= 6).astype(jnp.int32)
        return level * is_b + row * lat_last + col * last

    is_b = 4 * (w // 2)
    last = lon_last * (w % 2)
    klab = flags(lax.broadcasted_iota(jnp.int32, (144, 128), 0))
    lane = lax.broadcasted_iota(jnp.int32, (1, 128), 1) & 15
    qlab = [flags(lane + 16 * c) for c in range(9)]
    return klab, qlab


def weight_gradients(g, normed, cot, ctx, dqkv, grad):
    def keep(d, half, at, count):
        for b in range(2):
            piece = d[:, 128 * b : 128 * b + 128].astype(BF)
            grad[g, half, b, at : at + count] = piece.reshape(count, 16, 128)

    for part in range(3):
        at = 768 * g + 256 * part
        d = dot(normed[...], dqkv[:, at : at + 256], TN)
        keep(d, part // 2, 32 * (part % 2), 32)
    d = dot(ctx[:, 256 * g : 256 * g + 256], cot[...], TN)
    for half in range(2):
        keep(d[:, 256 * half : 256 * half + 256], 1, 32 + 16 * half, 16)


def place():
    lat, lon = lax.axis_index("lat"), lax.axis_index("lon")
    return (lon // 2) % 4, (lon // 8) * 2 + lat % 2, lat // 2, lon % 2


def device(x, y, z, core):
    return z * 2 + y % 2, ((y // 2) * 4 + x) * 2 + core


def first_at(b):
    x, y, z, core = place()
    return x if b == 0 else z


def first_device(b, to):
    x, y, z, core = place()
    return device(to, y, z, core) if b == 0 else device(x, y, to, core)


def second_at(b):
    x, y, z, core = place()
    return y * 4 + (z if b == 0 else x)


def second_device(b, to):
    x, y, z, core = place()
    return device(x, to // 4, to % 4, core) if b == 0 else device(to % 4, to // 4, z, core)


def beside(lat_step, lon_step):
    lat, lon = lax.axis_index("lat"), lax.axis_index("lon")
    return lax.rem(lat + lat_step + 8, 8), lax.rem(lon + lon_step + 16, 16)


def drain(ref, sem):
    pltpu.make_async_copy(ref, ref, sem).wait()


def greet():
    x, y, z, core = place()
    barrier = pltpu.get_barrier_semaphore()

    def signal(to):
        pl.semaphore_signal(barrier, inc=1, device_id=to, device_id_type=MESH)

    for steps in ((-1, 0), (0, -1), (-1, -1), (1, 0), (0, 1), (1, 1)):
        signal(beside(*steps))
    signal(device(x, y, z, 1 - core))
    for b in range(2):
        for k in range(1, 4):
            signal(first_device(b, first_at(b) ^ k))

        @pl.loop(1, 16)
        def _(t):
            signal(second_device(b, second_at(b) ^ t))


def meet():
    pl.semaphore_wait(pltpu.get_barrier_semaphore(), 43)


def halo(w, step, src, dst, send, recv):
    p, loc = w // 2, w % 2
    copies = []
    for s, (at, count, lat_step, lon_step) in enumerate(SENT[loc]):
        copies.append(pltpu.make_async_remote_copy(
            src_ref=src.at[p, pl.ds(at, count)], dst_ref=dst.at[p, pl.ds(at, count)],
            send_sem=send.at[w, s], recv_sem=recv.at[w, s],
            device_id=beside(step * lat_step, step * lon_step), device_id_type=MESH,
        ))
    return copies


def core_swap(src, dst, send, recv):
    x, y, z, core = place()
    return pltpu.make_async_remote_copy(
        src_ref=src, dst_ref=dst, send_sem=send, recv_sem=recv,
        device_id=device(x, y, z, 1 - core), device_id_type=MESH,
    )


def scatter_first(mixed, parts, send, recv):
    for b in range(2):
        at = first_at(b)
        for k in (2, 1, 3):
            pltpu.make_async_remote_copy(
                src_ref=mixed.at[b, pl.ds((at ^ k) * 16, 16)], dst_ref=parts.at[b, at],
                send_sem=send.at[b], recv_sem=recv.at[b],
                device_id=first_device(b, at ^ k), device_id_type=MESH,
            ).start()


def scatter_second(g, mixed, parts, send, recv):
    for b in range(2):
        at = second_at(b)

        @pl.loop(0, 15)
        def _(t):
            to = at ^ (15 - t)
            pltpu.make_async_remote_copy(
                src_ref=mixed.at[b, to, g], dst_ref=parts.at[b, at, g],
                send_sem=send.at[b], recv_sem=recv.at[b],
                device_id=second_device(b, to), device_id_type=MESH,
            ).start()


def gather_second(g, total, send, recv):
    for b in range(2):
        at = second_at(b)
        piece = total.at[b, first_at(b) * 16 + at, g]

        @pl.loop(0, 15)
        def _(t):
            pltpu.make_async_remote_copy(
                src_ref=piece, dst_ref=piece, send_sem=send.at[b], recv_sem=recv.at[b],
                device_id=second_device(b, at ^ (15 - t)), device_id_type=MESH,
            ).start()


def gather_first(g, b, total, send, recv):
    at = first_at(b)
    piece = total.at[b, pl.ds(at * 16, 16), g]
    for k in (2, 1, 3):
        pltpu.make_async_remote_copy(
            src_ref=piece, dst_ref=piece, send_sem=send.at[g, b, k], recv_sem=recv.at[g, b, k],
            device_id=first_device(b, at ^ k), device_id_type=MESH,
        ).start()


def kernel(
    tokens, cotangent, w_qkv_in, w_proj_in, pack_in, place_0, place_1, unplace_0, unplace_1, unpack_in,
    output, grad_tokens, total_out,
    moved, both, w_qkv, w_proj, w_qkv_t, w_proj_t, pack, place_a, place_b, unplace_a, unplace_b, unpack, out_halo, in_halo, out_back, in_back,
    tok, cot, hat, normed, inv, q, k, v, dc, qs, cs, pt, st, sf, df, ctx, dqkv, done,
    grad, swapped, mixed, parts, mixed2, parts2, total, load, store, swap_send, swap_recv, send, recv, core_send, core_recv, wide_send, wide_recv, hsend, hrecv, bsend, brecv,
):
    x, y, z, core = place()
    loads = []

    def fetch(src, dst):
        copy = pltpu.make_async_copy(src, dst, load.at[len(loads)])
        copy.start()
        loads.append(copy)

    def fetch_tiles(p):
        for half, src in enumerate((tokens, cotangent)):
            for level in range(2):
                fetch(
                    src.at[pl.ds(144 * ((2 * p + 1 + level) % 4), 144)],
                    both.at[p, pl.ds(288 * half + 144 * level, 144)],
                )

    fetch(pack_in, pack)
    fetch_tiles(0)
    early = len(loads)
    greet()
    fetch_tiles(1)
    middle = len(loads)
    fetch(place_0, place_a)
    fetch(place_1, place_b)
    fetch(w_qkv_in, w_qkv)
    fetch(w_proj_in, w_proj)
    fetch(unplace_0, unplace_a)
    fetch(unplace_1, unplace_b)
    fetch(unpack_in, unpack)
    for copy in loads[:early]:
        copy.wait()
    out_halo[0, SPAN[0]] = dot(pack[SPAN[0], :], both[0]).astype(BF)
    meet()
    coming = [halo(w, -1, out_halo, in_halo, hsend, hrecv) for w in range(4)]

    def send_in(w):
        for copy in coming[w]:
            copy.start()

    send_in(0)
    out_halo[0, SPAN[1]] = dot(pack[SPAN[1], :], both[0]).astype(BF)
    send_in(1)
    for copy in loads[early:middle]:
        copy.wait()
    out_halo[1] = dot(pack[...], both[1]).astype(BF)
    send_in(3)
    send_in(2)
    for copy in loads[middle:]:
        copy.wait()
    for g in range(2):
        for part in range(3):
            at = 512 * part + 256 * g
            to = 768 * g + 256 * part
            w_qkv_t[to : to + 256, :] = w_qkv[:, at : at + 256].T
    w_proj_t[...] = w_proj[...].T
    for i in range(2):
        pt[2 + i] = jnp.zeros((144, 1152), BF)
        st[2 + i] = jnp.zeros((144, 1152), BF)
    lat_last = 2 * (lax.axis_index("lat") == 7).astype(jnp.int32)
    lon_last = (lax.axis_index("lon") == 15).astype(jnp.int32)
    mask = head_mask(BF)
    maskf = head_mask(F32)

    def arrive(w):
        p, loc = w // 2, w % 2
        at, count = KEPT[loc]
        in_halo[p, at : at + count] = out_halo[p, at : at + count]
        for copy in coming[w]:
            copy.wait_recv()
        placed = dot((place_a, place_b)[loc][...], in_halo[p, SPAN[loc]]).astype(BF)
        tok[144 * w : 144 * w + 144, :] = placed[0:144]
        cot[144 * w : 144 * w + 144, :] = placed[144:288]
        project(w, tok, cot, w_qkv, w_proj_t, hat, normed, inv, q, k, v, dc)

    def attention(w, groups):
        attend(w, groups, lat_last, lon_last, mask, maskf, q, k, v, dc, qs, cs, pt, st, sf, df, ctx, dqkv)

    def swap_in(g):
        return core_swap(grad.at[g, 1 - core], swapped.at[g], swap_send.at[g], swap_recv.at[g])

    def sum_first(g):
        swap_in(g).wait()
        mixed[g] = (grad[g, core].astype(F32) + swapped[g].astype(F32)).astype(BF)
        scatter_first(mixed.at[g], parts.at[g], send.at[g], recv.at[g])
        for b in range(2):
            at = first_at(b)
            parts[g, b, at] = mixed[g, b, pl.ds(at * 16, 16)]

    def sum_second(g):
        for b in range(2):
            drain(parts.at[g, b, pl.ds(0, 3)], recv.at[g, b])
            mixed2[b, :, g] = jnp.sum(parts[g, b].astype(F32), axis=0).astype(BF)
        scatter_second(g, mixed2, parts2, send.at[2 + g], recv.at[2 + g])
        for b in range(2):
            at = second_at(b)
            parts2[b, at, g] = mixed2[b, at, g]

    def spread_second(g):
        for b in range(2):
            drain(parts2.at[b, pl.ds(0, 15), g], recv.at[2 + g, b])
            final = jnp.sum(parts2[b, :, g].astype(F32), axis=0) * NORM
            total[core, b, first_at(b) * 16 + second_at(b), g] = final.astype(BF)
        gather_second(g, total.at[core], send.at[4 + g], recv.at[4 + g])

    def core_out(g, b, i):
        part = total.at[core, b, pl.ds((first_at(b) ^ i) * 16, 16), g]
        return core_swap(part, part, core_send.at[g, b, i], core_recv.at[g, b, i])

    def spread_first(g):
        for b in range(2):
            drain(parts2.at[b, pl.ds(0, 15), g], recv.at[4 + g, b])
            gather_first(g, b, total.at[core], wide_send, wide_recv)
            core_out(g, b, 0).start()

    def spread_core(g):
        for i in (1, 3, 2):
            for b in range(2):
                drain(total.at[core, b, pl.ds(0, 16), g], wide_recv.at[g, b, i])
                core_out(g, b, i).start()

    def store_half(half, i):
        return pltpu.make_async_copy(total.at[half], total_out.at[half], store.at[2 + i])

    def store_moved():
        outs = (output, grad_tokens)
        return [pltpu.make_async_copy(moved.at[i], outs[i], store.at[i]) for i in range(2)]

    def drain_sends():
        for g in range(2):
            for b in range(2):
                drain(parts.at[g, b, pl.ds(0, 3)], send.at[g, b])
                drain(parts2.at[b, pl.ds(0, 15), g], send.at[2 + g, b])
                drain(parts2.at[b, pl.ds(0, 15), g], send.at[4 + g, b])
                for i in range(1, 4):
                    drain(total.at[core, b, pl.ds(0, 16), g], wide_send.at[g, b, i])

    def back(p):
        for w in (2 * p, 2 * p + 1):
            at, count = KEPT[w % 2]
            in_back[p, at : at + count] = out_back[p, at : at + count]
            for copy in going[w]:
                copy.wait_recv()
        for half in range(2):
            for level in range(2):
                at = 144 * ((2 * p + 1 + level) % 4)
                rows = slice(288 * half + 144 * level, 288 * half + 144 * level + 144)
                d = dot(unpack[rows, :], in_back[p]).astype(BF)
                moved[half, at : at + 144, :] = (both[p, rows, :].astype(F32) + d.astype(F32)).astype(BF)

    going = [halo(w, 1, out_back, in_back, bsend, brecv) for w in range(4)]

    def leave(p):
        finish(p, w_qkv_t, w_proj, hat, inv, ctx, dqkv, done)

    def send_back(p):
        for w in (2 * p, 2 * p + 1):
            unplace = (unplace_a, unplace_b)[w % 2]
            out_back[p, SPAN[w % 2]] = dot(unplace[...], done[w]).astype(BF)
            for copy in going[w]:
                copy.start()

    for w in (0, 1):
        arrive(w)
        attention(w, (0, 1))
    leave(0)
    send_back(0)
    arrive(3)
    attention(3, (0, 1))
    arrive(2)
    attention(2, (0,))
    weight_gradients(0, normed, cot, ctx, dqkv, grad)
    swap_in(0).start()
    attention(2, (1,))
    sum_first(0)
    weight_gradients(1, normed, cot, ctx, dqkv, grad)
    swap_in(1).start()
    leave(1)
    sum_first(1)
    back(0)
    sum_second(0)
    sum_second(1)
    spread_second(0)
    spread_second(1)
    spread_first(0)
    spread_first(1)
    send_back(1)
    spread_core(0)
    spread_core(1)
    store_half(core, 0).start()
    back(1)
    for copy in store_moved():
        copy.start()
    drain_sends()
    for w in range(4):
        for copy in coming[w] + going[w]:
            copy.wait_send()
    for g in range(2):
        for b in range(2):
            for i in range(4):
                core_out(g, b, i).wait()
    store_half(1 - core, 1).start()
    for copy in store_moved() + [store_half(core, 0), store_half(1 - core, 1)]:
        copy.wait()


def block(tokens, cotangent, w_qkv, w_proj):
    hbm = pl.BlockSpec(memory_space=pl.ANY)
    dma = pltpu.SemaphoreType.DMA
    return pl.pallas_call(
        kernel,
        out_shape=(
            jax.ShapeDtypeStruct((576, 512), BF),
            jax.ShapeDtypeStruct((576, 512), BF),
            jax.ShapeDtypeStruct((2, 2, 64, 2, 16, 128), BF),
        ),
        in_specs=[hbm] * 10,
        out_specs=(hbm,) * 3,
        scratch_shapes=[
            pltpu.VMEM((2, 576, 512), BF),
            pltpu.VMEM((2, 576, 512), BF),
            pltpu.VMEM((512, 1536), BF),
            pltpu.VMEM((512, 512), BF),
            pltpu.VMEM((1536, 512), BF),
            pltpu.VMEM((512, 512), BF),
            pltpu.VMEM((ROWS, 576), BF),
            pltpu.VMEM((288, 288), BF),
            pltpu.VMEM((288, 320), BF),
            pltpu.VMEM((288, 288), BF),
            pltpu.VMEM((320, 288), BF),
            pltpu.VMEM((576, ROWS), BF),
            pltpu.VMEM((2, ROWS, 512), BF),
            pltpu.VMEM((2, ROWS, 512), BF),
            pltpu.VMEM((2, ROWS, 512), BF),
            pltpu.VMEM((2, ROWS, 512), BF),
            pltpu.VMEM((576, 512), BF),
            pltpu.VMEM((576, 512), BF),
            pltpu.VMEM((576, 512), F32),
            pltpu.VMEM((576, 512), BF),
            pltpu.VMEM((576, 128), F32),
            pltpu.VMEM((2, 576, 256), BF),
            pltpu.VMEM((2, 576, 256), BF),
            pltpu.VMEM((2, 576, 256), BF),
            pltpu.VMEM((2, 576, 256), BF),
            pltpu.VMEM((2, 1152, 256), BF),
            pltpu.VMEM((2, 1152, 256), BF),
            pltpu.VMEM((4, 144, 1152), BF),
            pltpu.VMEM((4, 144, 1152), BF),
            pltpu.VMEM((2, 144, 1152), F32),
            pltpu.VMEM((2, 144, 1152), F32),
            pltpu.VMEM((576, 512), BF),
            pltpu.VMEM((576, 1536), BF),
            pltpu.VMEM((4, 288, 512), BF),
            pltpu.VMEM((2, 2, 2, 64, 16, 128), BF),
            pltpu.VMEM((2, 2, 64, 16, 128), BF),
            pltpu.VMEM((2, 2, 64, 16, 128), BF),
            pltpu.VMEM((2, 2, 4, 16, 16, 128), BF),
            pltpu.VMEM((2, 16, 2, 16, 128), BF),
            pltpu.VMEM((2, 16, 2, 16, 128), BF),
            pltpu.VMEM((2, 2, 64, 2, 16, 128), BF),
            dma((16,)),
            dma((4,)),
            dma((2,)),
            dma((2,)),
            dma((6, 2)),
            dma((6, 2)),
            dma((2, 2, 4)),
            dma((2, 2, 4)),
            dma((2, 2, 4)),
            dma((2, 2, 4)),
            dma((4, 3)),
            dma((4, 3)),
            dma((4, 3)),
            dma((4, 3)),
        ],
        compiler_params=pltpu.CompilerParams(
            vmem_limit_bytes=56 * 2**20, collective_id=0, has_side_effects=True
        ),
        name="window_block",
    )(tokens, cotangent, w_qkv, w_proj, *orders())


def hand_over(moved_a, moved_b, total_in, out_a, out_b, gqkv_out, gproj_out, moved, total, gqkv, gproj, load, store):
    loads = [
        pltpu.make_async_copy(moved_a, moved.at[0], load.at[0]),
        pltpu.make_async_copy(moved_b, moved.at[1], load.at[1]),
    ]
    for half in range(2):
        for b in range(2):
            src, dst = total_in.at[half, b], total.at[half, b]
            loads.append(pltpu.make_async_copy(src, dst, load.at[2 + 2 * half + b]))
    for copy in loads:
        copy.start()
    stores = []

    def write(src, dst):
        copy = pltpu.make_async_copy(src, dst, store.at[len(stores)])
        copy.start()
        stores.append(copy)

    def widen(part):
        for g in range(2):
            for b in range(2):
                at = 512 * part + 256 * g + 128 * b
                rows = slice(32 * (part % 2), 32 * (part % 2) + 32)
                gqkv[:, at : at + 128] = total[part // 2, b, rows, g].reshape(512, 128).astype(F32)
        at = pl.ds(512 * part, 512)
        write(gqkv.at[:, at], gqkv_out.at[:, at])

    loads[0].wait()
    write(moved.at[0], out_a)
    loads[1].wait()
    write(moved.at[1], out_b)
    for copy in loads[2:4]:
        copy.wait()
    widen(0)
    widen(1)
    for copy in loads[4:6]:
        copy.wait()
    widen(2)
    for g in range(2):
        for b in range(2):
            for side in range(2):
                at = 256 * side + 128 * b
                piece = total[1, b, 32 + 16 * side : 48 + 16 * side, g].reshape(256, 128)
                gproj[256 * g : 256 * g + 256, at : at + 128] = piece.astype(F32)
    write(gproj, gproj_out)
    for copy in stores:
        copy.wait()


def body(tokens, cotangent, w_qkv, w_proj):
    shape = tokens.shape
    results = block(tokens.reshape(576, 512), cotangent.reshape(576, 512), w_qkv, w_proj)
    hbm = pl.BlockSpec(memory_space=pl.ANY)
    output, grad_tokens, gqkv, gproj = pl.pallas_call(
        hand_over,
        out_shape=(
            jax.ShapeDtypeStruct((576, 512), BF),
            jax.ShapeDtypeStruct((576, 512), BF),
            jax.ShapeDtypeStruct((512, 1536), F32),
            jax.ShapeDtypeStruct((512, 512), F32),
        ),
        in_specs=[hbm] * 3,
        out_specs=(hbm,) * 4,
        scratch_shapes=[
            pltpu.VMEM((2, 576, 512), BF),
            pltpu.VMEM((2, 2, 64, 2, 16, 128), BF),
            pltpu.VMEM((512, 1536), F32),
            pltpu.VMEM((512, 512), F32),
            pltpu.SemaphoreType.DMA((6,)),
            pltpu.SemaphoreType.DMA((6,)),
        ],
        compiler_params=pltpu.CompilerParams(vmem_limit_bytes=56 * 2**20),
        name="hand_over",
    )(*results)
    return (output.reshape(shape), grad_tokens.reshape(shape), gqkv, gproj)


def solution(mesh):
    spec = P(None, "lat", "lon", None)
    return jax.shard_map(
        body,
        mesh=mesh,
        in_specs=(spec, spec, P(), P()),
        out_specs=(spec, spec, P(), P()),
        check_vma=False,
    )
```

```python
import numpy as np
import jax
import jax.numpy as jnp
from jax import lax
from jax.experimental import pallas as pl
from jax.experimental.pallas import tpu as pltpu
from jax.sharding import PartitionSpec as P

BF = jnp.bfloat16
F32 = jnp.float32
SCALE = 1.0 / 32**0.5
EXP2 = SCALE * 1.4426950408889634
NORM = 1.0 / 73728**0.5
NN = (((1,), (0,)), ((), ()))
NT = (((1,), (1,)), ((), ()))
TN = (((0,), (0,)), ((), ()))
MESH = pl.DeviceIdType.MESH

ROWS = 608
KEPT = ((0, 144), (288, 80))
SENT = (((144, 144, 1, 0),), ((368, 80, 1, 0), (448, 80, 0, 1), (528, 80, 1, 1)))
SPAN = (slice(0, 288), slice(288, 608))


def section_row(array, level, row, col):
    line = level * 3 + row % 3
    if 6 <= col < 18:
        return (144 if row < 3 else 0) + array * 72 + line * 12 + col - 6
    start = (448 if col < 6 else 288) + (80 if row < 3 else 0)
    return start + array * 36 + line * 6 + col % 18


def orders():
    pack = np.zeros((ROWS, 576), np.float32)
    place = np.zeros((2, 288, ROWS), np.float32)
    for array in range(2):
        for level in range(2):
            for row in range(6):
                for col in range(24):
                    at = array * 288 + level * 144 + row * 24 + col
                    pack[section_row(array, level, row, col), at] = 1
                    loc, c = col // 12, col % 12
                    at = array * 144 + level * 72 + row * 12 + c
                    source = section_row(array, level, (row + 3) % 6, (col + 6) % 24)
                    place[loc, at, source] = 1
    place = [place[loc][:, SPAN[loc]] for loc in range(2)]
    return [jnp.asarray(m, BF) for m in (pack, *place, place[0].T, place[1].T, pack.T)]


def dot(a, b, dims=NN):
    return lax.dot_general(a, b, dims, preferred_element_type=F32)


def head_mask(dtype):
    head = lax.broadcasted_iota(jnp.int32, (128, 256), 0) >> 4
    col = lax.broadcasted_iota(jnp.int32, (128, 256), 1) >> 5
    return (head == col).astype(dtype)


def window_rows(w):
    return pl.ds(pl.multiple_of(w * 144, 16), 144)


def pair_rows(p):
    return slice(288 * p, 288 * p + 288)


def project(w, tok, cot, w_qkv, w_proj_t, hat, normed, inv, q, k, v, dc):
    rows = slice(144 * w, 144 * w + 144)
    x = tok[rows, :].astype(F32)
    x = x - jnp.mean(x, axis=1, keepdims=True)
    scale = lax.rsqrt(jnp.mean(x * x, axis=1, keepdims=True) + 1e-05)
    x = x * scale
    hat[rows, :] = x
    inv[rows, :] = jnp.broadcast_to(scale, (144, 128))
    x = x.astype(BF)
    normed[rows, :] = x
    for g in range(2):
        for part, ref in enumerate((q, k, v)):
            at = 512 * part + 256 * g
            ref[g, rows, :] = dot(x, w_qkv[:, at : at + 256]).astype(BF)
        dc[g, rows, :] = dot(cot[rows, :], w_proj_t[:, 256 * g : 256 * g + 256]).astype(BF)


def key_rows(p, c):
    if p == 0 or c == 4:
        return slice(0, 144)
    return slice(0, 80) if c < 4 else slice(64, 144)


def spans(p):
    if p == 0:
        return [(slice(0, 144), slice(0, 1152))]
    return [(key_rows(p, c), slice(128 * c, 128 * d)) for c, d in ((0, 4), (4, 5), (5, 9))]


def attend(w, groups, lat_last, lon_last, mask, maskf, q, k, v, dc, qs, cs, pt, st, sf, df, ctx, dqkv):
    p = w // 2
    first = 144 * w
    rows = slice(first, first + 144)
    klab, qlab = labels(w, lat_last, lon_last)

    def scores(g):
        keys, vals = k[g, rows, :], v[g, rows, :]
        for c in range(9):
            at = slice(128 * c, 128 * c + 128)
            q16 = q[g, first + 16 * c : first + 16 * c + 16, :]
            d16 = dc[g, first + 16 * c : first + 16 * c + 16, :]
            qs[g, at, :] = jnp.concatenate([q16] * 8, axis=0) * mask
            cs[g, at, :] = jnp.concatenate([d16] * 8, axis=0) * mask
        for kr, at in spans(p):
            sf[g, kr, at] = dot(keys[kr], qs[g, at, :], NT)
            df[g, kr, at] = dot(vals[kr], cs[g, at, :], NT)

    def softmax(g):
        for c in range(9):
            at = slice(128 * c, 128 * c + 128)
            kr = key_rows(p, c)
            s = jnp.where(klab[kr] == qlab[c], sf[g, kr, at], -1e30)
            e = jnp.exp2((s - jnp.max(s, axis=0, keepdims=True)) * EXP2)
            prob = e * (1.0 / jnp.sum(e, axis=0, keepdims=True))
            pt[2 * p + g, kr, at] = prob.astype(BF)
            dp = df[g, kr, at]
            inner = jnp.sum(prob * dp, axis=0, keepdims=True)
            st[2 * p + g, kr, at] = ((prob * SCALE) * (dp - inner)).astype(BF)

    def fold(m, g, ref):
        out = [dot(m[2 * p + g, kr, at], ref[g, rows, :][kr], TN) for kr, at in spans(p)]
        out = jnp.concatenate(out, axis=0) if len(out) > 1 else out[0]
        out = out.reshape(9, 8, 16, 256) * maskf.reshape(1, 8, 16, 256)
        return jnp.sum(out, axis=1).reshape(144, 256).astype(BF)

    def results(g):
        at = 768 * g
        ctx[rows, 256 * g : 256 * g + 256] = fold(pt, g, v)
        dqkv[rows, at : at + 256] = fold(st, g, k)
        dqkv[rows, at + 256 : at + 512] = dot(st[2 * p + g], qs[g]).astype(BF)
        dqkv[rows, at + 512 : at + 768] = dot(pt[2 * p + g], cs[g]).astype(BF)

    for g in groups:
        scores(g)
    for g in groups:
        softmax(g)
        results(g)


def finish(p, w_qkv_t, w_proj, hat, inv, ctx, dqkv, done):
    rows = pair_rows(p)
    a = dot(ctx[rows, :], w_proj[...]).astype(BF)
    d = dot(dqkv[rows, :], w_qkv_t[...])
    h = hat[rows, :]
    d = d - jnp.mean(d, axis=1, keepdims=True) - h * jnp.mean(d * h, axis=1, keepdims=True)
    scale = jnp.concatenate([inv[rows, :]] * 4, axis=1)
    d = (d * scale).astype(BF)
    for i in range(2):
        own = slice(144 * i, 144 * i + 144)
        done[2 * p + i, 0:144, :] = a[own]
        done[2 * p + i, 144:288, :] = d[own]


def labels(w, lat_last, lon_last):
    def flags(t):
        level = (t >= 72).astype(jnp.int32)
        t = t - 72 * level
        row = (t >= 36).astype(jnp.int32)
        t = t - 36 * row
        t = jnp.where(t >= 24, t - 24, jnp.where(t >= 12, t - 12, t))
        col = (t >= 6).astype(jnp.int32)
        return level * is_b + row * lat_last + col * last

    is_b = 4 * (w // 2)
    last = lon_last * (w % 2)
    klab = flags(lax.broadcasted_iota(jnp.int32, (144, 128), 0))
    lane = lax.broadcasted_iota(jnp.int32, (1, 128), 1) & 15
    qlab = [flags(lane + 16 * c) for c in range(9)]
    return klab, qlab


def weight_gradients(g, normed, cot, ctx, dqkv, grad):
    def keep(d, half, at, count):
        for b in range(2):
            piece = d[:, 128 * b : 128 * b + 128].astype(BF)
            grad[g, half, b, at : at + count] = piece.reshape(count, 16, 128)

    for part in range(3):
        at = 768 * g + 256 * part
        d = dot(normed[...], dqkv[:, at : at + 256], TN)
        keep(d, part // 2, 32 * (part % 2), 32)
    d = dot(ctx[:, 256 * g : 256 * g + 256], cot[...], TN)
    for half in range(2):
        keep(d[:, 256 * half : 256 * half + 256], 1, 32 + 16 * half, 16)


def place():
    lat, lon = lax.axis_index("lat"), lax.axis_index("lon")
    return (lon // 2) % 4, (lon // 8) * 2 + lat % 2, lat // 2, lon % 2


def device(x, y, z, core):
    return z * 2 + y % 2, ((y // 2) * 4 + x) * 2 + core


def first_at(b):
    x, y, z, core = place()
    return x if b == 0 else z


def first_device(b, to):
    x, y, z, core = place()
    return device(to, y, z, core) if b == 0 else device(x, y, to, core)


def second_at(b):
    x, y, z, core = place()
    return y * 4 + (z if b == 0 else x)


def second_device(b, to):
    x, y, z, core = place()
    return device(x, to // 4, to % 4, core) if b == 0 else device(to % 4, to // 4, z, core)


def beside(lat_step, lon_step):
    lat, lon = lax.axis_index("lat"), lax.axis_index("lon")
    return lax.rem(lat + lat_step + 8, 8), lax.rem(lon + lon_step + 16, 16)


def drain(ref, sem):
    pltpu.make_async_copy(ref, ref, sem).wait()


def greet():
    x, y, z, core = place()
    barrier = pltpu.get_barrier_semaphore()

    def signal(to):
        pl.semaphore_signal(barrier, inc=1, device_id=to, device_id_type=MESH)

    for steps in ((-1, 0), (0, -1), (-1, -1), (1, 0), (0, 1), (1, 1)):
        signal(beside(*steps))
    signal(device(x, y, z, 1 - core))
    for b in range(2):
        for k in range(1, 4):
            signal(first_device(b, first_at(b) ^ k))

        @pl.loop(1, 16)
        def _(t):
            signal(second_device(b, second_at(b) ^ t))


def meet():
    pl.semaphore_wait(pltpu.get_barrier_semaphore(), 43)


def halo(w, step, src, dst, send, recv):
    p, loc = w // 2, w % 2
    copies = []
    for s, (at, count, lat_step, lon_step) in enumerate(SENT[loc]):
        copies.append(pltpu.make_async_remote_copy(
            src_ref=src.at[p, pl.ds(at, count)], dst_ref=dst.at[p, pl.ds(at, count)],
            send_sem=send.at[w, s], recv_sem=recv.at[w, s],
            device_id=beside(step * lat_step, step * lon_step), device_id_type=MESH,
        ))
    return copies


def core_swap(src, dst, send, recv):
    x, y, z, core = place()
    return pltpu.make_async_remote_copy(
        src_ref=src, dst_ref=dst, send_sem=send, recv_sem=recv,
        device_id=device(x, y, z, 1 - core), device_id_type=MESH,
    )


def scatter_first(mixed, parts, send, recv):
    for b in range(2):
        at = first_at(b)
        for k in (2, 1, 3):
            pltpu.make_async_remote_copy(
                src_ref=mixed.at[b, pl.ds((at ^ k) * 16, 16)], dst_ref=parts.at[b, at],
                send_sem=send.at[b], recv_sem=recv.at[b],
                device_id=first_device(b, at ^ k), device_id_type=MESH,
            ).start()


def scatter_second(g, mixed, parts, send, recv):
    for b in range(2):
        at = second_at(b)

        @pl.loop(0, 15)
        def _(t):
            to = at ^ (15 - t)
            pltpu.make_async_remote_copy(
                src_ref=mixed.at[b, to, g], dst_ref=parts.at[b, at, g],
                send_sem=send.at[b], recv_sem=recv.at[b],
                device_id=second_device(b, to), device_id_type=MESH,
            ).start()


def gather_second(g, total, send, recv):
    for b in range(2):
        at = second_at(b)
        piece = total.at[b, first_at(b) * 16 + at, g]

        @pl.loop(0, 15)
        def _(t):
            pltpu.make_async_remote_copy(
                src_ref=piece, dst_ref=piece, send_sem=send.at[b], recv_sem=recv.at[b],
                device_id=second_device(b, at ^ (15 - t)), device_id_type=MESH,
            ).start()


def gather_first(g, b, total, send, recv):
    at = first_at(b)
    piece = total.at[b, pl.ds(at * 16, 16), g]
    for k in (2, 1, 3):
        pltpu.make_async_remote_copy(
            src_ref=piece, dst_ref=piece, send_sem=send.at[g, b, k], recv_sem=recv.at[g, b, k],
            device_id=first_device(b, at ^ k), device_id_type=MESH,
        ).start()


def kernel(
    tokens, cotangent, w_qkv_in, w_proj_in, pack_in, place_0, place_1, unplace_0, unplace_1, unpack_in,
    output, grad_tokens, total_out,
    moved, both, w_qkv, w_proj, w_qkv_t, w_proj_t, pack, place_a, place_b, unplace_a, unplace_b, unpack, out_halo, in_halo, out_back, in_back,
    tok, cot, hat, normed, inv, q, k, v, dc, qs, cs, pt, st, sf, df, ctx, dqkv, done,
    grad, swapped, mixed, parts, mixed2, parts2, total, load, store, swap_send, swap_recv, send, recv, core_send, core_recv, wide_send, wide_recv, hsend, hrecv, bsend, brecv,
):
    x, y, z, core = place()
    loads = []

    def fetch(src, dst):
        copy = pltpu.make_async_copy(src, dst, load.at[len(loads)])
        copy.start()
        loads.append(copy)

    def fetch_tiles(p):
        for half, src in enumerate((tokens, cotangent)):
            for level in range(2):
                fetch(
                    src.at[pl.ds(144 * ((2 * p + 1 + level) % 4), 144)],
                    both.at[p, pl.ds(288 * half + 144 * level, 144)],
                )

    fetch(pack_in, pack)
    fetch_tiles(0)
    early = len(loads)
    greet()
    fetch_tiles(1)
    middle = len(loads)
    fetch(place_0, place_a)
    fetch(place_1, place_b)
    fetch(w_qkv_in, w_qkv)
    fetch(w_proj_in, w_proj)
    fetch(unplace_0, unplace_a)
    fetch(unplace_1, unplace_b)
    fetch(unpack_in, unpack)
    for copy in loads[:early]:
        copy.wait()
    out_halo[0, SPAN[0]] = dot(pack[SPAN[0], :], both[0]).astype(BF)
    meet()
    coming = [halo(w, -1, out_halo, in_halo, hsend, hrecv) for w in range(4)]

    def send_in(w):
        for copy in coming[w]:
            copy.start()

    send_in(0)
    out_halo[0, SPAN[1]] = dot(pack[SPAN[1], :], both[0]).astype(BF)
    send_in(1)
    for copy in loads[early:middle]:
        copy.wait()
    out_halo[1] = dot(pack[...], both[1]).astype(BF)
    send_in(3)
    send_in(2)
    for copy in loads[middle:]:
        copy.wait()
    for g in range(2):
        for part in range(3):
            at = 512 * part + 256 * g
            to = 768 * g + 256 * part
            w_qkv_t[to : to + 256, :] = w_qkv[:, at : at + 256].T
    w_proj_t[...] = w_proj[...].T
    for i in range(2):
        pt[2 + i] = jnp.zeros((144, 1152), BF)
        st[2 + i] = jnp.zeros((144, 1152), BF)
    lat_last = 2 * (lax.axis_index("lat") == 7).astype(jnp.int32)
    lon_last = (lax.axis_index("lon") == 15).astype(jnp.int32)
    mask = head_mask(BF)
    maskf = head_mask(F32)

    def arrive(w):
        p, loc = w // 2, w % 2
        at, count = KEPT[loc]
        in_halo[p, at : at + count] = out_halo[p, at : at + count]
        for copy in coming[w]:
            copy.wait_recv()
        placed = dot((place_a, place_b)[loc][...], in_halo[p, SPAN[loc]]).astype(BF)
        tok[144 * w : 144 * w + 144, :] = placed[0:144]
        cot[144 * w : 144 * w + 144, :] = placed[144:288]
        project(w, tok, cot, w_qkv, w_proj_t, hat, normed, inv, q, k, v, dc)

    def attention(w, groups):
        attend(w, groups, lat_last, lon_last, mask, maskf, q, k, v, dc, qs, cs, pt, st, sf, df, ctx, dqkv)

    def swap_in(g):
        return core_swap(grad.at[g, 1 - core], swapped.at[g], swap_send.at[g], swap_recv.at[g])

    def sum_first(g):
        swap_in(g).wait()
        mixed[g] = (grad[g, core].astype(F32) + swapped[g].astype(F32)).astype(BF)
        scatter_first(mixed.at[g], parts.at[g], send.at[g], recv.at[g])
        for b in range(2):
            at = first_at(b)
            parts[g, b, at] = mixed[g, b, pl.ds(at * 16, 16)]

    def sum_second(g):
        for b in range(2):
            drain(parts.at[g, b, pl.ds(0, 3)], recv.at[g, b])
            mixed2[b, :, g] = jnp.sum(parts[g, b].astype(F32), axis=0).astype(BF)
        scatter_second(g, mixed2, parts2, send.at[2 + g], recv.at[2 + g])
        for b in range(2):
            at = second_at(b)
            parts2[b, at, g] = mixed2[b, at, g]

    def spread_second(g):
        for b in range(2):
            drain(parts2.at[b, pl.ds(0, 15), g], recv.at[2 + g, b])
            final = jnp.sum(parts2[b, :, g].astype(F32), axis=0) * NORM
            total[core, b, first_at(b) * 16 + second_at(b), g] = final.astype(BF)
        gather_second(g, total.at[core], send.at[4 + g], recv.at[4 + g])

    def core_out(g, b, i):
        part = total.at[core, b, pl.ds((first_at(b) ^ i) * 16, 16), g]
        return core_swap(part, part, core_send.at[g, b, i], core_recv.at[g, b, i])

    def spread_first(g):
        for b in range(2):
            drain(parts2.at[b, pl.ds(0, 15), g], recv.at[4 + g, b])
            gather_first(g, b, total.at[core], wide_send, wide_recv)
            core_out(g, b, 0).start()

    def spread_core(g):
        for i in (1, 3, 2):
            for b in range(2):
                drain(total.at[core, b, pl.ds(0, 16), g], wide_recv.at[g, b, i])
                core_out(g, b, i).start()

    def store_half(half, i):
        return pltpu.make_async_copy(total.at[half], total_out.at[half], store.at[2 + i])

    def store_moved():
        outs = (output, grad_tokens)
        return [pltpu.make_async_copy(moved.at[i], outs[i], store.at[i]) for i in range(2)]

    def drain_sends():
        for g in range(2):
            for b in range(2):
                drain(parts.at[g, b, pl.ds(0, 3)], send.at[g, b])
                drain(parts2.at[b, pl.ds(0, 15), g], send.at[2 + g, b])
                drain(parts2.at[b, pl.ds(0, 15), g], send.at[4 + g, b])
                for i in range(1, 4):
                    drain(total.at[core, b, pl.ds(0, 16), g], wide_send.at[g, b, i])

    def back(p):
        for w in (2 * p, 2 * p + 1):
            at, count = KEPT[w % 2]
            in_back[p, at : at + count] = out_back[p, at : at + count]
            for copy in going[w]:
                copy.wait_recv()
        for half in range(2):
            for level in range(2):
                at = 144 * ((2 * p + 1 + level) % 4)
                rows = slice(288 * half + 144 * level, 288 * half + 144 * level + 144)
                d = dot(unpack[rows, :], in_back[p]).astype(BF)
                moved[half, at : at + 144, :] = (both[p, rows, :].astype(F32) + d.astype(F32)).astype(BF)

    going = [halo(w, 1, out_back, in_back, bsend, brecv) for w in range(4)]

    def leave(p):
        finish(p, w_qkv_t, w_proj, hat, inv, ctx, dqkv, done)

    def send_back(w):
        unplace = (unplace_a, unplace_b)[w % 2]
        out_back[w // 2, SPAN[w % 2]] = dot(unplace[...], done[w]).astype(BF)
        for copy in going[w]:
            copy.start()

    for w in (0, 1):
        arrive(w)
        attention(w, (0, 1))
    leave(0)
    send_back(0)
    send_back(1)
    arrive(3)
    attention(3, (0, 1))
    arrive(2)
    attention(2, (0,))
    weight_gradients(0, normed, cot, ctx, dqkv, grad)
    swap_in(0).start()
    attention(2, (1,))
    sum_first(0)
    weight_gradients(1, normed, cot, ctx, dqkv, grad)
    swap_in(1).start()
    leave(1)
    send_back(3)
    sum_first(1)
    back(0)
    sum_second(0)
    sum_second(1)
    spread_second(0)
    spread_second(1)
    send_back(2)
    spread_first(0)
    spread_first(1)
    spread_core(0)
    spread_core(1)
    store_half(core, 0).start()
    back(1)
    for copy in store_moved():
        copy.start()
    drain_sends()
    for w in range(4):
        for copy in coming[w] + going[w]:
            copy.wait_send()
    for g in range(2):
        for b in range(2):
            for i in range(4):
                core_out(g, b, i).wait()
    store_half(1 - core, 1).start()
    for copy in store_moved() + [store_half(core, 0), store_half(1 - core, 1)]:
        copy.wait()


def block(tokens, cotangent, w_qkv, w_proj):
    hbm = pl.BlockSpec(memory_space=pl.ANY)
    dma = pltpu.SemaphoreType.DMA
    return pl.pallas_call(
        kernel,
        out_shape=(
            jax.ShapeDtypeStruct((576, 512), BF),
            jax.ShapeDtypeStruct((576, 512), BF),
            jax.ShapeDtypeStruct((2, 2, 64, 2, 16, 128), BF),
        ),
        in_specs=[hbm] * 10,
        out_specs=(hbm,) * 3,
        scratch_shapes=[
            pltpu.VMEM((2, 576, 512), BF),
            pltpu.VMEM((2, 576, 512), BF),
            pltpu.VMEM((512, 1536), BF),
            pltpu.VMEM((512, 512), BF),
            pltpu.VMEM((1536, 512), BF),
            pltpu.VMEM((512, 512), BF),
            pltpu.VMEM((ROWS, 576), BF),
            pltpu.VMEM((288, 288), BF),
            pltpu.VMEM((288, 320), BF),
            pltpu.VMEM((288, 288), BF),
            pltpu.VMEM((320, 288), BF),
            pltpu.VMEM((576, ROWS), BF),
            pltpu.VMEM((2, ROWS, 512), BF),
            pltpu.VMEM((2, ROWS, 512), BF),
            pltpu.VMEM((2, ROWS, 512), BF),
            pltpu.VMEM((2, ROWS, 512), BF),
            pltpu.VMEM((576, 512), BF),
            pltpu.VMEM((576, 512), BF),
            pltpu.VMEM((576, 512), F32),
            pltpu.VMEM((576, 512), BF),
            pltpu.VMEM((576, 128), F32),
            pltpu.VMEM((2, 576, 256), BF),
            pltpu.VMEM((2, 576, 256), BF),
            pltpu.VMEM((2, 576, 256), BF),
            pltpu.VMEM((2, 576, 256), BF),
            pltpu.VMEM((2, 1152, 256), BF),
            pltpu.VMEM((2, 1152, 256), BF),
            pltpu.VMEM((4, 144, 1152), BF),
            pltpu.VMEM((4, 144, 1152), BF),
            pltpu.VMEM((2, 144, 1152), F32),
            pltpu.VMEM((2, 144, 1152), F32),
            pltpu.VMEM((576, 512), BF),
            pltpu.VMEM((576, 1536), BF),
            pltpu.VMEM((4, 288, 512), BF),
            pltpu.VMEM((2, 2, 2, 64, 16, 128), BF),
            pltpu.VMEM((2, 2, 64, 16, 128), BF),
            pltpu.VMEM((2, 2, 64, 16, 128), BF),
            pltpu.VMEM((2, 2, 4, 16, 16, 128), BF),
            pltpu.VMEM((2, 16, 2, 16, 128), BF),
            pltpu.VMEM((2, 16, 2, 16, 128), BF),
            pltpu.VMEM((2, 2, 64, 2, 16, 128), BF),
            dma((16,)),
            dma((4,)),
            dma((2,)),
            dma((2,)),
            dma((6, 2)),
            dma((6, 2)),
            dma((2, 2, 4)),
            dma((2, 2, 4)),
            dma((2, 2, 4)),
            dma((2, 2, 4)),
            dma((4, 3)),
            dma((4, 3)),
            dma((4, 3)),
            dma((4, 3)),
        ],
        compiler_params=pltpu.CompilerParams(
            vmem_limit_bytes=56 * 2**20, collective_id=0, has_side_effects=True
        ),
        name="window_block",
    )(tokens, cotangent, w_qkv, w_proj, *orders())


def hand_over(moved_a, moved_b, total_in, out_a, out_b, gqkv_out, gproj_out, moved, total, gqkv, gproj, load, store):
    loads = [
        pltpu.make_async_copy(moved_a, moved.at[0], load.at[0]),
        pltpu.make_async_copy(moved_b, moved.at[1], load.at[1]),
    ]
    for half in range(2):
        for b in range(2):
            src, dst = total_in.at[half, b], total.at[half, b]
            loads.append(pltpu.make_async_copy(src, dst, load.at[2 + 2 * half + b]))
    for copy in loads:
        copy.start()
    stores = []

    def write(src, dst):
        copy = pltpu.make_async_copy(src, dst, store.at[len(stores)])
        copy.start()
        stores.append(copy)

    def widen(part):
        for g in range(2):
            for b in range(2):
                at = 512 * part + 256 * g + 128 * b
                rows = slice(32 * (part % 2), 32 * (part % 2) + 32)
                gqkv[:, at : at + 128] = total[part // 2, b, rows, g].reshape(512, 128).astype(F32)
        at = pl.ds(512 * part, 512)
        write(gqkv.at[:, at], gqkv_out.at[:, at])

    loads[0].wait()
    write(moved.at[0], out_a)
    loads[1].wait()
    write(moved.at[1], out_b)
    for copy in loads[2:4]:
        copy.wait()
    widen(0)
    widen(1)
    for copy in loads[4:6]:
        copy.wait()
    widen(2)
    for g in range(2):
        for b in range(2):
            for side in range(2):
                at = 256 * side + 128 * b
                piece = total[1, b, 32 + 16 * side : 48 + 16 * side, g].reshape(256, 128)
                gproj[256 * g : 256 * g + 256, at : at + 128] = piece.astype(F32)
    write(gproj, gproj_out)
    for copy in stores:
        copy.wait()


def body(tokens, cotangent, w_qkv, w_proj):
    shape = tokens.shape
    results = block(tokens.reshape(576, 512), cotangent.reshape(576, 512), w_qkv, w_proj)
    hbm = pl.BlockSpec(memory_space=pl.ANY)
    output, grad_tokens, gqkv, gproj = pl.pallas_call(
        hand_over,
        out_shape=(
            jax.ShapeDtypeStruct((576, 512), BF),
            jax.ShapeDtypeStruct((576, 512), BF),
            jax.ShapeDtypeStruct((512, 1536), F32),
            jax.ShapeDtypeStruct((512, 512), F32),
        ),
        in_specs=[hbm] * 3,
        out_specs=(hbm,) * 4,
        scratch_shapes=[
            pltpu.VMEM((2, 576, 512), BF),
            pltpu.VMEM((2, 2, 64, 2, 16, 128), BF),
            pltpu.VMEM((512, 1536), F32),
            pltpu.VMEM((512, 512), F32),
            pltpu.SemaphoreType.DMA((6,)),
            pltpu.SemaphoreType.DMA((6,)),
        ],
        compiler_params=pltpu.CompilerParams(vmem_limit_bytes=56 * 2**20),
        name="hand_over",
    )(*results)
    return (output.reshape(shape), grad_tokens.reshape(shape), gqkv, gproj)


def solution(mesh):
    spec = P(None, "lat", "lon", None)
    return jax.shard_map(
        body,
        mesh=mesh,
        in_specs=(spec, spec, P(), P()),
        out_specs=(spec, spec, P(), P()),
        check_vma=False,
    )
```

```python
import numpy as np
import jax
import jax.numpy as jnp
from jax import lax
from jax.experimental import pallas as pl
from jax.experimental.pallas import tpu as pltpu
from jax.sharding import PartitionSpec as P

BF = jnp.bfloat16
F32 = jnp.float32
SCALE = 1.0 / 32**0.5
EXP2 = SCALE * 1.4426950408889634
NORM = 1.0 / 73728**0.5
NN = (((1,), (0,)), ((), ()))
NT = (((1,), (1,)), ((), ()))
TN = (((0,), (0,)), ((), ()))
MESH = pl.DeviceIdType.MESH

ROWS = 608
KEPT = ((0, 144), (288, 80))
SENT = (((144, 144, 1, 0),), ((368, 80, 1, 0), (448, 80, 0, 1), (528, 80, 1, 1)))
SPAN = (slice(0, 288), slice(288, 608))


def section_row(array, level, row, col):
    line = level * 3 + row % 3
    if 6 <= col < 18:
        return (144 if row < 3 else 0) + array * 72 + line * 12 + col - 6
    start = (448 if col < 6 else 288) + (80 if row < 3 else 0)
    return start + array * 36 + line * 6 + col % 18


def orders():
    pack = np.zeros((ROWS, 576), np.float32)
    place = np.zeros((2, 288, ROWS), np.float32)
    for array in range(2):
        for level in range(2):
            for row in range(6):
                for col in range(24):
                    at = array * 288 + level * 144 + row * 24 + col
                    pack[section_row(array, level, row, col), at] = 1
                    loc, c = col // 12, col % 12
                    at = array * 144 + level * 72 + row * 12 + c
                    source = section_row(array, level, (row + 3) % 6, (col + 6) % 24)
                    place[loc, at, source] = 1
    place = [place[loc][:, SPAN[loc]] for loc in range(2)]
    return [jnp.asarray(m, BF) for m in (pack, *place, place[0].T, place[1].T, pack.T)]


def dot(a, b, dims=NN):
    return lax.dot_general(a, b, dims, preferred_element_type=F32)


def head_mask(dtype):
    head = lax.broadcasted_iota(jnp.int32, (128, 256), 0) >> 4
    col = lax.broadcasted_iota(jnp.int32, (128, 256), 1) >> 5
    return (head == col).astype(dtype)


def window_rows(w):
    return pl.ds(pl.multiple_of(w * 144, 16), 144)


def pair_rows(p):
    return slice(288 * p, 288 * p + 288)


def project(w, tok, cot, w_qkv, w_proj_t, hat, normed, inv, q, k, v, dc):
    rows = slice(144 * w, 144 * w + 144)
    x = tok[rows, :].astype(F32)
    x = x - jnp.mean(x, axis=1, keepdims=True)
    scale = lax.rsqrt(jnp.mean(x * x, axis=1, keepdims=True) + 1e-05)
    x = x * scale
    hat[rows, :] = x
    inv[rows, :] = jnp.broadcast_to(scale, (144, 128))
    x = x.astype(BF)
    normed[rows, :] = x
    for g in range(2):
        for part, ref in enumerate((q, k, v)):
            at = 512 * part + 256 * g
            ref[g, rows, :] = dot(x, w_qkv[:, at : at + 256]).astype(BF)
        dc[g, rows, :] = dot(cot[rows, :], w_proj_t[:, 256 * g : 256 * g + 256]).astype(BF)


def key_rows(p, c):
    if p == 0 or c == 4:
        return slice(0, 144)
    return slice(0, 80) if c < 4 else slice(64, 144)


def spans(p):
    if p == 0:
        return [(slice(0, 144), slice(0, 1152))]
    return [(key_rows(p, c), slice(128 * c, 128 * d)) for c, d in ((0, 4), (4, 5), (5, 9))]


def attend(w, groups, lat_last, lon_last, mask, maskf, q, k, v, dc, qs, cs, pt, st, sf, df, ctx, dqkv):
    p = w // 2
    first = 144 * w
    rows = slice(first, first + 144)
    klab, qlab = labels(w, lat_last, lon_last)

    def scores(g):
        keys, vals = k[g, rows, :], v[g, rows, :]
        for c in range(9):
            at = slice(128 * c, 128 * c + 128)
            q16 = q[g, first + 16 * c : first + 16 * c + 16, :]
            d16 = dc[g, first + 16 * c : first + 16 * c + 16, :]
            qs[g, at, :] = jnp.concatenate([q16] * 8, axis=0) * mask
            cs[g, at, :] = jnp.concatenate([d16] * 8, axis=0) * mask
        for kr, at in spans(p):
            sf[g, kr, at] = dot(keys[kr], qs[g, at, :], NT)
            df[g, kr, at] = dot(vals[kr], cs[g, at, :], NT)

    def softmax(g):
        for c in range(9):
            at = slice(128 * c, 128 * c + 128)
            kr = key_rows(p, c)
            s = jnp.where(klab[kr] == qlab[c], sf[g, kr, at], -1e30)
            e = jnp.exp2((s - jnp.max(s, axis=0, keepdims=True)) * EXP2)
            prob = e * (1.0 / jnp.sum(e, axis=0, keepdims=True))
            pt[2 * p + g, kr, at] = prob.astype(BF)
            dp = df[g, kr, at]
            inner = jnp.sum(prob * dp, axis=0, keepdims=True)
            st[2 * p + g, kr, at] = ((prob * SCALE) * (dp - inner)).astype(BF)

    def fold(m, g, ref):
        out = [dot(m[2 * p + g, kr, at], ref[g, rows, :][kr], TN) for kr, at in spans(p)]
        out = jnp.concatenate(out, axis=0) if len(out) > 1 else out[0]
        out = out.reshape(9, 8, 16, 256) * maskf.reshape(1, 8, 16, 256)
        return jnp.sum(out, axis=1).reshape(144, 256).astype(BF)

    def results(g):
        at = 768 * g
        ctx[rows, 256 * g : 256 * g + 256] = fold(pt, g, v)
        dqkv[rows, at : at + 256] = fold(st, g, k)
        dqkv[rows, at + 256 : at + 512] = dot(st[2 * p + g], qs[g]).astype(BF)
        dqkv[rows, at + 512 : at + 768] = dot(pt[2 * p + g], cs[g]).astype(BF)

    for g in groups:
        scores(g)
    for g in groups:
        softmax(g)
        results(g)


def finish(w, w_qkv_t, w_proj, hat, inv, ctx, dqkv, done):
    rows = slice(144 * w, 144 * w + 144)
    a = dot(ctx[rows, :], w_proj[...]).astype(BF)
    d = dot(dqkv[rows, :], w_qkv_t[...])
    h = hat[rows, :]
    d = d - jnp.mean(d, axis=1, keepdims=True) - h * jnp.mean(d * h, axis=1, keepdims=True)
    scale = jnp.concatenate([inv[rows, :]] * 4, axis=1)
    d = (d * scale).astype(BF)
    done[w, 0:144, :] = a
    done[w, 144:288, :] = d


def labels(w, lat_last, lon_last):
    def flags(t):
        level = (t >= 72).astype(jnp.int32)
        t = t - 72 * level
        row = (t >= 36).astype(jnp.int32)
        t = t - 36 * row
        t = jnp.where(t >= 24, t - 24, jnp.where(t >= 12, t - 12, t))
        col = (t >= 6).astype(jnp.int32)
        return level * is_b + row * lat_last + col * last

    is_b = 4 * (w // 2)
    last = lon_last * (w % 2)
    klab = flags(lax.broadcasted_iota(jnp.int32, (144, 128), 0))
    lane = lax.broadcasted_iota(jnp.int32, (1, 128), 1) & 15
    qlab = [flags(lane + 16 * c) for c in range(9)]
    return klab, qlab


def weight_gradients(g, normed, cot, ctx, dqkv, grad):
    def keep(d, half, at, count):
        for b in range(2):
            piece = d[:, 128 * b : 128 * b + 128].astype(BF)
            grad[g, half, b, at : at + count] = piece.reshape(count, 16, 128)

    for part in range(3):
        at = 768 * g + 256 * part
        d = dot(normed[...], dqkv[:, at : at + 256], TN)
        keep(d, part // 2, 32 * (part % 2), 32)
    d = dot(ctx[:, 256 * g : 256 * g + 256], cot[...], TN)
    for half in range(2):
        keep(d[:, 256 * half : 256 * half + 256], 1, 32 + 16 * half, 16)


def place():
    lat, lon = lax.axis_index("lat"), lax.axis_index("lon")
    return (lon // 2) % 4, (lon // 8) * 2 + lat % 2, lat // 2, lon % 2


def device(x, y, z, core):
    return z * 2 + y % 2, ((y // 2) * 4 + x) * 2 + core


def first_at(b):
    x, y, z, core = place()
    return x if b == 0 else z


def first_device(b, to):
    x, y, z, core = place()
    return device(to, y, z, core) if b == 0 else device(x, y, to, core)


def second_at(b):
    x, y, z, core = place()
    return y * 4 + (z if b == 0 else x)


def second_device(b, to):
    x, y, z, core = place()
    return device(x, to // 4, to % 4, core) if b == 0 else device(to % 4, to // 4, z, core)


def beside(lat_step, lon_step):
    lat, lon = lax.axis_index("lat"), lax.axis_index("lon")
    return lax.rem(lat + lat_step + 8, 8), lax.rem(lon + lon_step + 16, 16)


def drain(ref, sem):
    pltpu.make_async_copy(ref, ref, sem).wait()


def greet():
    x, y, z, core = place()
    barrier = pltpu.get_barrier_semaphore()

    def signal(to):
        pl.semaphore_signal(barrier, inc=1, device_id=to, device_id_type=MESH)

    for steps in ((-1, 0), (0, -1), (-1, -1), (1, 0), (0, 1), (1, 1)):
        signal(beside(*steps))
    signal(device(x, y, z, 1 - core))
    for b in range(2):
        for k in range(1, 4):
            signal(first_device(b, first_at(b) ^ k))

        @pl.loop(1, 16)
        def _(t):
            signal(second_device(b, second_at(b) ^ t))


def meet():
    pl.semaphore_wait(pltpu.get_barrier_semaphore(), 43)


def halo(w, step, src, dst, send, recv):
    p, loc = w // 2, w % 2
    copies = []
    for s, (at, count, lat_step, lon_step) in enumerate(SENT[loc]):
        copies.append(pltpu.make_async_remote_copy(
            src_ref=src.at[p, pl.ds(at, count)], dst_ref=dst.at[p, pl.ds(at, count)],
            send_sem=send.at[w, s], recv_sem=recv.at[w, s],
            device_id=beside(step * lat_step, step * lon_step), device_id_type=MESH,
        ))
    return copies


def core_swap(src, dst, send, recv):
    x, y, z, core = place()
    return pltpu.make_async_remote_copy(
        src_ref=src, dst_ref=dst, send_sem=send, recv_sem=recv,
        device_id=device(x, y, z, 1 - core), device_id_type=MESH,
    )


def scatter_first(mixed, parts, send, recv):
    for b in range(2):
        at = first_at(b)
        for k in (2, 1, 3):
            pltpu.make_async_remote_copy(
                src_ref=mixed.at[b, pl.ds((at ^ k) * 16, 16)], dst_ref=parts.at[b, at],
                send_sem=send.at[b], recv_sem=recv.at[b],
                device_id=first_device(b, at ^ k), device_id_type=MESH,
            ).start()


def scatter_second(g, mixed, parts, send, recv):
    for b in range(2):
        at = second_at(b)

        @pl.loop(0, 15)
        def _(t):
            to = at ^ (15 - t)
            pltpu.make_async_remote_copy(
                src_ref=mixed.at[b, to, g], dst_ref=parts.at[b, at, g],
                send_sem=send.at[b], recv_sem=recv.at[b],
                device_id=second_device(b, to), device_id_type=MESH,
            ).start()


def gather_second(g, total, send, recv):
    for b in range(2):
        at = second_at(b)
        piece = total.at[b, first_at(b) * 16 + at, g]

        @pl.loop(0, 15)
        def _(t):
            pltpu.make_async_remote_copy(
                src_ref=piece, dst_ref=piece, send_sem=send.at[b], recv_sem=recv.at[b],
                device_id=second_device(b, at ^ (15 - t)), device_id_type=MESH,
            ).start()


def gather_first(g, b, total, send, recv):
    at = first_at(b)
    piece = total.at[b, pl.ds(at * 16, 16), g]
    for k in (2, 1, 3):
        pltpu.make_async_remote_copy(
            src_ref=piece, dst_ref=piece, send_sem=send.at[g, b, k], recv_sem=recv.at[g, b, k],
            device_id=first_device(b, at ^ k), device_id_type=MESH,
        ).start()


def kernel(
    tokens, cotangent, w_qkv_in, w_proj_in, pack_in, place_0, place_1, unplace_0, unplace_1, unpack_in,
    output, grad_tokens, total_out,
    moved, both, w_qkv, w_proj, w_qkv_t, w_proj_t, pack, place_a, place_b, unplace_a, unplace_b, unpack, out_halo, in_halo, out_back, in_back,
    tok, cot, hat, normed, inv, q, k, v, dc, qs, cs, pt, st, sf, df, ctx, dqkv, done,
    grad, swapped, mixed, parts, mixed2, parts2, total, load, store, swap_send, swap_recv, send, recv, core_send, core_recv, wide_send, wide_recv, hsend, hrecv, bsend, brecv,
):
    x, y, z, core = place()
    loads = []

    def fetch(src, dst):
        copy = pltpu.make_async_copy(src, dst, load.at[len(loads)])
        copy.start()
        loads.append(copy)

    def fetch_tiles(p):
        for half, src in enumerate((tokens, cotangent)):
            for level in range(2):
                fetch(
                    src.at[pl.ds(144 * ((2 * p + 1 + level) % 4), 144)],
                    both.at[p, pl.ds(288 * half + 144 * level, 144)],
                )

    fetch(pack_in, pack)
    fetch_tiles(0)
    early = len(loads)
    greet()
    fetch_tiles(1)
    middle = len(loads)
    fetch(place_0, place_a)
    fetch(place_1, place_b)
    fetch(w_qkv_in, w_qkv)
    fetch(w_proj_in, w_proj)
    fetch(unplace_0, unplace_a)
    fetch(unplace_1, unplace_b)
    fetch(unpack_in, unpack)
    for copy in loads[:early]:
        copy.wait()
    out_halo[0, SPAN[0]] = dot(pack[SPAN[0], :], both[0]).astype(BF)
    meet()
    coming = [halo(w, -1, out_halo, in_halo, hsend, hrecv) for w in range(4)]

    def send_in(w):
        for copy in coming[w]:
            copy.start()

    send_in(0)
    out_halo[0, SPAN[1]] = dot(pack[SPAN[1], :], both[0]).astype(BF)
    send_in(1)
    for copy in loads[early:middle]:
        copy.wait()
    out_halo[1] = dot(pack[...], both[1]).astype(BF)
    send_in(3)
    send_in(2)
    for copy in loads[middle:]:
        copy.wait()
    for g in range(2):
        for part in range(3):
            at = 512 * part + 256 * g
            to = 768 * g + 256 * part
            w_qkv_t[to : to + 256, :] = w_qkv[:, at : at + 256].T
    w_proj_t[...] = w_proj[...].T
    for i in range(2):
        pt[2 + i] = jnp.zeros((144, 1152), BF)
        st[2 + i] = jnp.zeros((144, 1152), BF)
    lat_last = 2 * (lax.axis_index("lat") == 7).astype(jnp.int32)
    lon_last = (lax.axis_index("lon") == 15).astype(jnp.int32)
    mask = head_mask(BF)
    maskf = head_mask(F32)

    def arrive(w):
        p, loc = w // 2, w % 2
        at, count = KEPT[loc]
        in_halo[p, at : at + count] = out_halo[p, at : at + count]
        for copy in coming[w]:
            copy.wait_recv()
        placed = dot((place_a, place_b)[loc][...], in_halo[p, SPAN[loc]]).astype(BF)
        tok[144 * w : 144 * w + 144, :] = placed[0:144]
        cot[144 * w : 144 * w + 144, :] = placed[144:288]
        project(w, tok, cot, w_qkv, w_proj_t, hat, normed, inv, q, k, v, dc)

    def attention(w, groups):
        attend(w, groups, lat_last, lon_last, mask, maskf, q, k, v, dc, qs, cs, pt, st, sf, df, ctx, dqkv)

    def swap_in(g):
        return core_swap(grad.at[g, 1 - core], swapped.at[g], swap_send.at[g], swap_recv.at[g])

    def sum_first(g):
        swap_in(g).wait()
        mixed[g] = (grad[g, core].astype(F32) + swapped[g].astype(F32)).astype(BF)
        scatter_first(mixed.at[g], parts.at[g], send.at[g], recv.at[g])
        for b in range(2):
            at = first_at(b)
            parts[g, b, at] = mixed[g, b, pl.ds(at * 16, 16)]

    def sum_second(g):
        for b in range(2):
            drain(parts.at[g, b, pl.ds(0, 3)], recv.at[g, b])
            mixed2[b, :, g] = jnp.sum(parts[g, b].astype(F32), axis=0).astype(BF)
        scatter_second(g, mixed2, parts2, send.at[2 + g], recv.at[2 + g])
        for b in range(2):
            at = second_at(b)
            parts2[b, at, g] = mixed2[b, at, g]

    def spread_second(g):
        for b in range(2):
            drain(parts2.at[b, pl.ds(0, 15), g], recv.at[2 + g, b])
            final = jnp.sum(parts2[b, :, g].astype(F32), axis=0) * NORM
            total[core, b, first_at(b) * 16 + second_at(b), g] = final.astype(BF)
        gather_second(g, total.at[core], send.at[4 + g], recv.at[4 + g])

    def core_out(g, b, i):
        part = total.at[core, b, pl.ds((first_at(b) ^ i) * 16, 16), g]
        return core_swap(part, part, core_send.at[g, b, i], core_recv.at[g, b, i])

    def spread_first(g):
        for b in range(2):
            drain(parts2.at[b, pl.ds(0, 15), g], recv.at[4 + g, b])
            gather_first(g, b, total.at[core], wide_send, wide_recv)
            core_out(g, b, 0).start()

    def spread_core(g):
        for i in (1, 3, 2):
            for b in range(2):
                drain(total.at[core, b, pl.ds(0, 16), g], wide_recv.at[g, b, i])
                core_out(g, b, i).start()

    def store_half(half, i):
        return pltpu.make_async_copy(total.at[half], total_out.at[half], store.at[2 + i])

    def store_moved():
        outs = (output, grad_tokens)
        return [pltpu.make_async_copy(moved.at[i], outs[i], store.at[i]) for i in range(2)]

    def drain_sends():
        for g in range(2):
            for b in range(2):
                drain(parts.at[g, b, pl.ds(0, 3)], send.at[g, b])
                drain(parts2.at[b, pl.ds(0, 15), g], send.at[2 + g, b])
                drain(parts2.at[b, pl.ds(0, 15), g], send.at[4 + g, b])
                for i in range(1, 4):
                    drain(total.at[core, b, pl.ds(0, 16), g], wide_send.at[g, b, i])

    def back(p):
        for w in (2 * p, 2 * p + 1):
            at, count = KEPT[w % 2]
            in_back[p, at : at + count] = out_back[p, at : at + count]
            for copy in going[w]:
                copy.wait_recv()
        for half in range(2):
            for level in range(2):
                at = 144 * ((2 * p + 1 + level) % 4)
                rows = slice(288 * half + 144 * level, 288 * half + 144 * level + 144)
                d = dot(unpack[rows, :], in_back[p]).astype(BF)
                moved[half, at : at + 144, :] = (both[p, rows, :].astype(F32) + d.astype(F32)).astype(BF)

    going = [halo(w, 1, out_back, in_back, bsend, brecv) for w in range(4)]

    def leave(w):
        finish(w, w_qkv_t, w_proj, hat, inv, ctx, dqkv, done)

    def send_back(w):
        unplace = (unplace_a, unplace_b)[w % 2]
        out_back[w // 2, SPAN[w % 2]] = dot(unplace[...], done[w]).astype(BF)
        for copy in going[w]:
            copy.start()

    for w in (0, 1):
        arrive(w)
        attention(w, (0, 1))
    leave(0)
    send_back(0)
    leave(1)
    send_back(1)
    arrive(3)
    attention(3, (0, 1))
    leave(3)
    send_back(3)
    arrive(2)
    attention(2, (0,))
    weight_gradients(0, normed, cot, ctx, dqkv, grad)
    swap_in(0).start()
    attention(2, (1,))
    sum_first(0)
    weight_gradients(1, normed, cot, ctx, dqkv, grad)
    swap_in(1).start()
    sum_first(1)
    leave(2)
    back(0)
    sum_second(0)
    sum_second(1)
    send_back(2)
    spread_second(0)
    spread_second(1)
    spread_first(0)
    spread_first(1)
    spread_core(0)
    spread_core(1)
    store_half(core, 0).start()
    back(1)
    for copy in store_moved():
        copy.start()
    drain_sends()
    for w in range(4):
        for copy in coming[w] + going[w]:
            copy.wait_send()
    for g in range(2):
        for b in range(2):
            for i in range(4):
                core_out(g, b, i).wait()
    store_half(1 - core, 1).start()
    for copy in store_moved() + [store_half(core, 0), store_half(1 - core, 1)]:
        copy.wait()


def block(tokens, cotangent, w_qkv, w_proj):
    hbm = pl.BlockSpec(memory_space=pl.ANY)
    dma = pltpu.SemaphoreType.DMA
    return pl.pallas_call(
        kernel,
        out_shape=(
            jax.ShapeDtypeStruct((576, 512), BF),
            jax.ShapeDtypeStruct((576, 512), BF),
            jax.ShapeDtypeStruct((2, 2, 64, 2, 16, 128), BF),
        ),
        in_specs=[hbm] * 10,
        out_specs=(hbm,) * 3,
        scratch_shapes=[
            pltpu.VMEM((2, 576, 512), BF),
            pltpu.VMEM((2, 576, 512), BF),
            pltpu.VMEM((512, 1536), BF),
            pltpu.VMEM((512, 512), BF),
            pltpu.VMEM((1536, 512), BF),
            pltpu.VMEM((512, 512), BF),
            pltpu.VMEM((ROWS, 576), BF),
            pltpu.VMEM((288, 288), BF),
            pltpu.VMEM((288, 320), BF),
            pltpu.VMEM((288, 288), BF),
            pltpu.VMEM((320, 288), BF),
            pltpu.VMEM((576, ROWS), BF),
            pltpu.VMEM((2, ROWS, 512), BF),
            pltpu.VMEM((2, ROWS, 512), BF),
            pltpu.VMEM((2, ROWS, 512), BF),
            pltpu.VMEM((2, ROWS, 512), BF),
            pltpu.VMEM((576, 512), BF),
            pltpu.VMEM((576, 512), BF),
            pltpu.VMEM((576, 512), F32),
            pltpu.VMEM((576, 512), BF),
            pltpu.VMEM((576, 128), F32),
            pltpu.VMEM((2, 576, 256), BF),
            pltpu.VMEM((2, 576, 256), BF),
            pltpu.VMEM((2, 576, 256), BF),
            pltpu.VMEM((2, 576, 256), BF),
            pltpu.VMEM((2, 1152, 256), BF),
            pltpu.VMEM((2, 1152, 256), BF),
            pltpu.VMEM((4, 144, 1152), BF),
            pltpu.VMEM((4, 144, 1152), BF),
            pltpu.VMEM((2, 144, 1152), F32),
            pltpu.VMEM((2, 144, 1152), F32),
            pltpu.VMEM((576, 512), BF),
            pltpu.VMEM((576, 1536), BF),
            pltpu.VMEM((4, 288, 512), BF),
            pltpu.VMEM((2, 2, 2, 64, 16, 128), BF),
            pltpu.VMEM((2, 2, 64, 16, 128), BF),
            pltpu.VMEM((2, 2, 64, 16, 128), BF),
            pltpu.VMEM((2, 2, 4, 16, 16, 128), BF),
            pltpu.VMEM((2, 16, 2, 16, 128), BF),
            pltpu.VMEM((2, 16, 2, 16, 128), BF),
            pltpu.VMEM((2, 2, 64, 2, 16, 128), BF),
            dma((16,)),
            dma((4,)),
            dma((2,)),
            dma((2,)),
            dma((6, 2)),
            dma((6, 2)),
            dma((2, 2, 4)),
            dma((2, 2, 4)),
            dma((2, 2, 4)),
            dma((2, 2, 4)),
            dma((4, 3)),
            dma((4, 3)),
            dma((4, 3)),
            dma((4, 3)),
        ],
        compiler_params=pltpu.CompilerParams(
            vmem_limit_bytes=56 * 2**20, collective_id=0, has_side_effects=True
        ),
        name="window_block",
    )(tokens, cotangent, w_qkv, w_proj, *orders())


def hand_over(moved_a, moved_b, total_in, out_a, out_b, gqkv_out, gproj_out, moved, total, gqkv, gproj, load, store):
    loads = [
        pltpu.make_async_copy(moved_a, moved.at[0], load.at[0]),
        pltpu.make_async_copy(moved_b, moved.at[1], load.at[1]),
    ]
    for half in range(2):
        for b in range(2):
            src, dst = total_in.at[half, b], total.at[half, b]
            loads.append(pltpu.make_async_copy(src, dst, load.at[2 + 2 * half + b]))
    for copy in loads:
        copy.start()
    stores = []

    def write(src, dst):
        copy = pltpu.make_async_copy(src, dst, store.at[len(stores)])
        copy.start()
        stores.append(copy)

    def widen(part):
        for g in range(2):
            for b in range(2):
                at = 512 * part + 256 * g + 128 * b
                rows = slice(32 * (part % 2), 32 * (part % 2) + 32)
                gqkv[:, at : at + 128] = total[part // 2, b, rows, g].reshape(512, 128).astype(F32)
        at = pl.ds(512 * part, 512)
        write(gqkv.at[:, at], gqkv_out.at[:, at])

    loads[0].wait()
    write(moved.at[0], out_a)
    loads[1].wait()
    write(moved.at[1], out_b)
    for copy in loads[2:4]:
        copy.wait()
    widen(0)
    widen(1)
    for copy in loads[4:6]:
        copy.wait()
    widen(2)
    for g in range(2):
        for b in range(2):
            for side in range(2):
                at = 256 * side + 128 * b
                piece = total[1, b, 32 + 16 * side : 48 + 16 * side, g].reshape(256, 128)
                gproj[256 * g : 256 * g + 256, at : at + 128] = piece.astype(F32)
    write(gproj, gproj_out)
    for copy in stores:
        copy.wait()


def body(tokens, cotangent, w_qkv, w_proj):
    shape = tokens.shape
    results = block(tokens.reshape(576, 512), cotangent.reshape(576, 512), w_qkv, w_proj)
    hbm = pl.BlockSpec(memory_space=pl.ANY)
    output, grad_tokens, gqkv, gproj = pl.pallas_call(
        hand_over,
        out_shape=(
            jax.ShapeDtypeStruct((576, 512), BF),
            jax.ShapeDtypeStruct((576, 512), BF),
            jax.ShapeDtypeStruct((512, 1536), F32),
            jax.ShapeDtypeStruct((512, 512), F32),
        ),
        in_specs=[hbm] * 3,
        out_specs=(hbm,) * 4,
        scratch_shapes=[
            pltpu.VMEM((2, 576, 512), BF),
            pltpu.VMEM((2, 2, 64, 2, 16, 128), BF),
            pltpu.VMEM((512, 1536), F32),
            pltpu.VMEM((512, 512), F32),
            pltpu.SemaphoreType.DMA((6,)),
            pltpu.SemaphoreType.DMA((6,)),
        ],
        compiler_params=pltpu.CompilerParams(vmem_limit_bytes=56 * 2**20),
        name="hand_over",
    )(*results)
    return (output.reshape(shape), grad_tokens.reshape(shape), gqkv, gproj)


def solution(mesh):
    spec = P(None, "lat", "lon", None)
    return jax.shard_map(
        body,
        mesh=mesh,
        in_specs=(spec, spec, P(), P()),
        out_specs=(spec, spec, P(), P()),
        check_vma=False,
    )
```
